512 devices in a mesh: pb: 16 (over y, core), ka: 32 (over z, x).
Axes of the slice: x: 4, y: 8, z: 8, core: 2. Of those that a mesh axis runs over, the one named last changes fastest.
Arguments:
- coupling: bfloat16 [400, 2, 196608], P('pb', None, 'ka'), may hold values from -0.3125 to 0.3125
- eigvecs: bfloat16 [32, 8192], P('ka'), may hold values from -0.75 to 0.75
- partner: int32 [16, 32], P('pb', 'ka'), may hold values from 0 to 31
- kpoints: float32 [3, 32], replicated, may hold values from 0 to 1
- qpoints: float32 [3, 16], replicated, may hold values from 0 to 1
- lattice: int32 [6, 400], replicated, may hold values from -4 to 4
Outputs:
- couplings_sq: bfloat16 [16, 32, 196608], P('pb', 'ka')
The draws below stay inside these ranges and needn't reach their ends.
All inputs are finite; a program needn't handle non-finite values.
Results may differ from the reference program's by a relative error of at most 0.008.
Values may be sent and summed in bfloat16 or wider, within the bound.
A program may use at most 64 MiB of HBM per device.

```python
import math
import jax
import jax.numpy as jnp
from jax import lax

W = 64
M = 48
P_SIZE = 400
K = 32
Q = 16


def set_ends(result, key, least, largest):
    shape = result.shape
    index_at = [jax.random.randint(jax.random.fold_in(key, axis), (), 0, shape[axis]) for axis in range(len(shape))]
    result = result.at[tuple(index_at)].set(least)
    longest = shape.index(max(shape))
    index_at[longest] = (index_at[longest] + 1) % shape[longest]
    return result.at[tuple(index_at)].set(largest)


def shard_levels(rng, extent, split, smallest, top_value):
    level = 1.0
    for dim, blocks in split:
        heights = jax.random.uniform(jax.random.fold_in(jax.random.fold_in(rng, 6), dim), (blocks,), jnp.float32, smallest / len(split), top_value / len(split))
        level = level * jnp.repeat(jnp.exp(heights), extent[dim] // blocks).reshape((-1,) + (1,) * (len(extent) - 1 - dim))
    return level


def centred(stream_key, shape, spread, most, pieces=(), kind=jnp.bfloat16):
    factor_of = shard_levels(stream_key, shape, pieces, -0.22, 0.18) if pieces else 1.0
    result = jax.random.normal(stream_key, shape, jnp.float32) * spread * factor_of
    return jnp.minimum(jnp.maximum(result, -most), most).astype(kind)


def setup_inputs(seed: int = 0) -> dict:
    seeds = jax.random.split(jax.random.key(seed), 7)
    return {
        "coupling": centred(seeds[0], (P_SIZE, 2, W * W * M), P_SIZE ** -0.5, 0.3125, ((0, 16), (2, 32))),
        "eigvecs": centred(seeds[1], (K, 2 * W * W), W ** -0.5, 0.75, ((0, 32),)),
        "partner": set_ends(jax.random.randint(seeds[2], (Q, K), 0, K), jax.random.fold_in(seeds[2], 1), 0, K - 1).astype(jnp.int32),
        "kpoints": jnp.clip(jax.random.uniform(seeds[3], (3, K), jnp.float32, 0.0, 1.0), 0.0, 1.0),
        "qpoints": jnp.clip(jax.random.uniform(seeds[4], (3, Q), jnp.float32, 0.0, 1.0), 0.0, 1.0),
        "lattice": set_ends(jax.random.randint(seeds[5], (6, P_SIZE), -4, 5), jax.random.fold_in(seeds[5], 1), -4, 4).astype(jnp.int32),
    }


def phase_pair(kpoints, qvector, lattice):
    lattice_f = lattice.astype(jnp.float32)
    kdot = kpoints[0][:, None] * lattice_f[0][None, :] + kpoints[1][:, None] * lattice_f[1][None, :] + kpoints[2][:, None] * lattice_f[2][None, :]
    qdot = qvector[0][:, None] * lattice_f[3][None, :] + qvector[1][:, None] * lattice_f[4][None, :] + qvector[2][:, None] * lattice_f[5][None, :]
    angle = (2.0 * math.pi) * (kdot[None, :, :] + qdot[:, None, :])
    return jnp.cos(angle).astype(jnp.bfloat16), jnp.sin(angle).astype(jnp.bfloat16)


def transform(cosines, sines, coupling):
    rows = coupling.shape[0]
    flat = coupling.reshape(rows, -1)
    with_cos = jnp.dot(cosines, flat, preferred_element_type=jnp.float32).reshape(cosines.shape[0], 2, -1)
    with_sin = jnp.dot(sines, flat, preferred_element_type=jnp.float32).reshape(sines.shape[0], 2, -1)
    real_part = with_cos[:, 0] - with_sin[:, 1]
    imag_part = with_cos[:, 1] + with_sin[:, 0]
    return jnp.stack([real_part, imag_part], axis=1).astype(jnp.bfloat16)


def rounded(value):
    return lax.optimization_barrier(value.astype(jnp.bfloat16)).astype(jnp.float32)


def rotate(bloch, far_vectors, near_vectors):
    count = bloch.shape[0]
    field = bloch.astype(jnp.float32).reshape(count, 2, W, W * M)
    left = far_vectors.astype(jnp.float32).reshape(count, 2, W, W)
    right = near_vectors.astype(jnp.float32).reshape(count, 2, W, W)
    half_real = jnp.einsum('kim,kix->kmx', left[:, 0], field[:, 0]) + jnp.einsum('kim,kix->kmx', left[:, 1], field[:, 1])
    half_imag = jnp.einsum('kim,kix->kmx', left[:, 0], field[:, 1]) - jnp.einsum('kim,kix->kmx', left[:, 1], field[:, 0])
    half_real = rounded(half_real).reshape(count, W, W, M)
    half_imag = rounded(half_imag).reshape(count, W, W, M)
    rot_real = jnp.einsum('kmjv,kjn->kmnv', half_real, right[:, 0]) - jnp.einsum('kmjv,kjn->kmnv', half_imag, right[:, 1])
    rot_imag = jnp.einsum('kmjv,kjn->kmnv', half_real, right[:, 1]) + jnp.einsum('kmjv,kjn->kmnv', half_imag, right[:, 0])
    return (rot_real * rot_real + rot_imag * rot_imag).astype(jnp.bfloat16).reshape(count, W * W * M)


def reference(coupling, eigvecs, partner, kpoints, qpoints, lattice):
    def per_qpoint(qindex):
        qvector = lax.dynamic_slice_in_dim(qpoints, qindex, 1, 1)
        cosines, sines = phase_pair(kpoints, qvector, lattice)
        bloch = transform(cosines[0], sines[0], coupling)
        targets = lax.dynamic_index_in_dim(partner, qindex, 0, keepdims=False)
        far_vectors = jnp.take(eigvecs, targets, axis=0)
        return rotate(bloch, far_vectors, eigvecs)

    return lax.map(per_qpoint, jnp.arange(Q, dtype=jnp.int32))
```

```python
import math

import jax
import jax.numpy as jnp
from jax import lax
from jax.experimental import pallas as pl
from jax.experimental.pallas import tpu as pltpu
from jax.sharding import PartitionSpec as P

MESH = pl.DeviceIdType.MESH
NPB = 16
NKA = 32
NZ = 8
NX = 4
VS = 3
F32 = jnp.float32
BF16 = jnp.bfloat16


def kernel(
    c_hbm, near_ref, eig_ref, part_ref, kp_ref, qp_ref, lat_ref, out_ref,
    ck, sk, cq, sq, phase, wmat, cols, bsend, brecv, table, parts, tmat, qsend, qrecv, spread,
    c_ss, c_rs, b_ss, b_rs, q_ss, q_rs, z_ss, z_rs, x_ss, x_rs, p_ss, p_rs, own_sem,
):
    pb = lax.axis_index("pb")
    ka = lax.axis_index("ka")
    zi = ka // NX
    xi = lax.rem(ka, NX)

    def pb_peer(step):
        return lax.rem(pb + step, NPB)

    def ka_peer(step):
        return lax.rem(ka + step, NKA)

    barrier = pltpu.get_barrier_semaphore()

    def greet_pb(step, carry):
        pl.semaphore_signal(barrier, inc=1, device_id=(pb_peer(step), ka), device_id_type=MESH)
        return carry

    def greet_ka(step, carry):
        pl.semaphore_signal(barrier, inc=1, device_id=(pb, ka_peer(step)), device_id_type=MESH)
        return carry

    lax.fori_loop(1, NPB, greet_pb, 0)
    lax.fori_loop(1, NKA, greet_ka, 0)

    own = pltpu.make_async_copy(c_hbm.at[pb], cols.at[:, pb], own_sem)
    own.start()

    def turn(points, first, extra):
        t = extra
        for axis in range(3):
            t = t + points[:, axis : axis + 1] * lat_ref[first + axis : first + axis + 1, :]
        return (2.0 * math.pi) * (t - jnp.round(t))

    ang = turn(kp_ref[...], 0, jnp.zeros((NKA, 1024), F32))
    ck[...] = jnp.cos(ang)
    sk[...] = jnp.sin(ang)
    ang = turn(qp_ref[...], 3, jnp.broadcast_to(lat_ref[6:7, :], (NPB, 1024)))
    cq[...] = jnp.cos(ang)
    sq[...] = jnp.sin(ang)

    wmat[...] = jnp.zeros_like(wmat)
    for i2 in range(2):
        rows0 = pl.ds(i2 * 64, 64)
        rows1 = pl.ds(128 + i2 * 64, 64)
        lanes0 = pl.ds(i2 * 128, 128)
        lanes1 = pl.ds(256 + i2 * 128, 128)
        wmat[rows0, lanes0] = near_ref[0]
        wmat[rows1, lanes0] = near_ref[1]
        wmat[rows0, lanes1] = -near_ref[1]
        wmat[rows1, lanes1] = near_ref[0]

    pl.semaphore_wait(barrier, NPB - 1 + NKA - 1)

    def c_copy(v, step):
        to = pb_peer(step)
        return pltpu.make_async_remote_copy(
            src_ref=c_hbm.at[to, v], dst_ref=cols.at[v, pb],
            send_sem=c_ss.at[v, to], recv_sem=c_rs.at[v, pb],
            device_id=(to, ka), device_id_type=MESH,
        )

    def c_recv(v, step):
        src = pb_peer(step)
        return pltpu.make_async_remote_copy(
            src_ref=c_hbm.at[src, v], dst_ref=cols.at[v, src],
            send_sem=c_ss.at[v, src], recv_sem=c_rs.at[v, src],
            device_id=(src, ka), device_id_type=MESH,
        )

    def z_copy(step, sending):
        other = lax.rem(zi + step, NZ)
        slot = zi if sending else other
        return pltpu.make_async_remote_copy(
            src_ref=eig_ref, dst_ref=table.at[xi, slot],
            send_sem=z_ss.at[other], recv_sem=z_rs.at[slot],
            device_id=(pb, other * NX + xi), device_id_type=MESH,
        )

    def x_copy(step, sending):
        other = lax.rem(xi + step, NX)
        slot = xi if sending else other
        return pltpu.make_async_remote_copy(
            src_ref=table.at[slot], dst_ref=table.at[slot],
            send_sem=x_ss.at[other], recv_sem=x_rs.at[slot],
            device_id=(pb, zi * NX + other), device_id_type=MESH,
        )

    def p_copy(step, sending):
        other = pb_peer(step)
        slot = pb if sending else other
        return pltpu.make_async_remote_copy(
            src_ref=part_ref, dst_ref=parts.at[slot],
            send_sem=p_ss.at[other], recv_sem=p_rs.at[slot],
            device_id=(other, ka), device_id_type=MESH,
        )

    def b_copy(v, step, sending):
        other = ka_peer(step)
        slot = ka if sending else other
        return pltpu.make_async_remote_copy(
            src_ref=bsend.at[v, other], dst_ref=brecv.at[v, slot],
            send_sem=b_ss.at[v, other], recv_sem=b_rs.at[v, slot],
            device_id=(pb, other), device_id_type=MESH,
        )

    def q_copy(v, step, sending):
        other = pb_peer(step)
        slot = pb if sending else other
        return pltpu.make_async_remote_copy(
            src_ref=qsend.at[v, other], dst_ref=qrecv.at[v, slot],
            send_sem=q_ss.at[v, other], recv_sem=q_rs.at[v, slot],
            device_id=(other, ka), device_id_type=MESH,
        )

    def loop(first, last, do):
        def step_of(step, carry):
            do(step)
            return carry

        lax.fori_loop(first, last, step_of, 0)

    loop(1, NPB, lambda s: c_copy(0, s).start())
    loop(1, NZ, lambda s: z_copy(s, True).start())
    loop(1, NPB, lambda s: c_copy(1, s).start())
    loop(1, NPB, lambda s: c_copy(2, s).start())
    loop(1, NPB, lambda s: p_copy(s, True).start())

    table[xi, zi] = eig_ref[...]
    parts[pb] = part_ref[...]

    def make_phase(k):
        c = ck[pl.ds(k, 1), :]
        s = sk[pl.ds(k, 1), :]
        phase[k, 0:16, :] = (c * cq[...] - s * sq[...]).astype(BF16)
        phase[k, 16:32, :] = (s * cq[...] + c * sq[...]).astype(BF16)

    loop(0, NKA, make_phase)

    loop(1, NZ, lambda s: z_copy(s, False).wait_recv())
    loop(1, NX, lambda s: x_copy(s, True).start())

    own.wait()

    def bloch_of(v):
        loop(1, NPB, lambda s: c_recv(v, s).wait_recv())

        def part(n):
            rows = pl.ds(n * 8, 8)
            got = jnp.dot(
                phase[rows].reshape(256, 1024), cols[v].reshape(1024, 128),
                preferred_element_type=F32,
            )
            bsend[v, rows] = got.astype(BF16).reshape(8, 32, 128)

        loop(0, 4, part)
        loop(1, NKA, lambda s: b_copy(v, s, True).start())
        brecv[v, ka] = bsend[v, ka]

    loop(0, VS, bloch_of)

    loop(1, NX, lambda s: x_copy(s, False).wait_recv())
    loop(1, NPB, lambda s: p_copy(s, False).wait_recv())

    low = lax.broadcasted_iota(jnp.int32, (32, 128), 1) < 64

    def squares(q):
        field = jnp.concatenate([tmat[t, pl.ds(q, 32, stride=16), :] for t in range(4)], axis=0)
        label = jnp.max(parts[q])
        far = table[lax.rem(label, NX), label // NX]
        turned = field.T.astype(BF16)
        got = lax.dot_general(
            turned, jnp.concatenate([far, far], axis=0), (((1,), (1,)), ((), ())),
            preferred_element_type=F32,
        )
        got = got * got
        both = got[0:64] + got[64:128]
        return jnp.where(low, both[0:32], both[32:64]).astype(BF16)

    def rotate(v):
        loop(1, NKA, lambda s: b_copy(v, s, False).wait_recv())

        def near(n):
            rows = pl.ds(n * 8, 8)
            field = jnp.concatenate(
                [brecv[v, rows, 0:16, :].reshape(128, 128), brecv[v, rows, 16:32, :].reshape(128, 128)],
                axis=1,
            )
            got = jnp.dot(field, wmat[...], preferred_element_type=F32)
            for t in range(4):
                tmat[t, pl.ds(n * 128, 128), :] = got[:, t * 128 : (t + 1) * 128]

        loop(0, 4, near)

        def one(s):
            q = pb_peer(s)
            qsend[v, q] = squares(q)
            q_copy(v, s, True).start()

        loop(1, NPB, one)
        qrecv[v, pb] = squares(pb)

    loop(0, VS, rotate)

    def place(v):
        loop(1, NPB, lambda s: q_copy(v, s, False).wait_recv())

        def one(s):
            spread[pl.ds(3 * s + v, 32, stride=48), :] = qrecv[v, s].astype(F32)

        loop(0, NPB, one)

    loop(0, VS, place)

    for n in range(12):
        block = spread[n * 128 : (n + 1) * 128, :].T.astype(BF16)
        out_ref[:, n * 128 : (n + 1) * 128] = block[0:64]
        out_ref[:, 1536 + n * 128 : 1536 + (n + 1) * 128] = block[64:128]

    loop(1, NZ, lambda s: z_copy(s, True).wait_send())
    loop(1, NX, lambda s: x_copy(s, True).wait_send())
    loop(1, NPB, lambda s: p_copy(s, True).wait_send())

    def drain(v):
        loop(1, NPB, lambda s: c_copy(v, s).wait_send())
        loop(1, NKA, lambda s: b_copy(v, s, True).wait_send())
        loop(1, NPB, lambda s: q_copy(v, s, True).wait_send())

    loop(0, VS, drain)


def couple(columns, near, eig, part, kp, qp, lat):
    vmem = pl.BlockSpec(memory_space=pltpu.VMEM)
    dma = pltpu.SemaphoreType.DMA
    return pl.pallas_call(
        kernel,
        out_shape=jax.ShapeDtypeStruct((64, 3072), BF16),
        in_specs=[pl.BlockSpec(memory_space=pl.ANY)] + [vmem] * 6,
        out_specs=vmem,
        scratch_shapes=[
            pltpu.VMEM((NKA, 1024), F32),
            pltpu.VMEM((NKA, 1024), F32),
            pltpu.VMEM((NPB, 1024), F32),
            pltpu.VMEM((NPB, 1024), F32),
            pltpu.VMEM((NKA, 32, 1024), BF16),
            pltpu.VMEM((256, 512), BF16),
            pltpu.VMEM((VS, NPB, 64, 128), BF16),
            pltpu.VMEM((VS, NKA, 32, 128), BF16),
            pltpu.VMEM((VS, NKA, 32, 128), BF16),
            pltpu.VMEM((NX, NZ, 64, 128), BF16),
            pltpu.VMEM((NPB, 8, 128), jnp.int32),
            pltpu.VMEM((4, 512, 128), F32),
            pltpu.VMEM((VS, NPB, 32, 128), BF16),
            pltpu.VMEM((VS, NPB, 32, 128), BF16),
            pltpu.VMEM((1536, 128), F32),
            dma((VS, NPB)), dma((VS, NPB)),
            dma((VS, NKA)), dma((VS, NKA)),
            dma((VS, NPB)), dma((VS, NPB)),
            dma((NZ,)), dma((NZ,)),
            dma((NX,)), dma((NX,)),
            dma((NPB,)), dma((NPB,)),
            dma(()),
        ],
        compiler_params=pltpu.CompilerParams(
            collective_id=0, has_side_effects=True, vmem_limit_bytes=40 << 20
        ),
        name="couple",
    )(columns, near, eig, part, kp, qp, lat)


def body(coupling, eigvecs, partner, kpoints, qpoints, lattice):
    columns = coupling.reshape(25, 2, 128, 48).transpose(3, 1, 0, 2)
    columns = jnp.pad(columns, ((0, 0), (0, 0), (0, 7), (0, 0))).reshape(NPB, VS, 64, 128)
    vectors = eigvecs.reshape(2, 64, 64)
    real, imag = vectors[0], vectors[1]
    near = jnp.stack([jnp.concatenate([real, imag], 1), jnp.concatenate([-imag, real], 1)])
    eig = vectors.reshape(2, 32, 2, 64).transpose(3, 0, 2, 1).reshape(64, 128)
    part = jnp.broadcast_to(partner, (8, 128))
    lat = jnp.pad(lattice.astype(F32).reshape(6, NPB, 1, 25), ((0, 0), (0, 0), (0, 0), (0, 7)))
    lat = jnp.broadcast_to(lat, (6, NPB, 2, 32)).reshape(6, 1024)
    quarter = jnp.broadcast_to(jnp.array([0.0, 0.25], F32).reshape(1, 1, 2, 1), (1, NPB, 2, 32))
    lat = jnp.concatenate([lat, quarter.reshape(1, 1024), jnp.zeros((1, 1024), F32)], 0)
    out = couple(columns, near, eig, part, kpoints.T, qpoints.T, lat)
    return out.reshape(1, 1, 196608)


def solution(mesh):
    in_specs = (P("pb", None, "ka"), P("ka", None), P("pb", "ka"), P(), P(), P())
    out_specs = P("pb", "ka", None)
    return jax.shard_map(body, mesh=mesh, in_specs=in_specs, out_specs=out_specs, check_vma=False)
```

```python
import math

import jax
import jax.numpy as jnp
from jax import lax
from jax.experimental import pallas as pl
from jax.experimental.pallas import tpu as pltpu
from jax.sharding import PartitionSpec as P

MESH = pl.DeviceIdType.MESH
NPB = 16
NKA = 32
NZ = 8
NX = 4
VS = 3
F32 = jnp.float32
BF16 = jnp.bfloat16


def kernel(
    c_hbm, near_ref, eig_ref, part_ref, kp_ref, qp_ref, lat_ref, out_ref,
    ck, sk, cq, sq, phase, wmat, cols, bsend, brecv, table, parts, tmat, qsend, qrecv, spread,
    c_ss, c_rs, b_ss, b_rs, q_ss, q_rs, z_ss, z_rs, x_ss, x_rs, p_ss, p_rs, own_sem,
):
    pb = lax.axis_index("pb")
    ka = lax.axis_index("ka")
    zi = ka // NX
    xi = lax.rem(ka, NX)

    def pb_peer(step):
        return lax.rem(pb + step, NPB)

    def ka_peer(step):
        return lax.rem(ka + step, NKA)

    barrier = pltpu.get_barrier_semaphore()

    def greet_pb(step, carry):
        pl.semaphore_signal(barrier, inc=1, device_id=(pb_peer(step), ka), device_id_type=MESH)
        return carry

    def greet_ka(step, carry):
        pl.semaphore_signal(barrier, inc=1, device_id=(pb, ka_peer(step)), device_id_type=MESH)
        return carry

    lax.fori_loop(1, NPB, greet_pb, 0)
    lax.fori_loop(1, NKA, greet_ka, 0)

    own = pltpu.make_async_copy(c_hbm.at[pb], cols.at[:, pb], own_sem)
    own.start()

    with jax.named_scope("entry"):
        pl.semaphore_wait(barrier, NPB - 1 + NKA - 1)

    def c_copy(v, step):
        to = pb_peer(step)
        return pltpu.make_async_remote_copy(
            src_ref=c_hbm.at[to, v], dst_ref=cols.at[v, pb],
            send_sem=c_ss.at[v], recv_sem=c_rs.at[v],
            device_id=(to, ka), device_id_type=MESH,
        )

    def z_copy(step):
        other = lax.rem(zi + step, NZ)
        return pltpu.make_async_remote_copy(
            src_ref=eig_ref, dst_ref=table.at[xi, zi],
            send_sem=z_ss, recv_sem=z_rs,
            device_id=(pb, other * NX + xi), device_id_type=MESH,
        )

    def x_copy(step):
        other = lax.rem(xi + step, NX)
        return pltpu.make_async_remote_copy(
            src_ref=table.at[xi], dst_ref=table.at[xi],
            send_sem=x_ss, recv_sem=x_rs,
            device_id=(pb, zi * NX + other), device_id_type=MESH,
        )

    def p_copy(step):
        other = pb_peer(step)
        return pltpu.make_async_remote_copy(
            src_ref=part_ref, dst_ref=parts.at[pb],
            send_sem=p_ss, recv_sem=p_rs,
            device_id=(other, ka), device_id_type=MESH,
        )

    def b_copy(v, step):
        other = ka_peer(step)
        return pltpu.make_async_remote_copy(
            src_ref=bsend.at[v, other], dst_ref=brecv.at[v, ka],
            send_sem=b_ss.at[v], recv_sem=b_rs.at[v],
            device_id=(pb, other), device_id_type=MESH,
        )

    def q_copy(v, step):
        other = pb_peer(step)
        return pltpu.make_async_remote_copy(
            src_ref=qsend.at[v, other], dst_ref=qrecv.at[v, pb],
            send_sem=q_ss.at[v], recv_sem=q_rs.at[v],
            device_id=(other, ka), device_id_type=MESH,
        )

    def wait_all(ref, count, sem):
        part = ref.at[pl.ds(0, count)]
        pltpu.make_async_copy(part, part, sem).wait()

    def loop(first, last, do):
        def step_of(step, carry):
            do(step)
            return carry

        lax.fori_loop(first, last, step_of, 0)

    loop(1, NPB, lambda s: c_copy(0, s).start())
    loop(1, NZ, lambda s: z_copy(s).start())
    loop(1, NPB, lambda s: c_copy(1, s).start())
    loop(1, NPB, lambda s: c_copy(2, s).start())
    loop(1, NPB, lambda s: p_copy(s).start())

    def turn(points, first, extra):
        t = extra
        for axis in range(3):
            t = t + points[:, axis : axis + 1] * lat_ref[first + axis : first + axis + 1, :]
        return (2.0 * math.pi) * (t - jnp.round(t))

    ang = turn(kp_ref[...], 0, jnp.zeros((NKA, 1024), F32))
    ck[...] = jnp.cos(ang)
    sk[...] = jnp.sin(ang)
    ang = turn(qp_ref[...], 3, jnp.broadcast_to(lat_ref[6:7, :], (NPB, 1024)))
    cq[...] = jnp.cos(ang)
    sq[...] = jnp.sin(ang)

    wmat[...] = jnp.zeros_like(wmat)
    for i2 in range(2):
        rows0 = pl.ds(i2 * 64, 64)
        rows1 = pl.ds(128 + i2 * 64, 64)
        lanes0 = pl.ds(i2 * 128, 128)
        lanes1 = pl.ds(256 + i2 * 128, 128)
        wmat[rows0, lanes0] = near_ref[0]
        wmat[rows1, lanes0] = near_ref[1]
        wmat[rows0, lanes1] = -near_ref[1]
        wmat[rows1, lanes1] = near_ref[0]

    table[xi, zi] = eig_ref[...]
    parts[pb] = part_ref[...]

    def make_phase(k):
        c = ck[pl.ds(k, 1), :]
        s = sk[pl.ds(k, 1), :]
        phase[k, 0:16, :] = (c * cq[...] - s * sq[...]).astype(BF16)
        phase[k, 16:32, :] = (s * cq[...] + c * sq[...]).astype(BF16)

    with jax.named_scope("phases"):
        loop(0, NKA, make_phase)

    with jax.named_scope("vectors_wait"):
        wait_all(table.at[0], NZ - 1, z_rs)
        loop(1, NX, lambda s: x_copy(s).start())

    own.wait()

    def bloch_of(v):
        with jax.named_scope("couplings_wait"):
            wait_all(cols.at[v], NPB - 1, c_rs.at[v])

        def part(n):
            rows = pl.ds(n * 8, 8)
            got = jnp.dot(
                phase[rows].reshape(256, 1024), cols[v].reshape(1024, 128),
                preferred_element_type=F32,
            )
            bsend[v, rows] = got.astype(BF16).reshape(8, 32, 128)

        with jax.named_scope("bloch"):
            loop(0, 4, part)
        with jax.named_scope("bloch_send"):
            loop(1, NKA, lambda s: b_copy(v, s).start())
        brecv[v, ka] = bsend[v, ka]

    loop(0, VS, bloch_of)

    with jax.named_scope("vectors_wait_x"):
        wait_all(table, NX - 1, x_rs)
        wait_all(parts, NPB - 1, p_rs)

    low = lax.broadcasted_iota(jnp.int32, (32, 128), 1) < 64

    def squares(q):
        field = jnp.concatenate([tmat[t, pl.ds(q, 32, stride=16), :] for t in range(4)], axis=0)
        label = jnp.max(parts[q])
        far = table[lax.rem(label, NX), label // NX]
        turned = field.T.astype(BF16)
        got = lax.dot_general(
            turned, jnp.concatenate([far, far], axis=0), (((1,), (1,)), ((), ())),
            preferred_element_type=F32,
        )
        got = got * got
        both = got[0:64] + got[64:128]
        return jnp.where(low, both[0:32], both[32:64]).astype(BF16)

    def rotate(v):
        with jax.named_scope("bloch_wait"):
            wait_all(brecv.at[v], NKA - 1, b_rs.at[v])

        def near(n):
            rows = pl.ds(n * 8, 8)
            field = jnp.concatenate(
                [brecv[v, rows, 0:16, :].reshape(128, 128), brecv[v, rows, 16:32, :].reshape(128, 128)],
                axis=1,
            )
            got = jnp.dot(field, wmat[...], preferred_element_type=F32)
            for t in range(4):
                tmat[t, pl.ds(n * 128, 128), :] = got[:, t * 128 : (t + 1) * 128]

        with jax.named_scope("near_rotation"):
            loop(0, 4, near)

        def four(n):
            for s in range(4):
                q = pb_peer(4 * n + s)
                qsend[v, q] = squares(q)

            def send(s):
                @pl.when(s > 0)
                def _():
                    q_copy(v, s).start()

            loop(4 * n, 4 * n + 4, send)

        with jax.named_scope("far_rotation"):
            loop(0, 4, four)
        qrecv[v, pb] = qsend[v, pb]

    loop(0, VS, rotate)

    def place(v):
        with jax.named_scope("squares_wait"):
            wait_all(qrecv.at[v], NPB - 1, q_rs.at[v])

        def one(s):
            spread[pl.ds(3 * s + v, 32, stride=48), :] = qrecv[v, s].astype(F32)

        loop(0, NPB, one)

    loop(0, VS, place)

    with jax.named_scope("output"):
        for n in range(12):
            block = spread[n * 128 : (n + 1) * 128, :].T.astype(BF16)
            out_ref[:, n * 128 : (n + 1) * 128] = block[0:64]
            out_ref[:, 1536 + n * 128 : 1536 + (n + 1) * 128] = block[64:128]

    with jax.named_scope("drain"):
        wait_all(table.at[0], NZ - 1, z_ss)
        wait_all(table, NX - 1, x_ss)
        wait_all(parts, NPB - 1, p_ss)

        def drain(v):
            wait_all(cols.at[v], NPB - 1, c_ss.at[v])
            wait_all(bsend.at[v], NKA - 1, b_ss.at[v])
            wait_all(qsend.at[v], NPB - 1, q_ss.at[v])

        loop(0, VS, drain)


def couple(columns, near, eig, part, kp, qp, lat):
    vmem = pl.BlockSpec(memory_space=pltpu.VMEM)
    dma = pltpu.SemaphoreType.DMA
    return pl.pallas_call(
        kernel,
        out_shape=jax.ShapeDtypeStruct((64, 3072), BF16),
        in_specs=[pl.BlockSpec(memory_space=pl.ANY)] + [vmem] * 6,
        out_specs=vmem,
        scratch_shapes=[
            pltpu.VMEM((NKA, 1024), F32),
            pltpu.VMEM((NKA, 1024), F32),
            pltpu.VMEM((NPB, 1024), F32),
            pltpu.VMEM((NPB, 1024), F32),
            pltpu.VMEM((NKA, 32, 1024), BF16),
            pltpu.VMEM((256, 512), BF16),
            pltpu.VMEM((VS, NPB, 64, 128), BF16),
            pltpu.VMEM((VS, NKA, 32, 128), BF16),
            pltpu.VMEM((VS, NKA, 32, 128), BF16),
            pltpu.VMEM((NX, NZ, 64, 128), BF16),
            pltpu.VMEM((NPB, 8, 128), jnp.int32),
            pltpu.VMEM((4, 512, 128), F32),
            pltpu.VMEM((VS, NPB, 32, 128), BF16),
            pltpu.VMEM((VS, NPB, 32, 128), BF16),
            pltpu.VMEM((1536, 128), F32),
            dma((VS,)), dma((VS,)),
            dma((VS,)), dma((VS,)),
            dma((VS,)), dma((VS,)),
            dma(()), dma(()),
            dma(()), dma(()),
            dma(()), dma(()),
            dma(()),
        ],
        compiler_params=pltpu.CompilerParams(
            collective_id=0, has_side_effects=True, vmem_limit_bytes=40 << 20
        ),
        name="couple",
    )(columns, near, eig, part, kp, qp, lat)


def body(coupling, eigvecs, partner, kpoints, qpoints, lattice):
    columns = coupling.reshape(25, 2, 128, 48).transpose(3, 1, 0, 2)
    columns = jnp.pad(columns, ((0, 0), (0, 0), (0, 7), (0, 0))).reshape(NPB, VS, 64, 128)
    vectors = eigvecs.reshape(2, 64, 64)
    real, imag = vectors[0], vectors[1]
    near = jnp.stack([jnp.concatenate([real, imag], 1), jnp.concatenate([-imag, real], 1)])
    eig = vectors.reshape(2, 32, 2, 64).transpose(3, 0, 2, 1).reshape(64, 128)
    part = jnp.broadcast_to(partner, (8, 128))
    lat = jnp.pad(lattice.astype(F32).reshape(6, NPB, 1, 25), ((0, 0), (0, 0), (0, 0), (0, 7)))
    lat = jnp.broadcast_to(lat, (6, NPB, 2, 32)).reshape(6, 1024)
    quarter = jnp.broadcast_to(jnp.array([0.0, 0.25], F32).reshape(1, 1, 2, 1), (1, NPB, 2, 32))
    lat = jnp.concatenate([lat, quarter.reshape(1, 1024), jnp.zeros((1, 1024), F32)], 0)
    out = couple(columns, near, eig, part, kpoints.T, qpoints.T, lat)
    return out.reshape(1, 1, 196608)


def solution(mesh):
    in_specs = (P("pb", None, "ka"), P("ka", None), P("pb", "ka"), P(), P(), P())
    out_specs = P("pb", "ka", None)
    return jax.shard_map(body, mesh=mesh, in_specs=in_specs, out_specs=out_specs, check_vma=False)
```

```python
import math

import jax
import jax.numpy as jnp
from jax import lax
from jax.experimental import pallas as pl
from jax.experimental.pallas import tpu as pltpu
from jax.sharding import PartitionSpec as P

MESH = pl.DeviceIdType.MESH
NPB = 16
NKA = 32
NZ = 8
NX = 4
VS = 3
F32 = jnp.float32
BF16 = jnp.bfloat16


def kernel(
    c_ref, vec_ref, part_ref, kp_ref, qp_ref, lat_ref, out_ref,
    turned, rest, csend, esend, erecv, cols, points, lat, vecs, eig, part,
    ck, sk, cq, sq, phase, wmat, bsend, brecv, table, parts, tmat, qsend, qrecv, spread,
    c_ss, c_rs, e_ss, e_rs, b_ss, b_rs, q_ss, q_rs, z_ss, z_rs, x_ss, x_rs, p_ss, p_rs,
):
    pb = lax.axis_index("pb")
    ka = lax.axis_index("ka")
    zi = ka // NX
    xi = lax.rem(ka, NX)

    def pb_peer(step):
        return lax.rem(pb + step, NPB)

    def ka_peer(step):
        return lax.rem(ka + step, NKA)

    barrier = pltpu.get_barrier_semaphore()

    def greet_pb(step, carry):
        pl.semaphore_signal(barrier, inc=1, device_id=(pb_peer(step), ka), device_id_type=MESH)
        return carry

    def greet_ka(step, carry):
        pl.semaphore_signal(barrier, inc=1, device_id=(pb, ka_peer(step)), device_id_type=MESH)
        return carry

    lax.fori_loop(1, NPB, greet_pb, 0)
    lax.fori_loop(1, NKA, greet_ka, 0)

    def c_copy(v, step):
        to = pb_peer(step)
        return pltpu.make_async_remote_copy(
            src_ref=csend.at[v, to], dst_ref=cols.at[v, pl.ds(pl.multiple_of(pb * 48, 16), 48)],
            send_sem=c_ss.at[v], recv_sem=c_rs.at[v],
            device_id=(to, ka), device_id_type=MESH,
        )

    def e_copy(step):
        to = pb_peer(step)
        return pltpu.make_async_remote_copy(
            src_ref=esend.at[to], dst_ref=erecv.at[pb],
            send_sem=e_ss, recv_sem=e_rs,
            device_id=(to, ka), device_id_type=MESH,
        )

    def z_copy(step):
        other = lax.rem(zi + step, NZ)
        return pltpu.make_async_remote_copy(
            src_ref=eig, dst_ref=table.at[xi, zi],
            send_sem=z_ss, recv_sem=z_rs,
            device_id=(pb, other * NX + xi), device_id_type=MESH,
        )

    def x_copy(step):
        other = lax.rem(xi + step, NX)
        return pltpu.make_async_remote_copy(
            src_ref=table.at[xi], dst_ref=table.at[xi],
            send_sem=x_ss, recv_sem=x_rs,
            device_id=(pb, zi * NX + other), device_id_type=MESH,
        )

    def p_copy(step):
        other = pb_peer(step)
        return pltpu.make_async_remote_copy(
            src_ref=part, dst_ref=parts.at[pb],
            send_sem=p_ss, recv_sem=p_rs,
            device_id=(other, ka), device_id_type=MESH,
        )

    def b_copy(v, step):
        other = ka_peer(step)
        return pltpu.make_async_remote_copy(
            src_ref=bsend.at[v, other], dst_ref=brecv.at[v, ka],
            send_sem=b_ss.at[v], recv_sem=b_rs.at[v],
            device_id=(pb, other), device_id_type=MESH,
        )

    def q_copy(v, step):
        other = pb_peer(step)
        return pltpu.make_async_remote_copy(
            src_ref=qsend.at[v, other], dst_ref=qrecv.at[v, pb],
            send_sem=q_ss.at[v], recv_sem=q_rs.at[v],
            device_id=(other, ka), device_id_type=MESH,
        )

    def wait_all(ref, count, sem):
        part = ref.at[pl.ds(0, count)]
        pltpu.make_async_copy(part, part, sem).wait()

    def loop(first, last, do):
        def step_of(step, carry):
            do(step)
            return carry

        lax.fori_loop(first, last, step_of, 0)

    low = lax.broadcasted_iota(jnp.int32, (32, 128), 1) < 64
    low64 = lax.broadcasted_iota(jnp.int32, (64, 128), 1) < 64
    line = lax.broadcasted_iota(jnp.int32, (128, 128), 0)
    unit = (line == lax.broadcasted_iota(jnp.int32, (128, 128), 1)).astype(BF16)

    def flip(block):
        return lax.dot_general(unit, block, (((1,), (1,)), ((), ())), preferred_element_type=F32)

    def turn_four(n):
        for t in range(4):
            first = pl.multiple_of((4 * n + t) * 128, 128)
            second = pl.multiple_of(3072 + (4 * n + t) * 128, 128)
            both = jnp.concatenate([c_ref[:, pl.ds(first, 128)], c_ref[:, pl.ds(second, 128)]], axis=0)
            turned[pl.ds(first, 128), :] = flip(both)

    def pick(v):
        def four(n):
            for t in range(4):
                to = 4 * n + t
                field = turned[pl.ds(3 * to + v, 64, stride=48), :].astype(BF16)
                got = flip(jnp.concatenate([field, field], axis=0))
                got = jnp.where(low64, got[0:64], got[64:128])
                csend[v, to] = got[0:48].astype(BF16)
                rest[to, 2 * v : 2 * v + 2, :] = got[48:50]

        loop(0, 4, four)
        cols[v, pl.ds(pl.multiple_of(pb * 48, 16), 48)] = csend[v, pb]

    rest[...] = jnp.zeros_like(rest)
    with jax.named_scope("transpose"):
        loop(0, 6, turn_four)
    with jax.named_scope("pick"):
        pick(0)

    with jax.named_scope("entry"):
        pl.semaphore_wait(barrier, NPB - 1 + NKA - 1)

    loop(1, NPB, lambda s: c_copy(0, s).start())
    with jax.named_scope("pick"):
        pick(1)
        pick(2)
    esend[...] = rest[...].astype(BF16)
    erecv[pb] = esend[pb]
    loop(1, NPB, lambda s: e_copy(s).start())
    loop(1, NPB, lambda s: c_copy(1, s).start())
    loop(1, NPB, lambda s: c_copy(2, s).start())

    with jax.named_scope("vectors"):
        vectors = vec_ref[...]
        vecs[...] = jnp.concatenate([vectors, vectors], axis=1).astype(F32)
        lines = [vecs[pl.ds(64 * c + i2, 32, stride=2), :] for c in range(2) for i2 in range(2)]
        eig[...] = jnp.concatenate(lines, axis=0).T[0:64].astype(BF16)
        table[xi, zi] = eig[...]
        loop(1, NZ, lambda s: z_copy(s).start())
        part[...] = jnp.full((8, 128), part_ref[0, 0], jnp.int32)
        parts[pb] = part[...]
        loop(1, NPB, lambda s: p_copy(s).start())

    def turn(where, first, rows):
        points[...] = jnp.zeros_like(points)
        points[0:3, 0 : where.shape[1]] = where[...]
        across = points[...].T
        t = jnp.zeros((rows, 1024), F32)
        for axis in range(3):
            t = t + across[0:rows, axis : axis + 1] * spots[first + axis : first + axis + 1, :]
        return t

    with jax.named_scope("tables"):
        lane = lax.broadcasted_iota(jnp.int32, (1, 1024), 1)
        source = lax.shift_right_logical(lane * 1366, 16)
        pair = lax.shift_right_logical(lane - 48 * source, 1)
        extra = 25 * lax.shift_right_logical(lane - 768, 4) + 24
        pair = jnp.where(lane < 768, 25 * source + pair, extra)
        quarter = jnp.where(lax.bitwise_and(lane, 1) == 1, 0.25, 0.0)
        lat[...] = jnp.zeros_like(lat)
        lat[0:6, 0:400] = lat_ref[...].astype(F32)
        chosen = (lax.broadcasted_iota(jnp.int32, (512, 1024), 0) == pair).astype(BF16)
        spots = jnp.dot(lat[...].astype(BF16), chosen, preferred_element_type=F32)
        ang = turn(kp_ref, 0, NKA)
        ang = (2.0 * math.pi) * (ang - jnp.round(ang))
        ck[...] = jnp.cos(ang)
        sk[...] = jnp.sin(ang)
        ang = turn(qp_ref, 3, NPB) + quarter
        ang = (2.0 * math.pi) * (ang - jnp.round(ang))
        cq[...] = jnp.cos(ang)
        sq[...] = jnp.sin(ang)

    real, imag = vectors[0:64], vectors[64:128]
    near0 = jnp.concatenate([real, imag], axis=1)
    near1 = jnp.concatenate([-imag, real], axis=1)
    wmat[...] = jnp.zeros_like(wmat)
    for i2 in range(2):
        rows0 = pl.ds(i2 * 64, 64)
        rows1 = pl.ds(128 + i2 * 64, 64)
        lanes0 = pl.ds(i2 * 128, 128)
        lanes1 = pl.ds(256 + i2 * 128, 128)
        wmat[rows0, lanes0] = near0
        wmat[rows1, lanes0] = near1
        wmat[rows0, lanes1] = -near1
        wmat[rows1, lanes1] = near0

    def make_phase(k):
        c = ck[pl.ds(k, 1), :]
        s = sk[pl.ds(k, 1), :]
        phase[k, 0:16, :] = (c * cq[...] - s * sq[...]).astype(BF16)
        phase[k, 16:32, :] = (s * cq[...] + c * sq[...]).astype(BF16)

    with jax.named_scope("phases"):
        loop(0, NKA, make_phase)

    with jax.named_scope("vectors_wait"):
        wait_all(table.at[0], NZ - 1, z_rs)
        loop(1, NX, lambda s: x_copy(s).start())

    with jax.named_scope("rest_wait"):
        wait_all(erecv, NPB - 1, e_rs)

    which = lax.shift_right_logical(lax.broadcasted_iota(jnp.int32, (NPB, 16, 128), 1), 1)

    def bloch_of(v):
        with jax.named_scope("couplings_wait"):
            arrived = cols.at[v, pl.ds(0, 48 * (NPB - 1))]
            pltpu.make_async_copy(arrived, arrived, c_rs.at[v]).wait()
        last = jnp.where(which == v, erecv[...].astype(F32), 0.0).astype(BF16)
        cols[v, 768:1024] = last.reshape(256, 128)

        def part(n):
            rows = pl.ds(n * 8, 8)
            got = jnp.dot(
                phase[rows].reshape(256, 1024), cols[v],
                preferred_element_type=F32,
            )
            bsend[v, rows] = got.astype(BF16).reshape(8, 32, 128)

        with jax.named_scope("bloch"):
            loop(0, 4, part)
        with jax.named_scope("bloch_send"):
            loop(1, NKA, lambda s: b_copy(v, s).start())
        brecv[v, ka] = bsend[v, ka]

    loop(0, VS, bloch_of)

    with jax.named_scope("vectors_wait_x"):
        wait_all(table, NX - 1, x_rs)
        wait_all(parts, NPB - 1, p_rs)

    def squares(q):
        field = jnp.concatenate([tmat[t, pl.ds(q, 32, stride=16), :] for t in range(4)], axis=0)
        label = jnp.max(parts[q])
        far = table[lax.rem(label, NX), label // NX]
        turned = field.T.astype(BF16)
        got = lax.dot_general(
            turned, jnp.concatenate([far, far], axis=0), (((1,), (1,)), ((), ())),
            preferred_element_type=F32,
        )
        got = got * got
        both = got[0:64] + got[64:128]
        return jnp.where(low, both[0:32], both[32:64]).astype(BF16)

    def rotate(v):
        with jax.named_scope("bloch_wait"):
            wait_all(brecv.at[v], NKA - 1, b_rs.at[v])

        def near(n):
            rows = pl.ds(n * 8, 8)
            field = jnp.concatenate(
                [brecv[v, rows, 0:16, :].reshape(128, 128), brecv[v, rows, 16:32, :].reshape(128, 128)],
                axis=1,
            )
            got = jnp.dot(field, wmat[...], preferred_element_type=F32)
            for t in range(4):
                tmat[t, pl.ds(n * 128, 128), :] = got[:, t * 128 : (t + 1) * 128]

        with jax.named_scope("near_rotation"):
            loop(0, 4, near)

        def four(n):
            for s in range(4):
                q = pb_peer(4 * n + s)
                qsend[v, q] = squares(q)

            def send(s):
                @pl.when(s > 0)
                def _():
                    q_copy(v, s).start()

            loop(4 * n, 4 * n + 4, send)

        with jax.named_scope("far_rotation"):
            loop(0, 4, four)
        qrecv[v, pb] = qsend[v, pb]

    loop(0, VS, rotate)

    def place(v):
        with jax.named_scope("squares_wait"):
            wait_all(qrecv.at[v], NPB - 1, q_rs.at[v])

        def one(s):
            spread[pl.ds(3 * s + v, 32, stride=48), :] = qrecv[v, s].astype(F32)

        loop(0, NPB, one)

    loop(0, VS, place)

    with jax.named_scope("output"):
        for n in range(12):
            block = spread[n * 128 : (n + 1) * 128, :].T.astype(BF16)
            out_ref[:, n * 128 : (n + 1) * 128] = block[0:64]
            out_ref[:, 1536 + n * 128 : 1536 + (n + 1) * 128] = block[64:128]

    with jax.named_scope("drain"):
        wait_all(table.at[0], NZ - 1, z_ss)
        wait_all(table, NX - 1, x_ss)
        wait_all(parts, NPB - 1, p_ss)
        wait_all(esend, NPB - 1, e_ss)

        def drain(v):
            wait_all(csend.at[v], NPB - 1, c_ss.at[v])
            wait_all(bsend.at[v], NKA - 1, b_ss.at[v])
            wait_all(qsend.at[v], NPB - 1, q_ss.at[v])

        loop(0, VS, drain)


def couple(columns, vectors, part, kp, qp, lat):
    vmem = pl.BlockSpec(memory_space=pltpu.VMEM)
    dma = pltpu.SemaphoreType.DMA
    return pl.pallas_call(
        kernel,
        out_shape=jax.ShapeDtypeStruct((64, 3072), BF16),
        in_specs=[vmem, vmem, pl.BlockSpec(memory_space=pltpu.SMEM), vmem, vmem, vmem],
        out_specs=vmem,
        scratch_shapes=[
            pltpu.VMEM((3072, 128), F32),
            pltpu.VMEM((NPB, 16, 128), F32),
            pltpu.VMEM((VS, NPB, 48, 128), BF16),
            pltpu.VMEM((NPB, 16, 128), BF16),
            pltpu.VMEM((NPB, 16, 128), BF16),
            pltpu.VMEM((VS, 1024, 128), BF16),
            pltpu.VMEM((8, 128), F32),
            pltpu.VMEM((8, 512), F32),
            pltpu.VMEM((128, 128), F32),
            pltpu.VMEM((64, 128), BF16),
            pltpu.VMEM((8, 128), jnp.int32),
            pltpu.VMEM((NKA, 1024), F32),
            pltpu.VMEM((NKA, 1024), F32),
            pltpu.VMEM((NPB, 1024), F32),
            pltpu.VMEM((NPB, 1024), F32),
            pltpu.VMEM((NKA, 32, 1024), BF16),
            pltpu.VMEM((256, 512), BF16),
            pltpu.VMEM((VS, NKA, 32, 128), BF16),
            pltpu.VMEM((VS, NKA, 32, 128), BF16),
            pltpu.VMEM((NX, NZ, 64, 128), BF16),
            pltpu.VMEM((NPB, 8, 128), jnp.int32),
            pltpu.VMEM((4, 512, 128), F32),
            pltpu.VMEM((VS, NPB, 32, 128), BF16),
            pltpu.VMEM((VS, NPB, 32, 128), BF16),
            pltpu.VMEM((1536, 128), F32),
            dma((VS,)), dma((VS,)),
            dma(()), dma(()),
            dma((VS,)), dma((VS,)),
            dma((VS,)), dma((VS,)),
            dma(()), dma(()),
            dma(()), dma(()),
            dma(()), dma(()),
        ],
        compiler_params=pltpu.CompilerParams(
            collective_id=0, has_side_effects=True, vmem_limit_bytes=40 << 20
        ),
        name="couple",
    )(columns, vectors, part, kp, qp, lat)


def body(coupling, eigvecs, partner, kpoints, qpoints, lattice):
    columns = jnp.pad(coupling.reshape(50, 6144), ((0, 14), (0, 0)))
    out = couple(columns, eigvecs.reshape(128, 64), partner, kpoints, qpoints, lattice)
    return out.reshape(1, 1, 196608)


def solution(mesh):
    in_specs = (P("pb", None, "ka"), P("ka", None), P("pb", "ka"), P(), P(), P())
    out_specs = P("pb", "ka", None)
    return jax.shard_map(body, mesh=mesh, in_specs=in_specs, out_specs=out_specs, check_vma=False)
```

```python
import math

import jax
import jax.numpy as jnp
from jax import lax
from jax.experimental import pallas as pl
from jax.experimental.pallas import tpu as pltpu
from jax.sharding import PartitionSpec as P

MESH = pl.DeviceIdType.MESH
NPB = 16
NKA = 32
NZ = 8
NX = 4
VS = 3
F32 = jnp.float32
BF16 = jnp.bfloat16


def kernel(
    c_hbm, vec_hbm, part_hbm, kp_hbm, qp_hbm, lat_hbm, out_ref,
    c_ref, vec_ref, part_ref, kp_ref, qp_ref, lat_ref, turned, rest, csend, esend, erecv, cols, points, lat, vecs, lines, eig, part,
    ck, sk, cq, sq, phase, wmat, bsend, brecv, table, parts, tmat, qsend, qrecv, spread,
    c_ss, c_rs, e_ss, e_rs, b_ss, b_rs, q_ss, q_rs, z_ss, z_rs, x_ss, x_rs, p_ss, p_rs, in_sem,
):
    pb = lax.axis_index("pb")
    ka = lax.axis_index("ka")
    zi = ka // NX
    xi = lax.rem(ka, NX)

    def pb_peer(step):
        return lax.rem(pb + step, NPB)

    def ka_peer(step):
        return lax.rem(ka + step, NKA)

    inputs = [
        pltpu.make_async_copy(c_hbm, c_ref.at[pl.ds(0, 25)], in_sem.at[0]),
        pltpu.make_async_copy(vec_hbm, vec_ref, in_sem.at[1]),
        pltpu.make_async_copy(part_hbm, part_ref, in_sem.at[2]),
        pltpu.make_async_copy(kp_hbm, kp_ref, in_sem.at[3]),
        pltpu.make_async_copy(qp_hbm, qp_ref, in_sem.at[4]),
        pltpu.make_async_copy(lat_hbm, lat_ref, in_sem.at[5]),
    ]
    for copy in inputs:
        copy.start()

    barrier = pltpu.get_barrier_semaphore()

    def greet_pb(step, carry):
        pl.semaphore_signal(barrier, inc=1, device_id=(pb_peer(step), ka), device_id_type=MESH)
        return carry

    def greet_ka(step, carry):
        pl.semaphore_signal(barrier, inc=1, device_id=(pb, ka_peer(step)), device_id_type=MESH)
        return carry

    lax.fori_loop(1, NPB, greet_pb, 0)
    lax.fori_loop(1, NKA, greet_ka, 0)

    def c_copy(v, step):
        to = pb_peer(step)
        return pltpu.make_async_remote_copy(
            src_ref=csend.at[v, to], dst_ref=cols.at[v, pl.ds(pl.multiple_of(pb * 48, 16), 48)],
            send_sem=c_ss.at[v], recv_sem=c_rs.at[v],
            device_id=(to, ka), device_id_type=MESH,
        )

    def e_copy(step):
        to = pb_peer(step)
        return pltpu.make_async_remote_copy(
            src_ref=esend.at[to], dst_ref=erecv.at[pb],
            send_sem=e_ss, recv_sem=e_rs,
            device_id=(to, ka), device_id_type=MESH,
        )

    def z_copy(step):
        other = lax.rem(zi + step, NZ)
        return pltpu.make_async_remote_copy(
            src_ref=eig, dst_ref=table.at[xi, zi],
            send_sem=z_ss, recv_sem=z_rs,
            device_id=(pb, other * NX + xi), device_id_type=MESH,
        )

    def x_copy(step):
        other = lax.rem(xi + step, NX)
        return pltpu.make_async_remote_copy(
            src_ref=table.at[xi], dst_ref=table.at[xi],
            send_sem=x_ss, recv_sem=x_rs,
            device_id=(pb, zi * NX + other), device_id_type=MESH,
        )

    def p_copy(step):
        other = pb_peer(step)
        return pltpu.make_async_remote_copy(
            src_ref=part, dst_ref=parts.at[pb],
            send_sem=p_ss, recv_sem=p_rs,
            device_id=(other, ka), device_id_type=MESH,
        )

    def b_copy(v, h, other):
        return pltpu.make_async_remote_copy(
            src_ref=bsend.at[v, h, other], dst_ref=brecv.at[v, h, ka],
            send_sem=b_ss.at[v, h], recv_sem=b_rs.at[v, h],
            device_id=(pb, other), device_id_type=MESH,
        )

    def q_copy(v, other):
        return pltpu.make_async_remote_copy(
            src_ref=qsend.at[v, other], dst_ref=qrecv.at[v, pb],
            send_sem=q_ss.at[v], recv_sem=q_rs.at[v],
            device_id=(other, ka), device_id_type=MESH,
        )

    def wait_all(ref, count, sem):
        part = ref.at[pl.ds(0, count)]
        pltpu.make_async_copy(part, part, sem).wait()

    def loop(first, last, do):
        def step_of(step, carry):
            do(step)
            return carry

        lax.fori_loop(first, last, step_of, 0)

    low = lax.broadcasted_iota(jnp.int32, (32, 128), 1) < 64
    low64 = lax.broadcasted_iota(jnp.int32, (64, 128), 1) < 64
    line = lax.broadcasted_iota(jnp.int32, (128, 128), 0)
    unit = (line == lax.broadcasted_iota(jnp.int32, (128, 128), 1)).astype(BF16)

    def flip(block):
        return lax.dot_general(unit, block, (((1,), (1,)), ((), ())), preferred_element_type=F32)

    def turn_some(n):
        for t in range(8):
            first = pl.multiple_of((8 * n + t) * 128, 128)
            second = pl.multiple_of(3072 + (8 * n + t) * 128, 128)
            both = jnp.concatenate(
                [c_ref[:, :, pl.ds(first, 128)].reshape(64, 128), c_ref[:, :, pl.ds(second, 128)].reshape(64, 128)],
                axis=0,
            )
            turned[pl.ds(first, 128), :] = flip(both)

    def pick(v):
        def some(n):
            for t in range(8):
                to = 8 * n + t
                field = turned[pl.ds(3 * to + v, 64, stride=48), :].astype(BF16)
                got = flip(jnp.concatenate([field, field], axis=0))
                got = jnp.where(low64, got[0:64], got[64:128])
                csend[v, to] = got[0:48].astype(BF16)
                rest[to, 2 * v : 2 * v + 2, :] = got[48:50]

        loop(0, 2, some)
        cols[v, pl.ds(pl.multiple_of(pb * 48, 16), 48)] = csend[v, pb]

    rest[...] = jnp.zeros_like(rest)
    c_ref[25:32] = jnp.zeros((7, 2, 6144), BF16)
    inputs[0].wait()
    with jax.named_scope("transpose"):
        loop(0, 3, turn_some)
    with jax.named_scope("pick"):
        pick(0)

    with jax.named_scope("entry"):
        pl.semaphore_wait(barrier, NPB - 1 + NKA - 1)

    loop(1, NPB, lambda s: c_copy(0, s).start())
    with jax.named_scope("pick"):
        pick(1)
        pick(2)
    esend[...] = rest[...].astype(BF16)
    erecv[pb] = esend[pb]
    loop(1, NPB, lambda s: e_copy(s).start())
    loop(1, NPB, lambda s: c_copy(1, s).start())
    loop(1, NPB, lambda s: c_copy(2, s).start())

    with jax.named_scope("vectors"):
        for copy in inputs[1:]:
            copy.wait()
        for t in range(64):
            vecs[t : t + 1, :] = vec_ref[:, t * 128 : (t + 1) * 128].astype(F32)
        across = jnp.concatenate([vecs[...], vecs[...]], axis=0).T
        eig[...] = jnp.where(low64, across[0:64], across[64:128]).astype(BF16)
        table[xi, zi] = eig[...]
        loop(1, NZ, lambda s: z_copy(s).start())
        part[...] = jnp.broadcast_to(part_ref[...], (8, 128))
        parts[pb] = part[...]
        loop(1, NPB, lambda s: p_copy(s).start())

    def turn(where, first, order):
        points[...] = jnp.zeros_like(points)
        points[0:3, 0 : where.shape[1]] = where[...]
        across = points[...].T
        if order is None:
            across = across[0:NKA]
        else:
            across = jnp.concatenate([across[q : q + 1] for q in order], axis=0)
        t = jnp.zeros((across.shape[0], 1024), F32)
        for axis in range(3):
            t = t + across[:, axis : axis + 1] * spots[first + axis : first + axis + 1, :]
        return t

    with jax.named_scope("tables"):
        lane = lax.broadcasted_iota(jnp.int32, (1, 1024), 1)
        source = lax.shift_right_logical(lane * 1366, 16)
        pair = lax.shift_right_logical(lane - 48 * source, 1)
        extra = 25 * lax.shift_right_logical(lane - 768, 4) + 24
        pair = jnp.where(lane < 768, 25 * source + pair, extra)
        quarter = jnp.where(lax.bitwise_and(lane, 1) == 1, 0.25, 0.0)
        lat[...] = jnp.zeros_like(lat)
        lat[0:6, 0:400] = lat_ref[...].astype(F32)
        chosen = (lax.broadcasted_iota(jnp.int32, (512, 1024), 0) == pair).astype(BF16)
        spots = jnp.dot(lat[...].astype(BF16), chosen, preferred_element_type=F32)
        ang = turn(kp_ref, 0, None)
        ang = (2.0 * math.pi) * (ang - jnp.round(ang))
        ck[...] = jnp.cos(ang)
        sk[...] = jnp.sin(ang)
        ang = turn(qp_ref, 3, [2 * y + core for core in range(2) for y in range(8)]) + quarter
        ang = (2.0 * math.pi) * (ang - jnp.round(ang))
        cq[...] = jnp.cos(ang)
        sq[...] = jnp.sin(ang)

    low32 = low64[0:32]
    real, imag = vecs[0:32], vecs[32:64]
    lines[pl.ds(0, 32, stride=2), :] = jnp.where(low32, real, pltpu.roll(imag, 64, 1))
    lines[pl.ds(1, 32, stride=2), :] = jnp.where(low32, pltpu.roll(real, 64, 1), imag)
    both = lines[...]
    near0 = both.astype(BF16)
    near1 = jnp.where(low64, -pltpu.roll(both, 64, 1), pltpu.roll(both, 64, 1)).astype(BF16)
    wmat[...] = jnp.zeros_like(wmat)
    for i2 in range(2):
        rows0 = pl.ds(i2 * 64, 64)
        rows1 = pl.ds(128 + i2 * 64, 64)
        lanes0 = pl.ds(i2 * 128, 128)
        lanes1 = pl.ds(256 + i2 * 128, 128)
        wmat[rows0, lanes0] = near0
        wmat[rows1, lanes0] = near1
        wmat[rows0, lanes1] = -near1
        wmat[rows1, lanes1] = near0

    def make_phase(k):
        c = ck[pl.ds(k, 1), :]
        s = sk[pl.ds(k, 1), :]
        for h in range(2):
            cos_q, sin_q = cq[8 * h : 8 * h + 8, :], sq[8 * h : 8 * h + 8, :]
            both = jnp.concatenate([c * cos_q - s * sin_q, s * cos_q + c * sin_q], axis=0)
            phase[h, k] = both.astype(BF16)

    with jax.named_scope("phases"):
        loop(0, NKA, make_phase)

    with jax.named_scope("vectors_wait"):
        wait_all(table.at[0], NZ - 1, z_rs)
        loop(1, NX, lambda s: x_copy(s).start())

    with jax.named_scope("rest_wait"):
        wait_all(erecv, NPB - 1, e_rs)

    which = lax.shift_right_logical(lax.broadcasted_iota(jnp.int32, (NPB, 16, 128), 1), 1)

    def bloch_of(v):
        with jax.named_scope("couplings_wait"):
            arrived = cols.at[v, pl.ds(0, 48 * (NPB - 1))]
            pltpu.make_async_copy(arrived, arrived, c_rs.at[v]).wait()
        last = jnp.where(which == v, erecv[...].astype(F32), 0.0).astype(BF16)
        cols[v, 768:1024] = last.reshape(256, 128)

        def part(n):
            h = n // 2
            side = lax.rem(n + ka // 16, 2)
            rows = pl.ds(side * 16, 16)
            with jax.named_scope("bloch"):
                got = jnp.dot(
                    phase[h, rows].reshape(256, 1024), cols[v],
                    preferred_element_type=F32,
                )
                bsend[v, h, rows] = got.astype(BF16).reshape(16, 16, 128)

            def send(t):
                other = side * 16 + lax.rem(ka + t, 16)

                @pl.when(other != ka)
                def _():
                    b_copy(v, h, other).start()

            with jax.named_scope("bloch_send"):
                loop(0, 16, send)

        loop(0, 4, part)
        brecv[v, 0, ka] = bsend[v, 0, ka]
        brecv[v, 1, ka] = bsend[v, 1, ka]

    loop(0, VS, bloch_of)

    with jax.named_scope("vectors_wait_x"):
        wait_all(table, NX - 1, x_rs)
        wait_all(parts, NPB - 1, p_rs)

    def squares(q, line):
        field = jnp.concatenate([tmat[t, pl.ds(line, 32, stride=8), :] for t in (0, 2, 1, 3)], axis=0)
        label = jnp.max(parts[q])
        far = table[lax.rem(label, NX), label // NX]
        turned_field = field.T.astype(BF16)
        got = lax.dot_general(
            turned_field, jnp.concatenate([far, far], axis=0), (((1,), (1,)), ((), ())),
            preferred_element_type=F32,
        )
        got = got * got
        both = got[0:64] + got[64:128]
        return jnp.where(low, both[0:32], both[32:64]).astype(BF16)

    def rotate(n):
        v, h = n // 2, lax.rem(n, 2)
        with jax.named_scope("bloch_wait"):
            wait_all(brecv.at[v, h], NKA - 1, b_rs.at[v, h])

        def near(t):
            field = brecv[v, h, pl.ds(t * 16, 16)].astype(F32)
            field = jnp.concatenate(
                [field[:, 0:8].reshape(128, 128), field[:, 8:16].reshape(128, 128)], axis=1
            ).astype(BF16)
            got = jnp.dot(field, wmat[...], preferred_element_type=F32)
            for t4 in range(4):
                tmat[t4, pl.ds(t * 128, 128), :] = got[:, t4 * 128 : (t4 + 1) * 128]

        with jax.named_scope("near_rotation"):
            loop(0, 2, near)

        def four(m):
            for s in range(4):
                line = lax.rem(pb // 2 + 4 * m + s, 8)
                q = 2 * line + h
                qsend[v, q] = squares(q, line)

            def send(s):
                q = 2 * lax.rem(pb // 2 + s, 8) + h

                @pl.when(q != pb)
                def _():
                    q_copy(v, q).start()

            loop(4 * m, 4 * m + 4, send)

        with jax.named_scope("far_rotation"):
            loop(0, 2, four)

    loop(0, 2 * VS, rotate)

    def keep(v):
        qrecv[v, pb] = qsend[v, pb]

    loop(0, VS, keep)

    def place(v):
        with jax.named_scope("squares_wait"):
            wait_all(qrecv.at[v], NPB - 1, q_rs.at[v])

        def one(s):
            spread[pl.ds(3 * s + v, 32, stride=48), :] = qrecv[v, s].astype(F32)

        loop(0, NPB, one)

    loop(0, VS, place)

    with jax.named_scope("output"):
        for n in range(12):
            block = spread[n * 128 : (n + 1) * 128, :].T.astype(BF16)
            out_ref[:, n * 128 : (n + 1) * 128] = block[0:64]
            out_ref[:, 1536 + n * 128 : 1536 + (n + 1) * 128] = block[64:128]

    with jax.named_scope("drain"):
        wait_all(table.at[0], NZ - 1, z_ss)
        wait_all(table, NX - 1, x_ss)
        wait_all(parts, NPB - 1, p_ss)
        wait_all(esend, NPB - 1, e_ss)

        def drain(v):
            wait_all(csend.at[v], NPB - 1, c_ss.at[v])
            wait_all(bsend.at[v, 0], NKA - 1, b_ss.at[v, 0])
            wait_all(bsend.at[v, 1], NKA - 1, b_ss.at[v, 1])
            wait_all(qsend.at[v], NPB - 1, q_ss.at[v])

        loop(0, VS, drain)


def couple(coupling, vectors, part, kp, qp, lat):
    vmem = pl.BlockSpec(memory_space=pltpu.VMEM)
    dma = pltpu.SemaphoreType.DMA
    return pl.pallas_call(
        kernel,
        out_shape=jax.ShapeDtypeStruct((64, 3072), BF16),
        in_specs=[pl.BlockSpec(memory_space=pl.ANY)] * 6,
        out_specs=vmem,
        scratch_shapes=[
            pltpu.VMEM((32, 2, 6144), BF16),
            pltpu.VMEM((1, 8192), BF16),
            pltpu.VMEM((1, 1), jnp.int32),
            pltpu.VMEM((3, NKA), F32),
            pltpu.VMEM((3, NPB), F32),
            pltpu.VMEM((6, 400), jnp.int32),
            pltpu.VMEM((3072, 128), F32),
            pltpu.VMEM((NPB, 16, 128), F32),
            pltpu.VMEM((VS, NPB, 48, 128), BF16),
            pltpu.VMEM((NPB, 16, 128), BF16),
            pltpu.VMEM((NPB, 16, 128), BF16),
            pltpu.VMEM((VS, 1024, 128), BF16),
            pltpu.VMEM((8, 128), F32),
            pltpu.VMEM((8, 512), F32),
            pltpu.VMEM((64, 128), F32),
            pltpu.VMEM((64, 128), F32),
            pltpu.VMEM((64, 128), BF16),
            pltpu.VMEM((8, 128), jnp.int32),
            pltpu.VMEM((NKA, 1024), F32),
            pltpu.VMEM((NKA, 1024), F32),
            pltpu.VMEM((NPB, 1024), F32),
            pltpu.VMEM((NPB, 1024), F32),
            pltpu.VMEM((2, NKA, 16, 1024), BF16),
            pltpu.VMEM((256, 512), BF16),
            pltpu.VMEM((VS, 2, NKA, 16, 128), BF16),
            pltpu.VMEM((VS, 2, NKA, 16, 128), BF16),
            pltpu.VMEM((NX, NZ, 64, 128), BF16),
            pltpu.VMEM((NPB, 8, 128), jnp.int32),
            pltpu.VMEM((4, 256, 128), F32),
            pltpu.VMEM((VS, NPB, 32, 128), BF16),
            pltpu.VMEM((VS, NPB, 32, 128), BF16),
            pltpu.VMEM((1536, 128), F32),
            dma((VS,)), dma((VS,)),
            dma(()), dma(()),
            dma((VS, 2)), dma((VS, 2)),
            dma((VS,)), dma((VS,)),
            dma(()), dma(()),
            dma(()), dma(()),
            dma(()), dma(()),
            dma((6,)),
        ],
        compiler_params=pltpu.CompilerParams(
            collective_id=0, has_side_effects=True, vmem_limit_bytes=60 << 20
        ),
        name="couple",
    )(coupling, vectors, part, kp, qp, lat)


def body(coupling, eigvecs, partner, kpoints, qpoints, lattice):
    out = couple(coupling, eigvecs, partner, kpoints, qpoints, lattice)
    return out.reshape(1, 1, 196608)


def solution(mesh):
    in_specs = (P("pb", None, "ka"), P("ka", None), P("pb", "ka"), P(), P(), P())
    out_specs = P("pb", "ka", None)
    return jax.shard_map(body, mesh=mesh, in_specs=in_specs, out_specs=out_specs, check_vma=False)
```

```python
import math

import jax
import jax.numpy as jnp
from jax import lax
from jax.experimental import pallas as pl
from jax.experimental.pallas import tpu as pltpu
from jax.sharding import PartitionSpec as P

MESH = pl.DeviceIdType.MESH
NPB = 16
NKA = 32
NZ = 8
NX = 4
VS = 3
F32 = jnp.float32
BF16 = jnp.bfloat16


def kernel(
    c_hbm, vec_hbm, part_hbm, kp_hbm, qp_hbm, lat_hbm, out_ref,
    c_ref, vec_ref, part_ref, kp_ref, qp_ref, lat_ref, turned, rest, csend, esend, erecv, cols, points, lat, vecs, lines, eig, part,
    ck, sk, cq, sq, phase, wmat, bsend, brecv, table, parts, tmat, qsend, qrecv, spread,
    c_ss, c_rs, e_ss, e_rs, b_ss, b_rs, q_ss, q_rs, z_ss, z_rs, x_ss, x_rs, p_ss, p_rs, in_sem,
):
    pb = lax.axis_index("pb")
    ka = lax.axis_index("ka")
    zi = ka // NX
    xi = lax.rem(ka, NX)

    def ring_offset(step, size):
        side = 1 - 2 * lax.rem(step, 2)
        return lax.rem(size // 2 + side * ((step + 1) // 2) + size, size)

    core = lax.rem(pb, 2)
    yi = pb // 2
    cores = [1 - core, core]
    xs = [lax.rem(xi + offset, NX) for offset in (2, 1, 3, 0)]

    def pb_each(do):
        def some(step, carry):
            y = lax.rem(yi + ring_offset(step, 8), 8)
            for c in range(2):
                do(2 * step + c, 2 * y + cores[c])
            return carry

        lax.fori_loop(0, 7, some, 0)
        do(14, 2 * yi + cores[0])

    def ka_each(do, first=0, last=NKA - 1):
        def some(step, carry):
            z = lax.rem(zi + ring_offset(step, NZ), NZ)
            for c in range(NX):
                do(NX * step + c, z * NX + xs[c])
            return carry

        lax.fori_loop(first // NX, last // NX, some, 0)
        for c in range(last % NX):
            do(last - last % NX + c, zi * NX + xs[c])

    inputs = [
        pltpu.make_async_copy(c_hbm, c_ref.at[pl.ds(0, 25)], in_sem.at[0]),
        pltpu.make_async_copy(vec_hbm, vec_ref, in_sem.at[1]),
        pltpu.make_async_copy(part_hbm, part_ref, in_sem.at[2]),
        pltpu.make_async_copy(kp_hbm, kp_ref, in_sem.at[3]),
        pltpu.make_async_copy(qp_hbm, qp_ref, in_sem.at[4]),
        pltpu.make_async_copy(lat_hbm, lat_ref, in_sem.at[5]),
    ]
    for copy in inputs:
        copy.start()

    barrier = pltpu.get_barrier_semaphore()

    def greet(to):
        pl.semaphore_signal(barrier, inc=1, device_id=to, device_id_type=MESH)

    pb_each(lambda step, other: greet((other, ka)))
    ka_each(lambda step, other: greet((pb, other)))

    def c_copy(v, to):
        return pltpu.make_async_remote_copy(
            src_ref=csend.at[v, to], dst_ref=cols.at[v, pl.ds(pl.multiple_of(pb * 48, 16), 48)],
            send_sem=c_ss.at[v], recv_sem=c_rs.at[v],
            device_id=(to, ka), device_id_type=MESH,
        )

    def e_copy(to):
        return pltpu.make_async_remote_copy(
            src_ref=esend.at[to], dst_ref=erecv.at[pb],
            send_sem=e_ss, recv_sem=e_rs,
            device_id=(to, ka), device_id_type=MESH,
        )

    def z_copy(step):
        other = lax.rem(zi + step, NZ)
        return pltpu.make_async_remote_copy(
            src_ref=eig, dst_ref=table.at[xi, zi],
            send_sem=z_ss, recv_sem=z_rs,
            device_id=(pb, other * NX + xi), device_id_type=MESH,
        )

    def x_copy(step):
        other = lax.rem(xi + step, NX)
        return pltpu.make_async_remote_copy(
            src_ref=table.at[xi], dst_ref=table.at[xi],
            send_sem=x_ss, recv_sem=x_rs,
            device_id=(pb, zi * NX + other), device_id_type=MESH,
        )

    def p_copy(other):
        return pltpu.make_async_remote_copy(
            src_ref=part, dst_ref=parts.at[pb],
            send_sem=p_ss, recv_sem=p_rs,
            device_id=(other, ka), device_id_type=MESH,
        )

    def b_copy(v, h, step, other):
        return pltpu.make_async_remote_copy(
            src_ref=bsend.at[v, h, step], dst_ref=brecv.at[v, h, ka],
            send_sem=b_ss.at[v, h], recv_sem=b_rs.at[v, h],
            device_id=(pb, other), device_id_type=MESH,
        )

    def q_copy(v, other):
        return pltpu.make_async_remote_copy(
            src_ref=qsend.at[v, other], dst_ref=qrecv.at[v, pb],
            send_sem=q_ss.at[v], recv_sem=q_rs.at[v],
            device_id=(other, ka), device_id_type=MESH,
        )

    def wait_all(ref, count, sem):
        part = ref.at[pl.ds(0, count)]
        pltpu.make_async_copy(part, part, sem).wait()

    def loop(first, last, do):
        def step_of(step, carry):
            do(step)
            return carry

        lax.fori_loop(first, last, step_of, 0)

    low = lax.broadcasted_iota(jnp.int32, (32, 128), 1) < 64
    low64 = lax.broadcasted_iota(jnp.int32, (64, 128), 1) < 64
    line = lax.broadcasted_iota(jnp.int32, (128, 128), 0)
    unit = (line == lax.broadcasted_iota(jnp.int32, (128, 128), 1)).astype(BF16)

    def flip(block):
        return lax.dot_general(unit, block, (((1,), (1,)), ((), ())), preferred_element_type=F32)

    def turn_some(n):
        for t in range(8):
            first = pl.multiple_of((8 * n + t) * 128, 128)
            second = pl.multiple_of(3072 + (8 * n + t) * 128, 128)
            both = jnp.concatenate(
                [c_ref[:, :, pl.ds(first, 128)].reshape(64, 128), c_ref[:, :, pl.ds(second, 128)].reshape(64, 128)],
                axis=0,
            )
            turned[pl.ds(first, 128), :] = flip(both)

    def pick(v):
        def some(n):
            for t in range(8):
                to = 8 * n + t
                field = turned[pl.ds(3 * to + v, 64, stride=48), :].astype(BF16)
                got = flip(jnp.concatenate([field, field], axis=0))
                got = jnp.where(low64, got[0:64], got[64:128])
                csend[v, to] = got[0:48].astype(BF16)
                rest[to, 2 * v : 2 * v + 2, :] = got[48:50]

        loop(0, 2, some)
        cols[v, pl.ds(pl.multiple_of(pb * 48, 16), 48)] = csend[v, pb]

    rest[...] = jnp.zeros_like(rest)
    c_ref[25:32] = jnp.zeros((7, 2, 6144), BF16)
    inputs[0].wait()
    with jax.named_scope("transpose"):
        loop(0, 3, turn_some)
    with jax.named_scope("pick"):
        pick(0)

    with jax.named_scope("entry"):
        pl.semaphore_wait(barrier, NPB - 1 + NKA - 1)

    pb_each(lambda step, other: c_copy(0, other).start())
    with jax.named_scope("pick"):
        pick(1)
        pick(2)
    esend[...] = rest[...].astype(BF16)
    erecv[pb] = esend[pb]
    pb_each(lambda step, other: e_copy(other).start())
    pb_each(lambda step, other: c_copy(1, other).start())
    pb_each(lambda step, other: c_copy(2, other).start())

    with jax.named_scope("vectors"):
        for copy in inputs[1:]:
            copy.wait()
        for t in range(64):
            vecs[t : t + 1, :] = vec_ref[:, t * 128 : (t + 1) * 128].astype(F32)
        across = jnp.concatenate([vecs[...], vecs[...]], axis=0).T
        eig[...] = jnp.where(low64, across[0:64], across[64:128]).astype(BF16)
        table[xi, zi] = eig[...]
        loop(1, NZ, lambda s: z_copy(s).start())
        part[...] = jnp.broadcast_to(part_ref[...], (8, 128))
        parts[pb] = part[...]
        pb_each(lambda step, other: p_copy(other).start())

    def turn(where, first, order):
        points[...] = jnp.zeros_like(points)
        points[0:3, 0 : where.shape[1]] = where[...]
        across = points[...].T
        if order is None:
            across = across[0:NKA]
        else:
            across = jnp.concatenate([across[q : q + 1] for q in order], axis=0)
        t = jnp.zeros((across.shape[0], 1024), F32)
        for axis in range(3):
            t = t + across[:, axis : axis + 1] * spots[first + axis : first + axis + 1, :]
        return t

    with jax.named_scope("tables"):
        lane = lax.broadcasted_iota(jnp.int32, (1, 1024), 1)
        source = lax.shift_right_logical(lane * 1366, 16)
        pair = lax.shift_right_logical(lane - 48 * source, 1)
        extra = 25 * lax.shift_right_logical(lane - 768, 4) + 24
        pair = jnp.where(lane < 768, 25 * source + pair, extra)
        quarter = jnp.where(lax.bitwise_and(lane, 1) == 1, 0.25, 0.0)
        lat[...] = jnp.zeros_like(lat)
        lat[0:6, 0:400] = lat_ref[...].astype(F32)
        chosen = (lax.broadcasted_iota(jnp.int32, (512, 1024), 0) == pair).astype(BF16)
        spots = jnp.dot(lat[...].astype(BF16), chosen, preferred_element_type=F32)
        ang = turn(kp_ref, 0, None)
        ang = (2.0 * math.pi) * (ang - jnp.round(ang))
        ck[...] = jnp.cos(ang)
        sk[...] = jnp.sin(ang)
        ang = turn(qp_ref, 3, [2 * y + core for core in range(2) for y in range(8)]) + quarter
        ang = (2.0 * math.pi) * (ang - jnp.round(ang))
        cq[...] = jnp.cos(ang)
        sq[...] = jnp.sin(ang)

    low32 = low64[0:32]
    real, imag = vecs[0:32], vecs[32:64]
    lines[pl.ds(0, 32, stride=2), :] = jnp.where(low32, real, pltpu.roll(imag, 64, 1))
    lines[pl.ds(1, 32, stride=2), :] = jnp.where(low32, pltpu.roll(real, 64, 1), imag)
    both = lines[...]
    near0 = both.astype(BF16)
    near1 = jnp.where(low64, -pltpu.roll(both, 64, 1), pltpu.roll(both, 64, 1)).astype(BF16)
    wmat[...] = jnp.zeros_like(wmat)
    for i2 in range(2):
        rows0 = pl.ds(i2 * 64, 64)
        rows1 = pl.ds(128 + i2 * 64, 64)
        lanes0 = pl.ds(i2 * 128, 128)
        lanes1 = pl.ds(256 + i2 * 128, 128)
        wmat[rows0, lanes0] = near0
        wmat[rows1, lanes0] = near1
        wmat[rows0, lanes1] = -near1
        wmat[rows1, lanes1] = near0

    def make_phase(step, k):
        c = ck[pl.ds(k, 1), :]
        s = sk[pl.ds(k, 1), :]
        for h in range(2):
            cos_q, sin_q = cq[8 * h : 8 * h + 8, :], sq[8 * h : 8 * h + 8, :]
            both = jnp.concatenate([c * cos_q - s * sin_q, s * cos_q + c * sin_q], axis=0)
            phase[h, step] = both.astype(BF16)

    with jax.named_scope("phases"):
        ka_each(make_phase)
        make_phase(NKA - 1, ka)

    with jax.named_scope("vectors_wait"):
        wait_all(table.at[0], NZ - 1, z_rs)
        loop(1, NX, lambda s: x_copy(s).start())

    with jax.named_scope("rest_wait"):
        wait_all(erecv, NPB - 1, e_rs)

    which = lax.shift_right_logical(lax.broadcasted_iota(jnp.int32, (NPB, 16, 128), 1), 1)

    def bloch_of(v):
        with jax.named_scope("couplings_wait"):
            arrived = cols.at[v, pl.ds(0, 48 * (NPB - 1))]
            pltpu.make_async_copy(arrived, arrived, c_rs.at[v]).wait()
        last = jnp.where(which == v, erecv[...].astype(F32), 0.0).astype(BF16)
        cols[v, 768:1024] = last.reshape(256, 128)

        for h in range(2):
            for first in (0, 16):
                rows = pl.ds(first, 16)
                with jax.named_scope("bloch"):
                    got = jnp.dot(
                        phase[h, rows].reshape(256, 1024), cols[v],
                        preferred_element_type=F32,
                    )
                    bsend[v, h, rows] = got.astype(BF16).reshape(16, 16, 128)
                with jax.named_scope("bloch_send"):
                    ka_each(
                        lambda step, other: b_copy(v, h, step, other).start(),
                        first, min(first + 16, NKA - 1),
                    )

        brecv[v, 0, ka] = bsend[v, 0, NKA - 1]
        brecv[v, 1, ka] = bsend[v, 1, NKA - 1]

    loop(0, VS, bloch_of)

    with jax.named_scope("vectors_wait_x"):
        wait_all(table, NX - 1, x_rs)
        wait_all(parts, NPB - 1, p_rs)

    def squares(q, line):
        field = jnp.concatenate([tmat[t, pl.ds(line, 32, stride=8), :] for t in (0, 2, 1, 3)], axis=0)
        label = jnp.max(parts[q])
        far = table[lax.rem(label, NX), label // NX]
        turned_field = field.T.astype(BF16)
        got = lax.dot_general(
            turned_field, jnp.concatenate([far, far], axis=0), (((1,), (1,)), ((), ())),
            preferred_element_type=F32,
        )
        got = got * got
        both = got[0:64] + got[64:128]
        return jnp.where(low, both[0:32], both[32:64]).astype(BF16)

    def rotate(n):
        v, h = n // 2, lax.rem(n, 2)
        with jax.named_scope("bloch_wait"):
            wait_all(brecv.at[v, h], NKA - 1, b_rs.at[v, h])

        def near(t):
            field = brecv[v, h, pl.ds(t * 16, 16)].astype(F32)
            field = jnp.concatenate(
                [field[:, 0:8].reshape(128, 128), field[:, 8:16].reshape(128, 128)], axis=1
            ).astype(BF16)
            got = jnp.dot(field, wmat[...], preferred_element_type=F32)
            for t4 in range(4):
                tmat[t4, pl.ds(t * 128, 128), :] = got[:, t4 * 128 : (t4 + 1) * 128]

        with jax.named_scope("near_rotation"):
            loop(0, 2, near)

        def four(m):
            others = []
            for s in range(4):
                line = lax.rem(yi + ring_offset(4 * m + s, 8), 8)
                q = 2 * line + h
                others.append(q)
                qsend[v, q] = squares(q, line)

            for s in range(4):
                @pl.when(others[s] != pb)
                def _():
                    q_copy(v, others[s]).start()

        with jax.named_scope("far_rotation"):
            loop(0, 2, four)

    loop(0, 2 * VS, rotate)

    def keep(v):
        qrecv[v, pb] = qsend[v, pb]

    loop(0, VS, keep)

    def place(v):
        with jax.named_scope("squares_wait"):
            wait_all(qrecv.at[v], NPB - 1, q_rs.at[v])

        def one(s):
            spread[pl.ds(3 * s + v, 32, stride=48), :] = qrecv[v, s].astype(F32)

        loop(0, NPB, one)

    loop(0, VS, place)

    with jax.named_scope("output"):
        for n in range(12):
            block = spread[n * 128 : (n + 1) * 128, :].T.astype(BF16)
            out_ref[:, n * 128 : (n + 1) * 128] = block[0:64]
            out_ref[:, 1536 + n * 128 : 1536 + (n + 1) * 128] = block[64:128]

    with jax.named_scope("drain"):
        wait_all(table.at[0], NZ - 1, z_ss)
        wait_all(table, NX - 1, x_ss)
        wait_all(parts, NPB - 1, p_ss)
        wait_all(esend, NPB - 1, e_ss)

        def drain(v):
            wait_all(csend.at[v], NPB - 1, c_ss.at[v])
            wait_all(bsend.at[v, 0], NKA - 1, b_ss.at[v, 0])
            wait_all(bsend.at[v, 1], NKA - 1, b_ss.at[v, 1])
            wait_all(qsend.at[v], NPB - 1, q_ss.at[v])

        loop(0, VS, drain)


def couple(coupling, vectors, part, kp, qp, lat):
    vmem = pl.BlockSpec(memory_space=pltpu.VMEM)
    dma = pltpu.SemaphoreType.DMA
    return pl.pallas_call(
        kernel,
        out_shape=jax.ShapeDtypeStruct((64, 3072), BF16),
        in_specs=[pl.BlockSpec(memory_space=pltpu.HBM)] * 6,
        out_specs=vmem,
        scratch_shapes=[
            pltpu.VMEM((32, 2, 6144), BF16),
            pltpu.VMEM((1, 8192), BF16),
            pltpu.VMEM((1, 1), jnp.int32),
            pltpu.VMEM((3, NKA), F32),
            pltpu.VMEM((3, NPB), F32),
            pltpu.VMEM((6, 400), jnp.int32),
            pltpu.VMEM((3072, 128), F32),
            pltpu.VMEM((NPB, 16, 128), F32),
            pltpu.VMEM((VS, NPB, 48, 128), BF16),
            pltpu.VMEM((NPB, 16, 128), BF16),
            pltpu.VMEM((NPB, 16, 128), BF16),
            pltpu.VMEM((VS, 1024, 128), BF16),
            pltpu.VMEM((8, 128), F32),
            pltpu.VMEM((8, 512), F32),
            pltpu.VMEM((64, 128), F32),
            pltpu.VMEM((64, 128), F32),
            pltpu.VMEM((64, 128), BF16),
            pltpu.VMEM((8, 128), jnp.int32),
            pltpu.VMEM((NKA, 1024), F32),
            pltpu.VMEM((NKA, 1024), F32),
            pltpu.VMEM((NPB, 1024), F32),
            pltpu.VMEM((NPB, 1024), F32),
            pltpu.VMEM((2, NKA, 16, 1024), BF16),
            pltpu.VMEM((256, 512), BF16),
            pltpu.VMEM((VS, 2, NKA, 16, 128), BF16),
            pltpu.VMEM((VS, 2, NKA, 16, 128), BF16),
            pltpu.VMEM((NX, NZ, 64, 128), BF16),
            pltpu.VMEM((NPB, 8, 128), jnp.int32),
            pltpu.VMEM((4, 256, 128), F32),
            pltpu.VMEM((VS, NPB, 32, 128), BF16),
            pltpu.VMEM((VS, NPB, 32, 128), BF16),
            pltpu.VMEM((1536, 128), F32),
            dma((VS,)), dma((VS,)),
            dma(()), dma(()),
            dma((VS, 2)), dma((VS, 2)),
            dma((VS,)), dma((VS,)),
            dma(()), dma(()),
            dma(()), dma(()),
            dma(()), dma(()),
            dma((6,)),
        ],
        compiler_params=pltpu.CompilerParams(
            collective_id=0, has_side_effects=True, vmem_limit_bytes=60 << 20
        ),
        name="couple",
    )(coupling, vectors, part, kp, qp, lat)


def body(coupling, eigvecs, partner, kpoints, qpoints, lattice):
    out = couple(coupling, eigvecs, partner, kpoints, qpoints, lattice)
    return out.reshape(1, 1, 196608)


def solution(mesh):
    in_specs = (P("pb", None, "ka"), P("ka", None), P("pb", "ka"), P(), P(), P())
    out_specs = P("pb", "ka", None)
    return jax.shard_map(body, mesh=mesh, in_specs=in_specs, out_specs=out_specs, check_vma=False)
```

```python
import math

import jax
import jax.numpy as jnp
from jax import lax
from jax.experimental import pallas as pl
from jax.experimental.pallas import tpu as pltpu
from jax.sharding import PartitionSpec as P

MESH = pl.DeviceIdType.MESH
NPB = 16
NKA = 32
NZ = 8
NX = 4
VS = 3
F32 = jnp.float32
BF16 = jnp.bfloat16


def kernel(
    c_hbm, vec_hbm, part_hbm, kp_hbm, qp_hbm, lat_hbm, out_ref,
    c_ref, vec_ref, part_ref, kp_ref, qp_ref, lat_ref, turned, rest, csend, esend, erecv, cols, points, grid, lat, vecs, lines, eig, part,
    ck, sk, cq, sq, phase, wmat, bsend, brecv, table, parts, tmat, qsend, qrecv, spread,
    c_ss, c_rs, e_ss, e_rs, b_ss, b_rs, q_ss, q_rs, z_ss, z_rs, x_ss, x_rs, m_ss, m_rs, p_ss, p_rs, in_sem, c_sem, inside,
):
    pb = lax.axis_index("pb")
    ka = lax.axis_index("ka")
    zi = ka // NX
    xi = lax.rem(ka, NX)

    def ring_offset(step, size):
        side = 1 - 2 * lax.rem(step, 2)
        return lax.rem(size // 2 + side * ((step + 1) // 2) + size, size)

    core = lax.rem(pb, 2)
    yi = pb // 2
    cores = [1 - core, core]
    xs = [lax.rem(xi + offset, NX) for offset in (2, 1, 3, 0)]

    def pb_each(do):
        def some(step, carry):
            y = lax.rem(yi + ring_offset(step, 8), 8)
            for c in range(2):
                do(2 * step + c, 2 * y + cores[c])
            return carry

        lax.fori_loop(0, 7, some, 0)
        do(14, 2 * yi + cores[0])

    def planes_each(do, first=0, last=NZ):
        def some(plane, carry):
            for c in range(NX):
                do(NX * plane + c, plane * NX + xs[c], True if c < NX - 1 else plane != zi)
            return carry

        lax.fori_loop(first, last, some, 0)

    def c_piece(n):
        lanes = pl.ds(n * 1024, 1024)
        return pltpu.make_async_copy(c_hbm.at[:, :, lanes], c_ref.at[pl.ds(0, 25), :, lanes], c_sem.at[n])

    for n in (0, 3, 1, 4, 2, 5):
        c_piece(n).start()
    inputs = [
        pltpu.make_async_copy(vec_hbm, vec_ref, in_sem.at[0]),
        pltpu.make_async_copy(part_hbm, part_ref, in_sem.at[1]),
        pltpu.make_async_copy(kp_hbm, kp_ref, in_sem.at[2]),
        pltpu.make_async_copy(qp_hbm, qp_ref, in_sem.at[3]),
        pltpu.make_async_copy(lat_hbm, lat_ref, in_sem.at[4]),
    ]
    for copy in inputs:
        copy.start()

    barrier = pltpu.get_barrier_semaphore()

    def greet(to):
        pl.semaphore_signal(barrier, inc=1, device_id=to, device_id_type=MESH)

    pb_each(lambda step, other: greet((other, ka)))
    for c in range(NX - 1):
        greet((pb, zi * NX + xs[c]))

    def greet_above(plane, carry):
        for c in range(NX):
            greet((pb, plane * NX + xs[c]))
        return carry

    lax.fori_loop(zi + 1, NZ, greet_above, 0)

    def c_copy(v, to):
        return pltpu.make_async_remote_copy(
            src_ref=csend.at[v, to], dst_ref=cols.at[v, pl.ds(pl.multiple_of(pb * 48, 16), 48)],
            send_sem=c_ss.at[v], recv_sem=c_rs.at[v],
            device_id=(to, ka), device_id_type=MESH,
        )

    def e_copy(to):
        return pltpu.make_async_remote_copy(
            src_ref=esend.at[to], dst_ref=erecv.at[pb],
            send_sem=e_ss, recv_sem=e_rs,
            device_id=(to, ka), device_id_type=MESH,
        )

    def z_copy(plane):
        return pltpu.make_async_remote_copy(
            src_ref=eig, dst_ref=table.at[core, xi, zi // 2],
            send_sem=z_ss, recv_sem=z_rs,
            device_id=(pb, plane * NX + xi), device_id_type=MESH,
        )

    def x_copy(other):
        return pltpu.make_async_remote_copy(
            src_ref=table.at[core, xi], dst_ref=table.at[core, xi],
            send_sem=x_ss, recv_sem=x_rs,
            device_id=(pb, zi * NX + other), device_id_type=MESH,
        )

    def m_copy():
        return pltpu.make_async_remote_copy(
            src_ref=table.at[core], dst_ref=table.at[core],
            send_sem=m_ss, recv_sem=m_rs,
            device_id=(2 * yi + cores[0], ka), device_id_type=MESH,
        )

    def b_send(v, h, step, other, remote):
        if remote is True:
            b_copy(v, h, step, other).start()
        else:
            @pl.when(remote)
            def _():
                b_copy(v, h, step, other).start()

    def p_copy(other):
        return pltpu.make_async_remote_copy(
            src_ref=part, dst_ref=parts.at[pb],
            send_sem=p_ss, recv_sem=p_rs,
            device_id=(other, ka), device_id_type=MESH,
        )

    def b_copy(v, h, step, other):
        return pltpu.make_async_remote_copy(
            src_ref=bsend.at[v, h, step], dst_ref=brecv.at[v, h, ka],
            send_sem=b_ss.at[v, h], recv_sem=b_rs.at[v, h],
            device_id=(pb, other), device_id_type=MESH,
        )

    def q_copy(v, other):
        return pltpu.make_async_remote_copy(
            src_ref=qsend.at[v, other], dst_ref=qrecv.at[v, pb],
            send_sem=q_ss.at[v], recv_sem=q_rs.at[v],
            device_id=(other, ka), device_id_type=MESH,
        )

    def wait_all(ref, count, sem):
        part = ref.at[pl.ds(0, count)]
        pltpu.make_async_copy(part, part, sem).wait()

    def loop(first, last, do):
        def step_of(step, carry):
            do(step)
            return carry

        lax.fori_loop(first, last, step_of, 0)

    low = lax.broadcasted_iota(jnp.int32, (32, 128), 1) < 64
    low64 = lax.broadcasted_iota(jnp.int32, (64, 128), 1) < 64
    line = lax.broadcasted_iota(jnp.int32, (128, 128), 0)
    unit = (line == lax.broadcasted_iota(jnp.int32, (128, 128), 1)).astype(BF16)

    def flip(block):
        return lax.dot_general(unit, block, (((1,), (1,)), ((), ())), preferred_element_type=F32)

    def turn_some(n):
        c_piece(n).wait()
        c_piece(n + 3).wait()
        for t in range(8):
            first = pl.multiple_of((8 * n + t) * 128, 128)
            second = pl.multiple_of(3072 + (8 * n + t) * 128, 128)
            both = jnp.concatenate(
                [c_ref[:, :, pl.ds(first, 128)].reshape(64, 128), c_ref[:, :, pl.ds(second, 128)].reshape(64, 128)],
                axis=0,
            )
            turned[pl.ds(first, 128), :] = flip(both)

    def pick(v):
        def some(n):
            for t in range(8):
                to = 8 * n + t
                field = turned[pl.ds(3 * to + v, 64, stride=48), :].astype(BF16)
                got = flip(jnp.concatenate([field, field], axis=0))
                got = jnp.where(low64, got[0:64], got[64:128])
                csend[v, to] = got[0:48].astype(BF16)
                rest[to, 2 * v : 2 * v + 2, :] = got[48:50]

        loop(0, 2, some)
        cols[v, pl.ds(pl.multiple_of(pb * 48, 16), 48)] = csend[v, pb]

    rest[...] = jnp.zeros_like(rest)
    c_ref[25:32] = jnp.zeros((7, 2, 6144), BF16)
    with jax.named_scope("transpose"):
        loop(0, 3, turn_some)
    with jax.named_scope("pick"):
        pick(0)

    with jax.named_scope("entry"):
        pl.semaphore_wait(barrier, NPB - 1 + NX - 1 + NX * zi)

    pb_each(lambda step, other: c_copy(0, other).start())

    def tell_below(plane, carry):
        for c in range(NX):
            pl.semaphore_signal(
                inside.at[zi], inc=1, device_id=(pb, plane * NX + xs[c]), device_id_type=MESH
            )
        return carry

    lax.fori_loop(0, zi, tell_below, 0)

    with jax.named_scope("pick"):
        pick(1)
        pick(2)
    esend[...] = rest[...].astype(BF16)
    erecv[pb] = esend[pb]
    pb_each(lambda step, other: e_copy(other).start())
    pb_each(lambda step, other: c_copy(1, other).start())
    pb_each(lambda step, other: c_copy(2, other).start())

    with jax.named_scope("vectors"):
        for copy in inputs:
            copy.wait()
        for t in range(64):
            vecs[t : t + 1, :] = vec_ref[:, t * 128 : (t + 1) * 128].astype(F32)
        across = jnp.concatenate([vecs[...], vecs[...]], axis=0).T
        eig[...] = jnp.where(low64, across[0:64], across[64:128]).astype(BF16)

        @pl.when(lax.rem(zi, 2) == core)
        def _():
            table[core, xi, zi // 2] = eig[...]
            loop(0, zi, lambda plane: z_copy(plane).start())

        part[...] = jnp.broadcast_to(part_ref[...], (8, 128))
        parts[pb] = part[...]
        pb_each(lambda step, other: p_copy(other).start())

    def turn(where, first, order):
        points[...] = jnp.zeros_like(points)
        points[0:3, 0 : where.shape[1]] = where[...]
        across = points[...].T
        if order is None:
            across = across[0:NKA]
        else:
            grid[...] = jnp.concatenate([across[0:NPB], jnp.zeros((NPB, 120), F32)], axis=1)
            across = jnp.concatenate([grid[pl.ds(q, 2), :] for q in order], axis=0)
        t = jnp.zeros((across.shape[0], 1024), F32)
        for axis in range(3):
            t = t + across[:, axis : axis + 1] * spots[first + axis : first + axis + 1, :]
        return t

    with jax.named_scope("tables"):
        lane = lax.broadcasted_iota(jnp.int32, (1, 1024), 1)
        source = lax.shift_right_logical(lane * 1366, 16)
        pair = lax.shift_right_logical(lane - 48 * source, 1)
        extra = 25 * lax.shift_right_logical(lane - 768, 4) + 24
        pair = jnp.where(lane < 768, 25 * source + pair, extra)
        quarter = jnp.where(lax.bitwise_and(lane, 1) == 1, 0.25, 0.0)
        lat[...] = jnp.zeros_like(lat)
        lat[0:6, 0:400] = lat_ref[...].astype(F32)
        chosen = (lax.broadcasted_iota(jnp.int32, (512, 1024), 0) == pair).astype(BF16)
        spots = jnp.dot(lat[...].astype(BF16), chosen, preferred_element_type=F32)
        ang = turn(kp_ref, 0, None)
        ang = (2.0 * math.pi) * (ang - jnp.round(ang))
        ck[...] = jnp.cos(ang)
        sk[...] = jnp.sin(ang)
        ang = turn(qp_ref, 3, [2 * lax.rem(yi + ring_offset(t, 8), 8) for t in range(8)]) + quarter
        ang = (2.0 * math.pi) * (ang - jnp.round(ang))
        cq[...] = jnp.cos(ang)
        sq[...] = jnp.sin(ang)

    low32 = low64[0:32]
    real, imag = vecs[0:32], vecs[32:64]
    lines[pl.ds(0, 32, stride=2), :] = jnp.where(low32, real, pltpu.roll(imag, 64, 1))
    lines[pl.ds(1, 32, stride=2), :] = jnp.where(low32, pltpu.roll(real, 64, 1), imag)
    both = lines[...]
    near0 = both.astype(BF16)
    near1 = jnp.where(low64, -pltpu.roll(both, 64, 1), pltpu.roll(both, 64, 1)).astype(BF16)
    wmat[...] = jnp.zeros_like(wmat)
    for i2 in range(2):
        rows0 = pl.ds(i2 * 64, 64)
        rows1 = pl.ds(128 + i2 * 64, 64)
        lanes0 = pl.ds(i2 * 128, 128)
        lanes1 = pl.ds(256 + i2 * 128, 128)
        wmat[rows0, lanes0] = near0
        wmat[rows1, lanes0] = near1
        wmat[rows0, lanes1] = -near1
        wmat[rows1, lanes1] = near0

    def make_phase(step, k, other):
        c = ck[pl.ds(k, 1), :]
        s = sk[pl.ds(k, 1), :]
        for h in range(2):
            cos_q, sin_q = cq[8 * h : 8 * h + 8, :], sq[8 * h : 8 * h + 8, :]
            both = jnp.concatenate([c * cos_q - s * sin_q, s * cos_q + c * sin_q], axis=0)
            phase[h, step] = both.astype(BF16)

    with jax.named_scope("phases"):
        planes_each(make_phase)

    with jax.named_scope("inside"):
        def enter_above(plane):
            pl.semaphore_wait(inside.at[plane], NX)

            @pl.when(lax.rem(zi, 2) == core)
            def _():
                z_copy(plane).start()

        loop(zi + 1, NZ, enter_above)

    with jax.named_scope("rest_wait"):
        wait_all(erecv, NPB - 1, e_rs)

    which = lax.shift_right_logical(lax.broadcasted_iota(jnp.int32, (NPB, 16, 128), 1), 1)

    def bloch_of(v):
        with jax.named_scope("couplings_wait"):
            arrived = cols.at[v, pl.ds(0, 48 * (NPB - 1))]
            pltpu.make_async_copy(arrived, arrived, c_rs.at[v]).wait()
        last = jnp.where(which == v, erecv[...].astype(F32), 0.0).astype(BF16)
        cols[v, 768:1024] = last.reshape(256, 128)

        for h in range(2):
            for first in (0, 16):
                rows = pl.ds(first, 16)
                with jax.named_scope("bloch"):
                    got = jnp.dot(
                        phase[h, rows].reshape(256, 1024), cols[v],
                        preferred_element_type=F32,
                    )
                    bsend[v, h, rows] = got.astype(BF16).reshape(16, 16, 128)
                with jax.named_scope("bloch_send"):
                    planes_each(lambda *peer: b_send(v, h, *peer), first // NX, first // NX + 4)

        brecv[v, 0, ka] = bsend[v, 0, NX * zi + NX - 1]
        brecv[v, 1, ka] = bsend[v, 1, NX * zi + NX - 1]

    def vectors_x():
        with jax.named_scope("vectors_wait_z"):
            @pl.when(lax.rem(zi, 2) == core)
            def _():
                wait_all(table.at[0, 0], NZ // 2 - 1, z_rs)

            @pl.when(lax.rem(zi, 2) != core)
            def _():
                wait_all(table.at[0, 0], NZ // 2, z_rs)

            for c in range(NX - 1):
                x_copy(xs[c]).start()

    def vectors_core():
        with jax.named_scope("vectors_wait_x"):
            wait_all(table.at[0], NX - 1, x_rs)
            m_copy().start()

    def vectors_done():
        with jax.named_scope("vectors_wait"):
            wait_all(table, 1, m_rs)
            wait_all(parts, NPB - 1, p_rs)

    def squares(q, line):
        field = jnp.concatenate([tmat[t, pl.ds(line, 32, stride=8), :] for t in (0, 2, 1, 3)], axis=0)
        label = jnp.max(parts[q])
        plane = label // NX
        far = table[lax.rem(plane, 2), lax.rem(label, NX), plane // 2]
        turned_field = field.T.astype(BF16)
        got = lax.dot_general(
            turned_field, jnp.concatenate([far, far], axis=0), (((1,), (1,)), ((), ())),
            preferred_element_type=F32,
        )
        got = got * got
        both = got[0:64] + got[64:128]
        return jnp.where(low, both[0:32], both[32:64]).astype(BF16)

    def rotate(n):
        v, h = n // 2, lax.rem(n, 2)
        with jax.named_scope("bloch_wait"):
            wait_all(brecv.at[v, h], NKA - 1, b_rs.at[v, h])

        def near(t):
            field = brecv[v, h, pl.ds(t * 16, 16)].astype(F32)
            field = jnp.concatenate(
                [field[:, 0:8].reshape(128, 128), field[:, 8:16].reshape(128, 128)], axis=1
            ).astype(BF16)
            got = jnp.dot(field, wmat[...], preferred_element_type=F32)
            for t4 in range(4):
                tmat[t4, pl.ds(t * 128, 128), :] = got[:, t4 * 128 : (t4 + 1) * 128]

        with jax.named_scope("near_rotation"):
            loop(0, 2, near)

        def four(m):
            others = []
            for s in range(4):
                line = 4 * m + s
                q = 2 * lax.rem(yi + ring_offset(4 * h + 2 * m + s // 2, 8), 8) + s % 2
                others.append(q)
                qsend[v, q] = squares(q, line)

            for s in range(4):
                @pl.when(others[s] != pb)
                def _():
                    q_copy(v, others[s]).start()

        with jax.named_scope("far_rotation"):
            loop(0, 2, four)

    @pl.when(zi >= 3)
    def _():
        vectors_x()

    bloch_of(0)

    @pl.when(zi < 3)
    def _():
        vectors_x()

    bloch_of(1)
    vectors_core()

    bloch_of(2)
    vectors_done()
    loop(0, 2 * VS, rotate)

    def keep(v):
        qrecv[v, pb] = qsend[v, pb]

    loop(0, VS, keep)

    def place(v):
        with jax.named_scope("squares_wait"):
            wait_all(qrecv.at[v], NPB - 1, q_rs.at[v])

        def one(s):
            spread[pl.ds(3 * s + v, 32, stride=48), :] = qrecv[v, s].astype(F32)

        loop(0, NPB, one)

    loop(0, VS, place)

    with jax.named_scope("output"):
        for n in range(12):
            block = spread[n * 128 : (n + 1) * 128, :].T.astype(BF16)
            out_ref[:, n * 128 : (n + 1) * 128] = block[0:64]
            out_ref[:, 1536 + n * 128 : 1536 + (n + 1) * 128] = block[64:128]

    with jax.named_scope("drain"):
        @pl.when(lax.rem(zi, 2) == core)
        def _():
            gone = cols.at[0, pl.ds(0, 64 * (NZ - 1))]
            pltpu.make_async_copy(gone, gone, z_ss).wait()

        wait_all(table.at[0], NX - 1, x_ss)
        wait_all(table, 1, m_ss)
        wait_all(parts, NPB - 1, p_ss)
        wait_all(esend, NPB - 1, e_ss)

        def drain(v):
            wait_all(csend.at[v], NPB - 1, c_ss.at[v])
            wait_all(bsend.at[v, 0], NKA - 1, b_ss.at[v, 0])
            wait_all(bsend.at[v, 1], NKA - 1, b_ss.at[v, 1])
            wait_all(qsend.at[v], NPB - 1, q_ss.at[v])

        loop(0, VS, drain)


def couple(coupling, vectors, part, kp, qp, lat):
    vmem = pl.BlockSpec(memory_space=pltpu.VMEM)
    dma = pltpu.SemaphoreType.DMA
    return pl.pallas_call(
        kernel,
        out_shape=jax.ShapeDtypeStruct((64, 3072), BF16),
        in_specs=[pl.BlockSpec(memory_space=pltpu.HBM)] * 6,
        out_specs=vmem,
        scratch_shapes=[
            pltpu.VMEM((32, 2, 6144), BF16),
            pltpu.VMEM((1, 8192), BF16),
            pltpu.VMEM((1, 1), jnp.int32),
            pltpu.VMEM((3, NKA), F32),
            pltpu.VMEM((3, NPB), F32),
            pltpu.VMEM((6, 400), jnp.int32),
            pltpu.VMEM((3072, 128), F32),
            pltpu.VMEM((NPB, 16, 128), F32),
            pltpu.VMEM((VS, NPB, 48, 128), BF16),
            pltpu.VMEM((NPB, 16, 128), BF16),
            pltpu.VMEM((NPB, 16, 128), BF16),
            pltpu.VMEM((VS, 1024, 128), BF16),
            pltpu.VMEM((8, 128), F32),
            pltpu.VMEM((NPB, 128), F32),
            pltpu.VMEM((8, 512), F32),
            pltpu.VMEM((64, 128), F32),
            pltpu.VMEM((64, 128), F32),
            pltpu.VMEM((64, 128), BF16),
            pltpu.VMEM((8, 128), jnp.int32),
            pltpu.VMEM((NKA, 1024), F32),
            pltpu.VMEM((NKA, 1024), F32),
            pltpu.VMEM((NPB, 1024), F32),
            pltpu.VMEM((NPB, 1024), F32),
            pltpu.VMEM((2, NKA, 16, 1024), BF16),
            pltpu.VMEM((256, 512), BF16),
            pltpu.VMEM((VS, 2, NKA, 16, 128), BF16),
            pltpu.VMEM((VS, 2, NKA, 16, 128), BF16),
            pltpu.VMEM((2, NX, NZ // 2, 64, 128), BF16),
            pltpu.VMEM((NPB, 8, 128), jnp.int32),
            pltpu.VMEM((4, 256, 128), F32),
            pltpu.VMEM((VS, NPB, 32, 128), BF16),
            pltpu.VMEM((VS, NPB, 32, 128), BF16),
            pltpu.VMEM((1536, 128), F32),
            dma((VS,)), dma((VS,)),
            dma(()), dma(()),
            dma((VS, 2)), dma((VS, 2)),
            dma((VS,)), dma((VS,)),
            dma(()), dma(()),
            dma(()), dma(()),
            dma(()), dma(()),
            dma(()), dma(()),
            dma((5,)),
            dma((6,)),
            pltpu.SemaphoreType.REGULAR((NZ,)),
        ],
        compiler_params=pltpu.CompilerParams(
            collective_id=0, has_side_effects=True, vmem_limit_bytes=60 << 20
        ),
        name="couple",
    )(coupling, vectors, part, kp, qp, lat)


def body(coupling, eigvecs, partner, kpoints, qpoints, lattice):
    out = couple(coupling, eigvecs, partner, kpoints, qpoints, lattice)
    return out.reshape(1, 1, 196608)


def solution(mesh):
    in_specs = (P("pb", None, "ka"), P("ka", None), P("pb", "ka"), P(), P(), P())
    out_specs = P("pb", "ka", None)
    return jax.shard_map(body, mesh=mesh, in_specs=in_specs, out_specs=out_specs, check_vma=False)
```

```python
import math

import jax
import jax.numpy as jnp
from jax import lax
from jax.experimental import pallas as pl
from jax.experimental.pallas import tpu as pltpu
from jax.sharding import PartitionSpec as P

MESH = pl.DeviceIdType.MESH
NPB = 16
NKA = 32
NZ = 8
NX = 4
VS = 3
F32 = jnp.float32
BF16 = jnp.bfloat16


def kernel(
    c_hbm, vec_hbm, part_hbm, kp_hbm, qp_hbm, lat_hbm, out_ref,
    c_ref, vec_ref, part_ref, kp_ref, qp_ref, lat_ref, turned, csend, crecv, cols, points, grid, lat, vecs, lines, eig, part,
    ck, sk, cq, sq, phase, wmat, bsend, brecv, table, parts, tmat, qsend, qrecv, spread,
    c_ss, c_rs, b_ss, b_rs, q_ss, q_rs, z_ss, z_rs, x_ss, x_rs, m_ss, m_rs, p_ss, p_rs, in_sem, c_sem, inside,
):
    pb = lax.axis_index("pb")
    ka = lax.axis_index("ka")
    zi = ka // NX
    xi = lax.rem(ka, NX)

    def ring_offset(step, size):
        side = 1 - 2 * lax.rem(step, 2)
        return lax.rem(size // 2 + side * ((step + 1) // 2) + size, size)

    core = lax.rem(pb, 2)
    yi = pb // 2
    cores = [1 - core, core]
    xs = [lax.rem(xi + offset, NX) for offset in (2, 1, 3, 0)]

    def pb_each(do):
        def some(step, carry):
            y = lax.rem(yi + ring_offset(step, 8), 8)
            for c in range(2):
                do(2 * step + c, 2 * y + cores[c])
            return carry

        lax.fori_loop(0, 7, some, 0)
        do(14, 2 * yi + cores[0])

    def planes_each(do, first=0, last=NZ):
        def some(plane, carry):
            for c in range(NX):
                do(NX * plane + c, plane * NX + xs[c], True if c < NX - 1 else plane != zi)
            return carry

        lax.fori_loop(first, last, some, 0)

    def c_piece(n):
        lanes = pl.ds(n * 1024, 1024)
        return pltpu.make_async_copy(c_hbm.at[:, :, lanes], c_ref.at[pl.ds(0, 25), :, lanes], c_sem.at[n])

    for n in (0, 3, 1, 4, 2, 5):
        c_piece(n).start()
    inputs = [
        pltpu.make_async_copy(vec_hbm, vec_ref, in_sem.at[0]),
        pltpu.make_async_copy(part_hbm, part_ref, in_sem.at[1]),
        pltpu.make_async_copy(kp_hbm, kp_ref, in_sem.at[2]),
        pltpu.make_async_copy(qp_hbm, qp_ref, in_sem.at[3]),
        pltpu.make_async_copy(lat_hbm, lat_ref, in_sem.at[4]),
    ]
    for copy in inputs:
        copy.start()

    barrier = pltpu.get_barrier_semaphore()

    def greet(to):
        pl.semaphore_signal(barrier, inc=1, device_id=to, device_id_type=MESH)

    pb_each(lambda step, other: greet((other, ka)))
    for c in range(NX - 1):
        greet((pb, zi * NX + xs[c]))

    def greet_above(plane, carry):
        for c in range(NX):
            greet((pb, plane * NX + xs[c]))
        return carry

    lax.fori_loop(zi + 1, NZ, greet_above, 0)

    def c_copy(v, to):
        return pltpu.make_async_remote_copy(
            src_ref=csend.at[v, to], dst_ref=crecv.at[v, pb],
            send_sem=c_ss.at[v], recv_sem=c_rs.at[v],
            device_id=(to, ka), device_id_type=MESH,
        )

    def z_copy(plane):
        return pltpu.make_async_remote_copy(
            src_ref=eig, dst_ref=table.at[core, xi, zi // 2],
            send_sem=z_ss, recv_sem=z_rs,
            device_id=(pb, plane * NX + xi), device_id_type=MESH,
        )

    def x_copy(other):
        return pltpu.make_async_remote_copy(
            src_ref=table.at[core, xi], dst_ref=table.at[core, xi],
            send_sem=x_ss, recv_sem=x_rs,
            device_id=(pb, zi * NX + other), device_id_type=MESH,
        )

    def m_copy():
        return pltpu.make_async_remote_copy(
            src_ref=table.at[core], dst_ref=table.at[core],
            send_sem=m_ss, recv_sem=m_rs,
            device_id=(2 * yi + cores[0], ka), device_id_type=MESH,
        )

    def b_send(v, h, step, other, remote):
        if remote is True:
            b_copy(v, h, step, other).start()
        else:
            @pl.when(remote)
            def _():
                b_copy(v, h, step, other).start()

    def p_copy(other):
        return pltpu.make_async_remote_copy(
            src_ref=part, dst_ref=parts.at[pb],
            send_sem=p_ss, recv_sem=p_rs,
            device_id=(other, ka), device_id_type=MESH,
        )

    def b_copy(v, h, step, other):
        return pltpu.make_async_remote_copy(
            src_ref=bsend.at[v, h, step], dst_ref=brecv.at[v, h, ka],
            send_sem=b_ss.at[v, h], recv_sem=b_rs.at[v, h],
            device_id=(pb, other), device_id_type=MESH,
        )

    def q_copy(v, other):
        return pltpu.make_async_remote_copy(
            src_ref=qsend.at[v, other], dst_ref=qrecv.at[v, pb],
            send_sem=q_ss.at[v], recv_sem=q_rs.at[v],
            device_id=(other, ka), device_id_type=MESH,
        )

    def wait_all(ref, count, sem):
        part = ref.at[pl.ds(0, count)]
        pltpu.make_async_copy(part, part, sem).wait()

    def loop(first, last, do):
        def step_of(step, carry):
            do(step)
            return carry

        lax.fori_loop(first, last, step_of, 0)

    low = lax.broadcasted_iota(jnp.int32, (32, 128), 1) < 64
    low64 = lax.broadcasted_iota(jnp.int32, (64, 128), 1) < 64
    line = lax.broadcasted_iota(jnp.int32, (128, 128), 0)
    unit = (line == lax.broadcasted_iota(jnp.int32, (128, 128), 1)).astype(BF16)

    def flip(block):
        return lax.dot_general(unit, block, (((1,), (1,)), ((), ())), preferred_element_type=F32)

    def turn_some(n):
        c_piece(n).wait()
        c_piece(n + 3).wait()
        for t in range(8):
            first = pl.multiple_of((8 * n + t) * 128, 128)
            second = pl.multiple_of(3072 + (8 * n + t) * 128, 128)
            both = jnp.concatenate(
                [c_ref[:, :, pl.ds(first, 128)].reshape(64, 128), c_ref[:, :, pl.ds(second, 128)].reshape(64, 128)],
                axis=0,
            )
            turned[pl.ds(first, 128), :] = flip(both)

    def pick(v):
        def some(n):
            for t in range(8):
                to = 8 * n + t
                field = turned[pl.ds(3 * to + v, 64, stride=48), :].astype(BF16)
                got = flip(jnp.concatenate([field, field], axis=0))
                got = jnp.where(low64, got[0:64], got[64:128])
                csend[v, to] = got[0:50].astype(BF16).reshape(25, 2, 128)

        loop(0, 2, some)
        crecv[v, pb] = csend[v, pb]

    c_ref[25:32] = jnp.zeros((7, 2, 6144), BF16)
    with jax.named_scope("transpose"):
        loop(0, 3, turn_some)
    with jax.named_scope("pick"):
        pick(0)

    with jax.named_scope("entry"):
        pl.semaphore_wait(barrier, NPB - 1 + NX - 1 + NX * zi)

    pb_each(lambda step, other: c_copy(0, other).start())

    def tell_below(plane, carry):
        for c in range(NX):
            pl.semaphore_signal(
                inside.at[zi], inc=1, device_id=(pb, plane * NX + xs[c]), device_id_type=MESH
            )
        return carry

    lax.fori_loop(0, zi, tell_below, 0)

    with jax.named_scope("pick"):
        pick(1)
        pick(2)
    pb_each(lambda step, other: c_copy(1, other).start())
    pb_each(lambda step, other: c_copy(2, other).start())

    with jax.named_scope("vectors"):
        for copy in inputs:
            copy.wait()
        for t in range(64):
            vecs[t : t + 1, :] = vec_ref[:, t * 128 : (t + 1) * 128].astype(F32)
        across = jnp.concatenate([vecs[...], vecs[...]], axis=0).T
        eig[...] = jnp.where(low64, across[0:64], across[64:128]).astype(BF16)

        @pl.when(lax.rem(zi, 2) == core)
        def _():
            table[core, xi, zi // 2] = eig[...]
            loop(0, zi, lambda plane: z_copy(plane).start())

        part[...] = jnp.broadcast_to(part_ref[...], (8, 128))
        parts[pb] = part[...]
        pb_each(lambda step, other: p_copy(other).start())

    def turn(where, first, order):
        points[...] = jnp.zeros_like(points)
        points[0:3, 0 : where.shape[1]] = where[...]
        across = points[...].T
        if order is None:
            across = across[0:NKA]
        else:
            grid[...] = jnp.concatenate([across[0:NPB], jnp.zeros((NPB, 120), F32)], axis=1)
            across = jnp.concatenate([grid[pl.ds(q, 2), :] for q in order], axis=0)
        t = jnp.zeros((across.shape[0], 1024), F32)
        for axis in range(3):
            t = t + across[:, axis : axis + 1] * spots[first + axis : first + axis + 1, :]
        return t

    with jax.named_scope("tables"):
        lane = lax.broadcasted_iota(jnp.int32, (1, 1024), 1)
        pair = lax.shift_right_logical(lane, 1)
        quarter = jnp.where(lax.bitwise_and(lane, 1) == 1, 0.25, 0.0)
        lat[...] = jnp.zeros_like(lat)
        lat[0:6, 0:400] = lat_ref[...].astype(F32)
        chosen = (lax.broadcasted_iota(jnp.int32, (512, 1024), 0) == pair).astype(BF16)
        spots = jnp.dot(lat[...].astype(BF16), chosen, preferred_element_type=F32)
        ang = turn(kp_ref, 0, None)
        ang = (2.0 * math.pi) * (ang - jnp.round(ang))
        ck[...] = jnp.cos(ang)
        sk[...] = jnp.sin(ang)
        ang = turn(qp_ref, 3, [2 * lax.rem(yi + ring_offset(t, 8), 8) for t in range(8)]) + quarter
        ang = (2.0 * math.pi) * (ang - jnp.round(ang))
        cq[...] = jnp.cos(ang)
        sq[...] = jnp.sin(ang)

    low32 = low64[0:32]
    real, imag = vecs[0:32], vecs[32:64]
    lines[pl.ds(0, 32, stride=2), :] = jnp.where(low32, real, pltpu.roll(imag, 64, 1))
    lines[pl.ds(1, 32, stride=2), :] = jnp.where(low32, pltpu.roll(real, 64, 1), imag)
    both = lines[...]
    near0 = both.astype(BF16)
    near1 = jnp.where(low64, -pltpu.roll(both, 64, 1), pltpu.roll(both, 64, 1)).astype(BF16)
    wmat[...] = jnp.zeros_like(wmat)
    for i2 in range(2):
        rows0 = pl.ds(i2 * 64, 64)
        rows1 = pl.ds(128 + i2 * 64, 64)
        lanes0 = pl.ds(i2 * 128, 128)
        lanes1 = pl.ds(256 + i2 * 128, 128)
        wmat[rows0, lanes0] = near0
        wmat[rows1, lanes0] = near1
        wmat[rows0, lanes1] = -near1
        wmat[rows1, lanes1] = near0

    def make_phase(step, k, other):
        c = ck[pl.ds(k, 1), :]
        s = sk[pl.ds(k, 1), :]
        for h in range(2):
            cos_q, sin_q = cq[8 * h : 8 * h + 8, :], sq[8 * h : 8 * h + 8, :]
            both = jnp.concatenate([c * cos_q - s * sin_q, s * cos_q + c * sin_q], axis=0)
            phase[h, step] = both.astype(BF16)

    with jax.named_scope("phases"):
        planes_each(make_phase)

    with jax.named_scope("inside"):
        def enter_above(plane):
            pl.semaphore_wait(inside.at[plane], NX)

            @pl.when(lax.rem(zi, 2) == core)
            def _():
                z_copy(plane).start()

        loop(zi + 1, NZ, enter_above)

    cols[800:1024] = jnp.zeros((224, 128), BF16)

    def bloch_of(v):
        with jax.named_scope("couplings_wait"):
            wait_all(crecv.at[v], NPB - 1, c_rs.at[v])
            cols[0:800] = crecv[v].reshape(800, 128)

        for h in range(2):
            for first in (0, 16):
                rows = pl.ds(first, 16)
                with jax.named_scope("bloch"):
                    got = jnp.dot(
                        phase[h, rows].reshape(256, 1024), cols[...],
                        preferred_element_type=F32,
                    )
                    bsend[v, h, rows] = got.astype(BF16).reshape(16, 16, 128)
                with jax.named_scope("bloch_send"):
                    planes_each(lambda *peer: b_send(v, h, *peer), first // NX, first // NX + 4)

        brecv[v, 0, ka] = bsend[v, 0, NX * zi + NX - 1]
        brecv[v, 1, ka] = bsend[v, 1, NX * zi + NX - 1]

    def vectors_x():
        with jax.named_scope("vectors_wait_z"):
            @pl.when(lax.rem(zi, 2) == core)
            def _():
                wait_all(table.at[0, 0], NZ // 2 - 1, z_rs)

            @pl.when(lax.rem(zi, 2) != core)
            def _():
                wait_all(table.at[0, 0], NZ // 2, z_rs)

            for c in range(NX - 1):
                x_copy(xs[c]).start()

    def vectors_core():
        with jax.named_scope("vectors_wait_x"):
            wait_all(table.at[0], NX - 1, x_rs)
            m_copy().start()

    def vectors_done():
        with jax.named_scope("vectors_wait"):
            wait_all(table, 1, m_rs)
            wait_all(parts, NPB - 1, p_rs)

    def squares(q, line):
        field = jnp.concatenate([tmat[t, pl.ds(line, 32, stride=8), :] for t in (0, 2, 1, 3)], axis=0)
        label = jnp.max(parts[q])
        plane = label // NX
        far = table[lax.rem(plane, 2), lax.rem(label, NX), plane // 2]
        turned_field = field.T.astype(BF16)
        got = lax.dot_general(
            turned_field, jnp.concatenate([far, far], axis=0), (((1,), (1,)), ((), ())),
            preferred_element_type=F32,
        )
        got = got * got
        both = got[0:64] + got[64:128]
        return jnp.where(low, both[0:32], both[32:64]).astype(BF16)

    def rotate(n):
        v, h = n // 2, lax.rem(n, 2)
        with jax.named_scope("bloch_wait"):
            wait_all(brecv.at[v, h], NKA - 1, b_rs.at[v, h])

        def near(t):
            field = brecv[v, h, pl.ds(t * 16, 16)].astype(F32)
            field = jnp.concatenate(
                [field[:, 0:8].reshape(128, 128), field[:, 8:16].reshape(128, 128)], axis=1
            ).astype(BF16)
            got = jnp.dot(field, wmat[...], preferred_element_type=F32)
            for t4 in range(4):
                tmat[t4, pl.ds(t * 128, 128), :] = got[:, t4 * 128 : (t4 + 1) * 128]

        with jax.named_scope("near_rotation"):
            loop(0, 2, near)

        def four(m):
            others = []
            for s in range(4):
                line = 4 * m + s
                q = 2 * lax.rem(yi + ring_offset(4 * h + 2 * m + s // 2, 8), 8) + s % 2
                others.append(q)
                qsend[v, q] = squares(q, line)

            for s in range(4):
                @pl.when(others[s] != pb)
                def _():
                    q_copy(v, others[s]).start()

        with jax.named_scope("far_rotation"):
            loop(0, 2, four)

    @pl.when(zi >= 3)
    def _():
        vectors_x()

    bloch_of(0)

    @pl.when(zi < 3)
    def _():
        vectors_x()

    bloch_of(1)
    vectors_core()

    bloch_of(2)
    vectors_done()
    loop(0, 2 * VS, rotate)

    def keep(v):
        qrecv[v, pb] = qsend[v, pb]

    loop(0, VS, keep)

    def place(v):
        with jax.named_scope("squares_wait"):
            wait_all(qrecv.at[v], NPB - 1, q_rs.at[v])

        def one(s):
            spread[pl.ds(3 * s + v, 32, stride=48), :] = qrecv[v, s].astype(F32)

        loop(0, NPB, one)

    loop(0, VS, place)

    with jax.named_scope("output"):
        for n in range(12):
            block = spread[n * 128 : (n + 1) * 128, :].T.astype(BF16)
            out_ref[:, n * 128 : (n + 1) * 128] = block[0:64]
            out_ref[:, 1536 + n * 128 : 1536 + (n + 1) * 128] = block[64:128]

    with jax.named_scope("drain"):
        @pl.when(lax.rem(zi, 2) == core)
        def _():
            gone = cols.at[pl.ds(0, 64 * (NZ - 1))]
            pltpu.make_async_copy(gone, gone, z_ss).wait()

        wait_all(table.at[0], NX - 1, x_ss)
        wait_all(table, 1, m_ss)
        wait_all(parts, NPB - 1, p_ss)

        def drain(v):
            wait_all(csend.at[v], NPB - 1, c_ss.at[v])
            wait_all(bsend.at[v, 0], NKA - 1, b_ss.at[v, 0])
            wait_all(bsend.at[v, 1], NKA - 1, b_ss.at[v, 1])
            wait_all(qsend.at[v], NPB - 1, q_ss.at[v])

        loop(0, VS, drain)


def couple(coupling, vectors, part, kp, qp, lat):
    vmem = pl.BlockSpec(memory_space=pltpu.VMEM)
    dma = pltpu.SemaphoreType.DMA
    return pl.pallas_call(
        kernel,
        out_shape=jax.ShapeDtypeStruct((64, 3072), BF16),
        in_specs=[pl.BlockSpec(memory_space=pltpu.HBM)] * 6,
        out_specs=vmem,
        scratch_shapes=[
            pltpu.VMEM((32, 2, 6144), BF16),
            pltpu.VMEM((1, 8192), BF16),
            pltpu.VMEM((1, 1), jnp.int32),
            pltpu.VMEM((3, NKA), F32),
            pltpu.VMEM((3, NPB), F32),
            pltpu.VMEM((6, 400), jnp.int32),
            pltpu.VMEM((3072, 128), F32),
            pltpu.VMEM((VS, NPB, 25, 2, 128), BF16),
            pltpu.VMEM((VS, NPB, 25, 2, 128), BF16),
            pltpu.VMEM((1024, 128), BF16),
            pltpu.VMEM((8, 128), F32),
            pltpu.VMEM((NPB, 128), F32),
            pltpu.VMEM((8, 512), F32),
            pltpu.VMEM((64, 128), F32),
            pltpu.VMEM((64, 128), F32),
            pltpu.VMEM((64, 128), BF16),
            pltpu.VMEM((8, 128), jnp.int32),
            pltpu.VMEM((NKA, 1024), F32),
            pltpu.VMEM((NKA, 1024), F32),
            pltpu.VMEM((NPB, 1024), F32),
            pltpu.VMEM((NPB, 1024), F32),
            pltpu.VMEM((2, NKA, 16, 1024), BF16),
            pltpu.VMEM((256, 512), BF16),
            pltpu.VMEM((VS, 2, NKA, 16, 128), BF16),
            pltpu.VMEM((VS, 2, NKA, 16, 128), BF16),
            pltpu.VMEM((2, NX, NZ // 2, 64, 128), BF16),
            pltpu.VMEM((NPB, 8, 128), jnp.int32),
            pltpu.VMEM((4, 256, 128), F32),
            pltpu.VMEM((VS, NPB, 32, 128), BF16),
            pltpu.VMEM((VS, NPB, 32, 128), BF16),
            pltpu.VMEM((1536, 128), F32),
            dma((VS,)), dma((VS,)),
            dma((VS, 2)), dma((VS, 2)),
            dma((VS,)), dma((VS,)),
            dma(()), dma(()),
            dma(()), dma(()),
            dma(()), dma(()),
            dma(()), dma(()),
            dma((5,)),
            dma((6,)),
            pltpu.SemaphoreType.REGULAR((NZ,)),
        ],
        compiler_params=pltpu.CompilerParams(
            collective_id=0, has_side_effects=True, vmem_limit_bytes=60 << 20
        ),
        name="couple",
    )(coupling, vectors, part, kp, qp, lat)


def body(coupling, eigvecs, partner, kpoints, qpoints, lattice):
    out = couple(coupling, eigvecs, partner, kpoints, qpoints, lattice)
    return out.reshape(1, 1, 196608)


def solution(mesh):
    in_specs = (P("pb", None, "ka"), P("ka", None), P("pb", "ka"), P(), P(), P())
    out_specs = P("pb", "ka", None)
    return jax.shard_map(body, mesh=mesh, in_specs=in_specs, out_specs=out_specs, check_vma=False)
```

```python
import math

import jax
import jax.numpy as jnp
from jax import lax
from jax.experimental import pallas as pl
from jax.experimental.pallas import tpu as pltpu
from jax.sharding import PartitionSpec as P

MESH = pl.DeviceIdType.MESH
NPB = 16
NKA = 32
NZ = 8
NX = 4
VS = 3
F32 = jnp.float32
BF16 = jnp.bfloat16


def kernel(
    c_hbm, vec_hbm, part_hbm, kp_hbm, qp_hbm, lat_hbm, out_ref,
    c_ref, vec_ref, part_ref, kp_ref, qp_ref, lat_ref, turned, asend, arecv, csend, crecv, cols, acols, points, grid, lat, vecs, lines, eig, part,
    ck, sk, cq, sq, phase, wmat, wfold, bsend, brecv, table, parts, tmat, qsend, qrecv, spread,
    a_ss, a_rs, c_ss, c_rs, b_ss, b_rs, q_ss, q_rs, z_ss, z_rs, x_ss, x_rs, m_ss, m_rs, p_ss, p_rs, in_sem, c_sem, inside,
):
    pb = lax.axis_index("pb")
    ka = lax.axis_index("ka")
    zi = ka // NX
    xi = lax.rem(ka, NX)

    def ring_offset(step, size):
        side = 1 - 2 * lax.rem(step, 2)
        return lax.rem(size // 2 + side * ((step + 1) // 2) + size, size)

    core = lax.rem(pb, 2)
    yi = pb // 2
    cores = [1 - core, core]
    xs = [lax.rem(xi + offset, NX) for offset in (2, 1, 3, 0)]

    def pb_each(do):
        def some(step, carry):
            y = lax.rem(yi + ring_offset(step, 8), 8)
            for c in range(2):
                do(2 * step + c, 2 * y + cores[c])
            return carry

        lax.fori_loop(0, 7, some, 0)
        do(14, 2 * yi + cores[0])

    def planes_each(do, first=0, last=NZ):
        def some(plane, carry):
            for c in range(NX):
                do(NX * plane + c, plane * NX + xs[c], True if c < NX - 1 else plane != zi)
            return carry

        lax.fori_loop(first, last, some, 0)

    def c_piece(n):
        lanes = pl.ds(n * 1024, 1024)
        return pltpu.make_async_copy(c_hbm.at[:, :, lanes], c_ref.at[pl.ds(0, 25), :, lanes], c_sem.at[n])

    for n in (0, 3, 1, 4, 2, 5):
        c_piece(n).start()
    inputs = [
        pltpu.make_async_copy(vec_hbm, vec_ref, in_sem.at[0]),
        pltpu.make_async_copy(part_hbm, part_ref, in_sem.at[1]),
        pltpu.make_async_copy(kp_hbm, kp_ref, in_sem.at[2]),
        pltpu.make_async_copy(qp_hbm, qp_ref, in_sem.at[3]),
        pltpu.make_async_copy(lat_hbm, lat_ref, in_sem.at[4]),
    ]
    for copy in inputs:
        copy.start()

    barrier = pltpu.get_barrier_semaphore()

    def greet(to):
        pl.semaphore_signal(barrier, inc=1, device_id=to, device_id_type=MESH)

    pb_each(lambda step, other: greet((other, ka)))
    for c in range(NX - 1):
        greet((pb, zi * NX + xs[c]))

    def greet_above(plane, carry):
        for c in range(NX):
            greet((pb, plane * NX + xs[c]))
        return carry

    lax.fori_loop(zi + 1, NZ, greet_above, 0)

    def a_copy(i2, to):
        return pltpu.make_async_remote_copy(
            src_ref=asend.at[i2, to], dst_ref=arecv.at[i2, pb],
            send_sem=a_ss.at[i2], recv_sem=a_rs.at[i2],
            device_id=(to, ka), device_id_type=MESH,
        )

    def c_copy(v, to):
        return pltpu.make_async_remote_copy(
            src_ref=csend.at[v - 1, to], dst_ref=crecv.at[v - 1, pb],
            send_sem=c_ss.at[v - 1], recv_sem=c_rs.at[v - 1],
            device_id=(to, ka), device_id_type=MESH,
        )

    def z_copy(plane):
        return pltpu.make_async_remote_copy(
            src_ref=eig, dst_ref=table.at[core, xi, zi // 2],
            send_sem=z_ss, recv_sem=z_rs,
            device_id=(pb, plane * NX + xi), device_id_type=MESH,
        )

    def x_copy(other):
        return pltpu.make_async_remote_copy(
            src_ref=table.at[core, xi], dst_ref=table.at[core, xi],
            send_sem=x_ss, recv_sem=x_rs,
            device_id=(pb, zi * NX + other), device_id_type=MESH,
        )

    def m_copy():
        return pltpu.make_async_remote_copy(
            src_ref=table.at[core], dst_ref=table.at[core],
            send_sem=m_ss, recv_sem=m_rs,
            device_id=(2 * yi + cores[0], ka), device_id_type=MESH,
        )

    def b_send(v, h, step, other, remote):
        if remote is True:
            b_copy(v, h, step, other).start()
        else:
            @pl.when(remote)
            def _():
                b_copy(v, h, step, other).start()

    def p_copy(other):
        return pltpu.make_async_remote_copy(
            src_ref=part, dst_ref=parts.at[pb],
            send_sem=p_ss, recv_sem=p_rs,
            device_id=(other, ka), device_id_type=MESH,
        )

    def b_copy(v, h, step, other):
        return pltpu.make_async_remote_copy(
            src_ref=bsend.at[v, h, step], dst_ref=brecv.at[v, h, ka],
            send_sem=b_ss.at[v, h], recv_sem=b_rs.at[v, h],
            device_id=(pb, other), device_id_type=MESH,
        )

    def q_copy(v, other):
        return pltpu.make_async_remote_copy(
            src_ref=qsend.at[v, other], dst_ref=qrecv.at[v, pb],
            send_sem=q_ss.at[v], recv_sem=q_rs.at[v],
            device_id=(other, ka), device_id_type=MESH,
        )

    def wait_all(ref, count, sem):
        part = ref.at[pl.ds(0, count)]
        pltpu.make_async_copy(part, part, sem).wait()

    def loop(first, last, do):
        def step_of(step, carry):
            do(step)
            return carry

        lax.fori_loop(first, last, step_of, 0)

    low = lax.broadcasted_iota(jnp.int32, (32, 128), 1) < 64
    low64 = lax.broadcasted_iota(jnp.int32, (64, 128), 1) < 64
    line = lax.broadcasted_iota(jnp.int32, (128, 128), 0)
    unit = (line == lax.broadcasted_iota(jnp.int32, (128, 128), 1)).astype(BF16)

    inner = lax.bitwise_and(line, 63)
    moved = (line - inner) + 2 * lax.bitwise_and(inner, 31) + lax.shift_right_logical(inner, 5)
    by_part = (moved == lax.broadcasted_iota(jnp.int32, (128, 128), 1)).astype(BF16)

    def flip(block, order=unit):
        return lax.dot_general(order, block, (((1,), (1,)), ((), ())), preferred_element_type=F32)

    def turn_some(n):
        c_piece(n).wait()
        c_piece(n + 3).wait()
        for t in range(8):
            first = pl.multiple_of((8 * n + t) * 128, 128)
            second = pl.multiple_of(3072 + (8 * n + t) * 128, 128)
            both = jnp.concatenate(
                [c_ref[:, :, pl.ds(first, 128)].reshape(64, 128), c_ref[:, :, pl.ds(second, 128)].reshape(64, 128)],
                axis=0,
            )
            turned[pl.ds(first, 128), :] = flip(both)

    def mode_of(to, v):
        field = turned[pl.ds(3 * to + v, 64, stride=48), :].astype(BF16)
        return jnp.concatenate([field, field], axis=0)

    def pick_folded(n):
        for t in range(8):
            to = 8 * n + t
            got = flip(mode_of(to, 0), by_part)
            for i2 in range(2):
                block = jnp.where(low, got[64 * i2 : 64 * i2 + 32], got[64 * i2 + 32 : 64 * i2 + 64])
                asend[i2, to] = block[0:26].astype(BF16).reshape(13, 2, 128)

    def pick(v):
        def some(n):
            for t in range(8):
                to = 8 * n + t
                got = flip(mode_of(to, v))
                got = jnp.where(low64, got[0:64], got[64:128])
                csend[v - 1, to] = got[0:50].astype(BF16).reshape(25, 2, 128)

        loop(0, 2, some)
        crecv[v - 1, pb] = csend[v - 1, pb]

    c_ref[25:32] = jnp.zeros((7, 2, 6144), BF16)
    with jax.named_scope("transpose"):
        loop(0, 3, turn_some)
    with jax.named_scope("pick"):
        loop(0, 2, pick_folded)
        arecv[:, pb] = asend[:, pb]

    with jax.named_scope("entry"):
        pl.semaphore_wait(barrier, NPB - 1 + NX - 1 + NX * zi)

    pb_each(lambda step, other: a_copy(0, other).start())
    pb_each(lambda step, other: a_copy(1, other).start())

    def tell_below(plane, carry):
        for c in range(NX):
            pl.semaphore_signal(
                inside.at[zi], inc=1, device_id=(pb, plane * NX + xs[c]), device_id_type=MESH
            )
        return carry

    lax.fori_loop(0, zi, tell_below, 0)

    with jax.named_scope("pick"):
        pick(1)
        pick(2)
    pb_each(lambda step, other: c_copy(1, other).start())
    pb_each(lambda step, other: c_copy(2, other).start())

    with jax.named_scope("vectors"):
        for copy in inputs:
            copy.wait()
        for t in range(64):
            vecs[t : t + 1, :] = vec_ref[:, t * 128 : (t + 1) * 128].astype(F32)
        across = jnp.concatenate([vecs[...], vecs[...]], axis=0).T
        eig[...] = jnp.where(low64, across[0:64], across[64:128]).astype(BF16)

        @pl.when(lax.rem(zi, 2) == core)
        def _():
            table[core, xi, zi // 2] = eig[...]
            loop(0, zi, lambda plane: z_copy(plane).start())

        part[...] = jnp.broadcast_to(part_ref[...], (8, 128))
        parts[pb] = part[...]
        pb_each(lambda step, other: p_copy(other).start())

    def turn(where, first, order):
        points[...] = jnp.zeros_like(points)
        points[0:3, 0 : where.shape[1]] = where[...]
        across = points[...].T
        if order is None:
            across = across[0:NKA]
        else:
            grid[...] = jnp.concatenate([across[0:NPB], jnp.zeros((NPB, 120), F32)], axis=1)
            across = jnp.concatenate([grid[pl.ds(q, 2), :] for q in order], axis=0)
        t = jnp.zeros((across.shape[0], 2048), F32)
        for axis in range(3):
            t = t + across[:, axis : axis + 1] * spots[first + axis : first + axis + 1, :]
        return t

    with jax.named_scope("tables"):
        lane = lax.broadcasted_iota(jnp.int32, (1, 2048), 1)
        inner = lax.bitwise_and(lane, 511)
        folded = inner - lax.shift_right_logical(inner * 2521, 16)
        pair = jnp.where(lane < 1024, lax.shift_right_logical(lane, 1), folded)
        second = jnp.where(lane < 1024, lax.bitwise_and(lane, 1), lax.shift_right_logical(lane - 1024, 9))
        quarter = jnp.where(second == 1, 0.25, 0.0)
        lat[...] = jnp.zeros_like(lat)
        lat[0:6, 0:400] = lat_ref[...].astype(F32)
        chosen = (lax.broadcasted_iota(jnp.int32, (512, 2048), 0) == pair).astype(BF16)
        spots = jnp.dot(lat[...].astype(BF16), chosen, preferred_element_type=F32)
        ang = turn(kp_ref, 0, None)
        ang = (2.0 * math.pi) * (ang - jnp.round(ang))
        ck[...] = jnp.cos(ang)
        sk[...] = jnp.sin(ang)
        ang = turn(qp_ref, 3, [2 * lax.rem(yi + ring_offset(t, 8), 8) for t in range(8)]) + quarter
        ang = (2.0 * math.pi) * (ang - jnp.round(ang))
        cq[...] = jnp.cos(ang)
        sq[...] = jnp.sin(ang)

    low32 = low64[0:32]
    real, imag = vecs[0:32], vecs[32:64]
    lines[pl.ds(0, 32, stride=2), :] = jnp.where(low32, real, pltpu.roll(imag, 64, 1))
    lines[pl.ds(1, 32, stride=2), :] = jnp.where(low32, pltpu.roll(real, 64, 1), imag)
    both = lines[...]
    near0 = both.astype(BF16)
    near1 = jnp.where(low64, -pltpu.roll(both, 64, 1), pltpu.roll(both, 64, 1)).astype(BF16)
    wmat[...] = jnp.zeros_like(wmat)
    wfold[...] = jnp.zeros_like(wfold)
    for i2 in range(2):
        rows0 = pl.ds(i2 * 64, 64)
        rows1 = pl.ds(128 + i2 * 64, 64)
        lanes0 = pl.ds(i2 * 128, 128)
        lanes1 = pl.ds(256 + i2 * 128, 128)
        wmat[rows0, lanes0] = near0
        wmat[rows1, lanes0] = near1
        wmat[rows0, lanes1] = -near1
        wmat[rows1, lanes1] = near0
        rows0 = pl.ds(i2 * 128, 64)
        rows1 = pl.ds(i2 * 128 + 64, 64)
        wfold[rows0, lanes0] = near0
        wfold[rows1, lanes0] = near1
        wfold[rows0, lanes1] = -near1
        wfold[rows1, lanes1] = near0

    def make_phase(step, k, other):
        c = ck[pl.ds(k, 1), :]
        s = sk[pl.ds(k, 1), :]
        for h in range(2):
            cos_q, sin_q = cq[8 * h : 8 * h + 8, :], sq[8 * h : 8 * h + 8, :]
            both = jnp.concatenate([c * cos_q - s * sin_q, s * cos_q + c * sin_q], axis=0)
            phase[h, step] = both.astype(BF16)

    with jax.named_scope("phases"):
        planes_each(make_phase)

    with jax.named_scope("inside"):
        def enter_above(plane):
            pl.semaphore_wait(inside.at[plane], NX)

            @pl.when(lax.rem(zi, 2) == core)
            def _():
                z_copy(plane).start()

        loop(zi + 1, NZ, enter_above)

    cols[800:1024] = jnp.zeros((224, 128), BF16)
    acols[416:512] = jnp.zeros((96, 128), BF16)

    def bloch_folded(i2):
        with jax.named_scope("couplings_wait"):
            wait_all(arecv.at[i2], NPB - 1, a_rs.at[i2])
            acols[0:416] = arecv[i2].reshape(416, 128)

        def part(n):
            rows = pl.ds(8 * n, 8)
            with jax.named_scope("bloch"):
                first = jnp.dot(
                    phase[:, rows, :, 1024:1536].reshape(256, 512), acols[...], preferred_element_type=F32
                ).reshape(2, 8, 2, 8, 128)
                second = jnp.dot(
                    phase[:, rows, :, 1536:2048].reshape(256, 512), acols[...], preferred_element_type=F32
                ).reshape(2, 8, 2, 8, 128)

                def across(block):
                    return pltpu.roll(block.reshape(128, 128), 64, 1).reshape(2, 8, 8, 128)

                real = first[:, :, 0] + across(second[:, :, 0])
                imag = across(first[:, :, 1]) + second[:, :, 1]
                both = jnp.where(low_lane, real, imag)
                both = jnp.concatenate([both[0], both[1]], axis=1)
                bsend[0, i2, rows] = both.astype(BF16)
            with jax.named_scope("bloch_send"):
                planes_each(lambda *peer: b_send(0, i2, *peer), 2 * n, 2 * n + 2)

        loop(0, 4, part)
        brecv[0, i2, ka] = bsend[0, i2, NX * zi + NX - 1]

    low_lane = lax.broadcasted_iota(jnp.int32, (2, 8, 8, 128), 3) < 64

    def bloch_of(v):
        with jax.named_scope("couplings_wait"):
            wait_all(crecv.at[v - 1], NPB - 1, c_rs.at[v - 1])
            cols[0:800] = crecv[v - 1].reshape(800, 128)

        for h in range(2):
            for first in (0, 16):
                rows = pl.ds(first, 16)
                with jax.named_scope("bloch"):
                    got = jnp.dot(
                        phase[h, rows, :, 0:1024].reshape(256, 1024), cols[...],
                        preferred_element_type=F32,
                    )
                    bsend[v, h, rows] = got.astype(BF16).reshape(16, 16, 128)
                with jax.named_scope("bloch_send"):
                    planes_each(lambda *peer: b_send(v, h, *peer), first // NX, first // NX + 4)

        brecv[v, 0, ka] = bsend[v, 0, NX * zi + NX - 1]
        brecv[v, 1, ka] = bsend[v, 1, NX * zi + NX - 1]

    def vectors_x():
        with jax.named_scope("vectors_wait_z"):
            @pl.when(lax.rem(zi, 2) == core)
            def _():
                wait_all(table.at[0, 0], NZ // 2 - 1, z_rs)

            @pl.when(lax.rem(zi, 2) != core)
            def _():
                wait_all(table.at[0, 0], NZ // 2, z_rs)

            for c in range(NX - 1):
                x_copy(xs[c]).start()

    def vectors_core():
        with jax.named_scope("vectors_wait_x"):
            wait_all(table.at[0], NX - 1, x_rs)
            m_copy().start()

    def vectors_done():
        with jax.named_scope("vectors_wait"):
            wait_all(table, 1, m_rs)
            wait_all(parts, NPB - 1, p_rs)

    def squares(q, line):
        field = jnp.concatenate([tmat[t, pl.ds(line, 32, stride=8), :] for t in (0, 2, 1, 3)], axis=0)
        label = jnp.max(parts[q])
        plane = label // NX
        far = table[lax.rem(plane, 2), lax.rem(label, NX), plane // 2]
        turned_field = field.T.astype(BF16)
        got = lax.dot_general(
            turned_field, jnp.concatenate([far, far], axis=0), (((1,), (1,)), ((), ())),
            preferred_element_type=F32,
        )
        got = got * got
        both = got[0:64] + got[64:128]
        return jnp.where(low, both[0:32], both[32:64]).astype(BF16)

    def rotate(n):
        v, h = n // 2, lax.rem(n, 2)
        with jax.named_scope("bloch_wait"):
            @pl.when(n == 0)
            def _():
                wait_all(brecv.at[0, 0], NKA - 1, b_rs.at[0, 0])
                wait_all(brecv.at[0, 1], NKA - 1, b_rs.at[0, 1])

            @pl.when(n > 1)
            def _():
                wait_all(brecv.at[v, h], NKA - 1, b_rs.at[v, h])

        def near(t, pieces, weights):
            field = jnp.concatenate([piece.reshape(128, 128) for piece in pieces], axis=1).astype(BF16)
            got = jnp.dot(field, weights[...], preferred_element_type=F32)
            for t4 in range(4):
                tmat[t4, pl.ds(t * 128, 128), :] = got[:, t4 * 128 : (t4 + 1) * 128]

        def near_folded(t):
            fields = [brecv[0, i2, pl.ds(t * 16, 16)].astype(F32) for i2 in range(2)]
            near(t, [jnp.where(h == 0, field[:, 0:8], field[:, 8:16]) for field in fields], wfold)

        def near_other(t):
            field = brecv[v, h, pl.ds(t * 16, 16)].astype(F32)
            near(t, [field[:, 0:8], field[:, 8:16]], wmat)

        with jax.named_scope("near_rotation"):
            @pl.when(n < 2)
            def _():
                loop(0, 2, near_folded)

            @pl.when(n > 1)
            def _():
                loop(0, 2, near_other)

        def four(m):
            others = []
            for s in range(4):
                line = 4 * m + s
                q = 2 * lax.rem(yi + ring_offset(4 * h + 2 * m + s // 2, 8), 8) + s % 2
                others.append(q)
                qsend[v, q] = squares(q, line)

            for s in range(4):
                @pl.when(others[s] != pb)
                def _():
                    q_copy(v, others[s]).start()

        with jax.named_scope("far_rotation"):
            loop(0, 2, four)

    bloch_folded(0)

    @pl.when(zi >= 3)
    def _():
        vectors_x()

    bloch_folded(1)

    @pl.when(zi < 3)
    def _():
        vectors_x()

    bloch_of(1)
    vectors_core()

    bloch_of(2)
    vectors_done()
    loop(0, 2 * VS, rotate)

    def keep(v):
        qrecv[v, pb] = qsend[v, pb]

    loop(0, VS, keep)

    def place(v):
        with jax.named_scope("squares_wait"):
            wait_all(qrecv.at[v], NPB - 1, q_rs.at[v])

        def one(s):
            spread[pl.ds(3 * s + v, 32, stride=48), :] = qrecv[v, s].astype(F32)

        loop(0, NPB, one)

    loop(0, VS, place)

    with jax.named_scope("output"):
        for n in range(12):
            block = spread[n * 128 : (n + 1) * 128, :].T.astype(BF16)
            out_ref[:, n * 128 : (n + 1) * 128] = block[0:64]
            out_ref[:, 1536 + n * 128 : 1536 + (n + 1) * 128] = block[64:128]

    with jax.named_scope("drain"):
        @pl.when(lax.rem(zi, 2) == core)
        def _():
            gone = cols.at[pl.ds(0, 64 * (NZ - 1))]
            pltpu.make_async_copy(gone, gone, z_ss).wait()

        wait_all(table.at[0], NX - 1, x_ss)
        wait_all(table, 1, m_ss)
        wait_all(parts, NPB - 1, p_ss)

        def drain(v):
            wait_all(bsend.at[v, 0], NKA - 1, b_ss.at[v, 0])
            wait_all(bsend.at[v, 1], NKA - 1, b_ss.at[v, 1])
            wait_all(qsend.at[v], NPB - 1, q_ss.at[v])

        loop(0, VS, drain)
        for n in range(2):
            wait_all(asend.at[n], NPB - 1, a_ss.at[n])
            wait_all(csend.at[n], NPB - 1, c_ss.at[n])


def couple(coupling, vectors, part, kp, qp, lat):
    vmem = pl.BlockSpec(memory_space=pltpu.VMEM)
    dma = pltpu.SemaphoreType.DMA
    return pl.pallas_call(
        kernel,
        out_shape=jax.ShapeDtypeStruct((64, 3072), BF16),
        in_specs=[pl.BlockSpec(memory_space=pltpu.HBM)] * 6,
        out_specs=vmem,
        scratch_shapes=[
            pltpu.VMEM((32, 2, 6144), BF16),
            pltpu.VMEM((1, 8192), BF16),
            pltpu.VMEM((1, 1), jnp.int32),
            pltpu.VMEM((3, NKA), F32),
            pltpu.VMEM((3, NPB), F32),
            pltpu.VMEM((6, 400), jnp.int32),
            pltpu.VMEM((3072, 128), F32),
            pltpu.VMEM((2, NPB, 13, 2, 128), BF16),
            pltpu.VMEM((2, NPB, 13, 2, 128), BF16),
            pltpu.VMEM((VS - 1, NPB, 25, 2, 128), BF16),
            pltpu.VMEM((VS - 1, NPB, 25, 2, 128), BF16),
            pltpu.VMEM((1024, 128), BF16),
            pltpu.VMEM((512, 128), BF16),
            pltpu.VMEM((8, 128), F32),
            pltpu.VMEM((NPB, 128), F32),
            pltpu.VMEM((8, 512), F32),
            pltpu.VMEM((64, 128), F32),
            pltpu.VMEM((64, 128), F32),
            pltpu.VMEM((64, 128), BF16),
            pltpu.VMEM((8, 128), jnp.int32),
            pltpu.VMEM((NKA, 2048), F32),
            pltpu.VMEM((NKA, 2048), F32),
            pltpu.VMEM((NPB, 2048), F32),
            pltpu.VMEM((NPB, 2048), F32),
            pltpu.VMEM((2, NKA, 16, 2048), BF16),
            pltpu.VMEM((256, 512), BF16),
            pltpu.VMEM((256, 512), BF16),
            pltpu.VMEM((VS, 2, NKA, 16, 128), BF16),
            pltpu.VMEM((VS, 2, NKA, 16, 128), BF16),
            pltpu.VMEM((2, NX, NZ // 2, 64, 128), BF16),
            pltpu.VMEM((NPB, 8, 128), jnp.int32),
            pltpu.VMEM((4, 256, 128), F32),
            pltpu.VMEM((VS, NPB, 32, 128), BF16),
            pltpu.VMEM((VS, NPB, 32, 128), BF16),
            pltpu.VMEM((1536, 128), F32),
            dma((2,)), dma((2,)),
            dma((VS - 1,)), dma((VS - 1,)),
            dma((VS, 2)), dma((VS, 2)),
            dma((VS,)), dma((VS,)),
            dma(()), dma(()),
            dma(()), dma(()),
            dma(()), dma(()),
            dma(()), dma(()),
            dma((5,)),
            dma((6,)),
            pltpu.SemaphoreType.REGULAR((NZ,)),
        ],
        compiler_params=pltpu.CompilerParams(
            collective_id=0, has_side_effects=True, vmem_limit_bytes=60 << 20
        ),
        name="couple",
    )(coupling, vectors, part, kp, qp, lat)


def body(coupling, eigvecs, partner, kpoints, qpoints, lattice):
    out = couple(coupling, eigvecs, partner, kpoints, qpoints, lattice)
    return out.reshape(1, 1, 196608)


def solution(mesh):
    in_specs = (P("pb", None, "ka"), P("ka", None), P("pb", "ka"), P(), P(), P())
    out_specs = P("pb", "ka", None)
    return jax.shard_map(body, mesh=mesh, in_specs=in_specs, out_specs=out_specs, check_vma=False)
```

```python
import math

import jax
import jax.numpy as jnp
from jax import lax
from jax.experimental import pallas as pl
from jax.experimental.pallas import tpu as pltpu
from jax.sharding import PartitionSpec as P

MESH = pl.DeviceIdType.MESH
NPB = 16
NKA = 32
NZ = 8
NX = 4
VS = 3
F32 = jnp.float32
BF16 = jnp.bfloat16


def kernel(
    c_hbm, vec_hbm, part_hbm, kp_hbm, qp_hbm, lat_hbm, out_ref,
    c_ref, vec_ref, part_ref, kp_ref, qp_ref, lat_ref, turned, asend, arecv, csend, crecv, cols, acols, points, grid, lat, vecs, lines, eig, part,
    ck, sk, cq, sq, phase, wmat, wfold, bsend, brecv, table, parts, far, tmat, qsend, qrecv, spread,
    a_ss, a_rs, c_ss, c_rs, b_ss, b_rs, q_ss, q_rs, z_ss, z_rs, x_ss, x_rs, m_ss, m_rs, p_ss, p_rs, in_sem, c_sem, inside,
):
    pb = lax.axis_index("pb")
    ka = lax.axis_index("ka")
    zi = ka // NX
    xi = lax.rem(ka, NX)

    def ring_offset(step, size):
        side = 1 - 2 * lax.rem(step, 2)
        return lax.rem(size // 2 + side * ((step + 1) // 2) + size, size)

    core = lax.rem(pb, 2)
    yi = pb // 2
    cores = [1 - core, core]
    xs = [lax.rem(xi + offset, NX) for offset in (2, 1, 3, 0)]

    def pb_each(do):
        def some(step, carry):
            y = lax.rem(yi + ring_offset(step, 8), 8)
            for c in range(2):
                do(2 * step + c, 2 * y + cores[c])
            return carry

        lax.fori_loop(0, 7, some, 0)
        do(14, 2 * yi + cores[0])

    def planes_each(do, first=0, last=NZ):
        def some(plane, carry):
            for c in range(NX):
                do(NX * plane + c, plane * NX + xs[c], True if c < NX - 1 else plane != zi)
            return carry

        lax.fori_loop(first, last, some, 0)

    def c_piece(n):
        lanes = pl.ds(n * 1024, 1024)
        return pltpu.make_async_copy(c_hbm.at[:, :, lanes], c_ref.at[pl.ds(0, 25), :, lanes], c_sem.at[n])

    for n in (0, 3, 1, 4, 2, 5):
        c_piece(n).start()
    inputs = [
        pltpu.make_async_copy(vec_hbm, vec_ref, in_sem.at[0]),
        pltpu.make_async_copy(part_hbm, part_ref, in_sem.at[1]),
        pltpu.make_async_copy(kp_hbm, kp_ref, in_sem.at[2]),
        pltpu.make_async_copy(qp_hbm, qp_ref, in_sem.at[3]),
        pltpu.make_async_copy(lat_hbm, lat_ref, in_sem.at[4]),
    ]
    for copy in inputs:
        copy.start()

    barrier = pltpu.get_barrier_semaphore()

    def greet(to):
        pl.semaphore_signal(barrier, inc=1, device_id=to, device_id_type=MESH)

    pb_each(lambda step, other: greet((other, ka)))
    for c in range(NX - 1):
        greet((pb, zi * NX + xs[c]))

    def greet_above(plane, carry):
        for c in range(NX):
            greet((pb, plane * NX + xs[c]))
        return carry

    lax.fori_loop(zi + 1, NZ, greet_above, 0)

    def a_copy(i2, to):
        return pltpu.make_async_remote_copy(
            src_ref=asend.at[i2, to], dst_ref=arecv.at[i2, pb],
            send_sem=a_ss.at[i2], recv_sem=a_rs.at[i2],
            device_id=(to, ka), device_id_type=MESH,
        )

    def c_copy(v, to):
        return pltpu.make_async_remote_copy(
            src_ref=csend.at[v - 1, to], dst_ref=crecv.at[v - 1, pb],
            send_sem=c_ss.at[v - 1], recv_sem=c_rs.at[v - 1],
            device_id=(to, ka), device_id_type=MESH,
        )

    def z_copy(plane):
        return pltpu.make_async_remote_copy(
            src_ref=eig, dst_ref=table.at[core, xi, zi // 2],
            send_sem=z_ss, recv_sem=z_rs,
            device_id=(pb, plane * NX + xi), device_id_type=MESH,
        )

    def x_copy(other):
        return pltpu.make_async_remote_copy(
            src_ref=table.at[core, xi], dst_ref=table.at[core, xi],
            send_sem=x_ss, recv_sem=x_rs,
            device_id=(pb, zi * NX + other), device_id_type=MESH,
        )

    def m_copy():
        return pltpu.make_async_remote_copy(
            src_ref=table.at[core], dst_ref=table.at[core],
            send_sem=m_ss, recv_sem=m_rs,
            device_id=(2 * yi + cores[0], ka), device_id_type=MESH,
        )

    def b_send(v, h, step, other, remote):
        if remote is True:
            b_copy(v, h, step, other).start()
        else:
            @pl.when(remote)
            def _():
                b_copy(v, h, step, other).start()

    def p_copy(other):
        return pltpu.make_async_remote_copy(
            src_ref=part, dst_ref=parts.at[pb],
            send_sem=p_ss, recv_sem=p_rs,
            device_id=(other, ka), device_id_type=MESH,
        )

    def b_copy(v, h, step, other):
        def piece(ref, row):
            return ref.at[v, row] if h is None else ref.at[v, row, h]

        sem = 0 if h is None else h
        return pltpu.make_async_remote_copy(
            src_ref=piece(bsend, step), dst_ref=piece(brecv, ka),
            send_sem=b_ss.at[v, sem], recv_sem=b_rs.at[v, sem],
            device_id=(pb, other), device_id_type=MESH,
        )

    def q_copy(v, other):
        return pltpu.make_async_remote_copy(
            src_ref=qsend.at[v, other], dst_ref=qrecv.at[v, pb],
            send_sem=q_ss.at[v], recv_sem=q_rs.at[v],
            device_id=(other, ka), device_id_type=MESH,
        )

    def wait_all(ref, count, sem):
        part = ref.at[pl.ds(0, count)]
        pltpu.make_async_copy(part, part, sem).wait()

    def wait_pieces(ref, v, h, sems):
        part = ref.at[v, pl.ds(0, NKA - 1), h]
        pltpu.make_async_copy(part, part, sems.at[v, h]).wait()

    def loop(first, last, do):
        def step_of(step, carry):
            do(step)
            return carry

        lax.fori_loop(first, last, step_of, 0)

    low = lax.broadcasted_iota(jnp.int32, (32, 128), 1) < 64
    low64 = lax.broadcasted_iota(jnp.int32, (64, 128), 1) < 64
    line = lax.broadcasted_iota(jnp.int32, (128, 128), 0)
    unit = (line == lax.broadcasted_iota(jnp.int32, (128, 128), 1)).astype(BF16)

    inner = lax.bitwise_and(line, 63)
    moved = (line - inner) + 2 * lax.bitwise_and(inner, 31) + lax.shift_right_logical(inner, 5)
    by_part = (moved == lax.broadcasted_iota(jnp.int32, (128, 128), 1)).astype(BF16)

    def flip(block, order=unit):
        return lax.dot_general(order, block, (((1,), (1,)), ((), ())), preferred_element_type=F32)

    def turn_some(n):
        c_piece(n).wait()
        c_piece(n + 3).wait()
        for t in range(8):
            first = pl.multiple_of((8 * n + t) * 128, 128)
            second = pl.multiple_of(3072 + (8 * n + t) * 128, 128)
            both = jnp.concatenate(
                [c_ref[:, :, pl.ds(first, 128)].reshape(64, 128), c_ref[:, :, pl.ds(second, 128)].reshape(64, 128)],
                axis=0,
            )
            turned[pl.ds(first, 128), :] = flip(both) if t % 3 else both.T.astype(F32)

    def mode_of(to, v):
        field = turned[pl.ds(3 * to + v, 64, stride=48), :].astype(BF16)
        return jnp.concatenate([field, field], axis=0)

    def pick_folded(n):
        for t in range(8):
            to = 8 * n + t
            got = flip(mode_of(to, 0), by_part)
            for i2 in range(2):
                block = jnp.where(low, got[64 * i2 : 64 * i2 + 32], got[64 * i2 + 32 : 64 * i2 + 64])
                asend[i2, to] = block[0:26].astype(BF16).reshape(13, 2, 128)

    def pick(v):
        def some(n):
            for t in range(8):
                to = 8 * n + t
                got = flip(mode_of(to, v))
                got = jnp.where(low64, got[0:64], got[64:128])
                csend[v - 1, to] = got[0:50].astype(BF16).reshape(25, 2, 128)

        loop(0, 2, some)
        crecv[v - 1, pb] = csend[v - 1, pb]

    c_ref[25:32] = jnp.zeros((7, 2, 6144), BF16)
    with jax.named_scope("transpose"):
        loop(0, 3, turn_some)
    with jax.named_scope("pick"):
        loop(0, 2, pick_folded)
        arecv[:, pb] = asend[:, pb]

    with jax.named_scope("entry"):
        pl.semaphore_wait(barrier, NPB - 1 + NX - 1 + NX * zi)

    pb_each(lambda step, other: a_copy(0, other).start())
    pb_each(lambda step, other: a_copy(1, other).start())

    def tell_below(plane, carry):
        for c in range(NX):
            pl.semaphore_signal(
                inside.at[zi], inc=1, device_id=(pb, plane * NX + xs[c]), device_id_type=MESH
            )
        return carry

    lax.fori_loop(0, zi, tell_below, 0)

    with jax.named_scope("pick"):
        pick(1)
        pick(2)
    pb_each(lambda step, other: c_copy(1, other).start())
    pb_each(lambda step, other: c_copy(2, other).start())

    with jax.named_scope("vectors"):
        for copy in inputs:
            copy.wait()
        for t in range(64):
            vecs[t : t + 1, :] = vec_ref[:, t * 128 : (t + 1) * 128].astype(F32)
        across = jnp.concatenate([vecs[...], vecs[...]], axis=0).T
        eig[...] = jnp.where(low64, across[0:64], across[64:128]).astype(BF16)

        @pl.when(lax.rem(zi, 2) == core)
        def _():
            table[core, xi, zi // 2] = eig[...]
            loop(0, zi, lambda plane: z_copy(plane).start())

        part[...] = jnp.broadcast_to(part_ref[...], (8, 128))
        parts[pb] = part[...]
        pb_each(lambda step, other: p_copy(other).start())

    def turn(where, first, order):
        points[...] = jnp.zeros_like(points)
        points[0:3, 0 : where.shape[1]] = where[...]
        across = points[...].T
        if order is None:
            across = across[0:NKA]
        else:
            grid[...] = jnp.concatenate([across[0:NPB], jnp.zeros((NPB, 120), F32)], axis=1)
            across = jnp.concatenate([grid[pl.ds(q, 2), :] for q in order], axis=0)
        t = jnp.zeros((across.shape[0], 1536), F32)
        for axis in range(3):
            t = t + across[:, axis : axis + 1] * spots[first + axis : first + axis + 1, :]
        return t

    with jax.named_scope("tables"):
        lane = lax.broadcasted_iota(jnp.int32, (1, 1536), 1)
        inner = lane - 1024
        folded = inner - lax.shift_right_logical(inner * 2521, 16)
        pair = jnp.where(lane < 1024, lax.shift_right_logical(lane, 1), folded)
        second = jnp.where(lane < 1024, lax.bitwise_and(lane, 1), 0)
        quarter = jnp.where(second == 1, 0.25, 0.0)
        lat[...] = jnp.zeros_like(lat)
        lat[0:6, 0:400] = lat_ref[...].astype(F32)
        chosen = (lax.broadcasted_iota(jnp.int32, (512, 1536), 0) == pair).astype(BF16)
        spots = jnp.dot(lat[...].astype(BF16), chosen, preferred_element_type=F32)
        ang = turn(kp_ref, 0, None)
        ang = (2.0 * math.pi) * (ang - jnp.round(ang))
        ck[...] = jnp.cos(ang)
        sk[...] = jnp.sin(ang)
        ang = turn(qp_ref, 3, [2 * lax.rem(yi + ring_offset(t, 8), 8) for t in range(8)]) + quarter
        ang = (2.0 * math.pi) * (ang - jnp.round(ang))
        cq[...] = jnp.cos(ang)
        sq[...] = jnp.sin(ang)

    low32 = low64[0:32]
    real, imag = vecs[0:32], vecs[32:64]
    lines[pl.ds(0, 32, stride=2), :] = jnp.where(low32, real, pltpu.roll(imag, 64, 1))
    lines[pl.ds(1, 32, stride=2), :] = jnp.where(low32, pltpu.roll(real, 64, 1), imag)
    both = lines[...]
    near0 = both.astype(BF16)
    near1 = jnp.where(low64, -pltpu.roll(both, 64, 1), pltpu.roll(both, 64, 1)).astype(BF16)
    wmat[...] = jnp.zeros_like(wmat)
    wfold[...] = jnp.zeros_like(wfold)
    for i2 in range(2):
        rows0 = pl.ds(i2 * 64, 64)
        rows1 = pl.ds(128 + i2 * 64, 64)
        lanes0 = pl.ds(i2 * 128, 128)
        lanes1 = pl.ds(256 + i2 * 128, 128)
        wmat[rows0, lanes0] = near0
        wmat[rows1, lanes0] = near1
        wmat[rows0, lanes1] = -near1
        wmat[rows1, lanes1] = near0
        rows0 = pl.ds(i2 * 128, 64)
        rows1 = pl.ds(i2 * 128 + 64, 64)
        wfold[rows0, lanes0] = near0
        wfold[rows1, lanes0] = near1
        wfold[rows0, lanes1] = -near1
        wfold[rows1, lanes1] = near0

    def make_phase(step, k, other):
        c = ck[pl.ds(k, 1), :]
        s = sk[pl.ds(k, 1), :]
        for h in range(2):
            cos_q, sin_q = cq[8 * h : 8 * h + 8, :], sq[8 * h : 8 * h + 8, :]
            cosine, sine = c * cos_q - s * sin_q, s * cos_q + c * sin_q
            phase[h, step, :, 0:1536] = jnp.concatenate([cosine, sine], axis=0).astype(BF16)
            cosine, sine = -sine[:, 1024:1536], cosine[:, 1024:1536]
            phase[h, step, :, 1536:2048] = jnp.concatenate([cosine, sine], axis=0).astype(BF16)

    with jax.named_scope("phases"):
        planes_each(make_phase)

    with jax.named_scope("inside"):
        def enter_above(plane):
            pl.semaphore_wait(inside.at[plane], NX)

            @pl.when(lax.rem(zi, 2) == core)
            def _():
                z_copy(plane).start()

        loop(zi + 1, NZ, enter_above)

    cols[800:1024] = jnp.zeros((224, 128), BF16)
    acols[416:512] = jnp.zeros((96, 128), BF16)

    def bloch_folded(i2):
        with jax.named_scope("couplings_wait"):
            wait_all(arecv.at[i2], NPB - 1, a_rs.at[i2])
            acols[0:416] = arecv[i2].reshape(416, 128)

        def part(n):
            rows = pl.ds(8 * n, 8)
            with jax.named_scope("bloch"):
                first = jnp.dot(
                    phase[:, rows, :, 1024:1536].reshape(256, 512), acols[...], preferred_element_type=F32
                ).reshape(2, 8, 2, 8, 128)
                second = jnp.dot(
                    phase[:, rows, :, 1536:2048].reshape(256, 512), acols[...], preferred_element_type=F32
                ).reshape(2, 8, 2, 8, 128)

                def across(block):
                    return pltpu.roll(block.reshape(128, 128), 64, 1).reshape(2, 8, 8, 128)

                real = first[:, :, 0] + across(second[:, :, 0])
                imag = across(first[:, :, 1]) + second[:, :, 1]
                both = jnp.where(low_lane, real, imag)
                both = jnp.concatenate([both[0], both[1]], axis=1)
                bsend[0, rows, i2] = both.astype(BF16)
            with jax.named_scope("bloch_send"):
                planes_each(lambda *peer: b_send(0, i2, *peer), 2 * n, 2 * n + 2)

        loop(0, 4, part)
        brecv[0, ka, i2] = bsend[0, NX * zi + NX - 1, i2]

    low_lane = lax.broadcasted_iota(jnp.int32, (2, 8, 8, 128), 3) < 64

    def bloch_of(v, whole):
        with jax.named_scope("couplings_wait"):
            wait_all(crecv.at[v - 1], NPB - 1, c_rs.at[v - 1])
            cols[0:800] = crecv[v - 1].reshape(800, 128)

        def half(h, first):
            rows = pl.ds(first, 16)
            with jax.named_scope("bloch"):
                got = jnp.dot(
                    phase[h, rows, :, 0:1024].reshape(256, 1024), cols[...],
                    preferred_element_type=F32,
                )
                bsend[v, rows, h] = got.astype(BF16).reshape(16, 16, 128)

        def send(h, first):
            with jax.named_scope("bloch_send"):
                planes_each(lambda *peer: b_send(v, h, *peer), first // NX, first // NX + 4)

        if whole:
            for first in (0, 16):
                half(0, first)
                half(1, first)
                send(None, first)
        else:
            for h in range(2):
                for first in (0, 16):
                    half(h, first)
                    send(h, first)
        brecv[v, ka] = bsend[v, NX * zi + NX - 1]

    def vectors_x():
        with jax.named_scope("vectors_wait_z"):
            @pl.when(lax.rem(zi, 2) == core)
            def _():
                wait_all(table.at[0, 0], NZ // 2 - 1, z_rs)

            @pl.when(lax.rem(zi, 2) != core)
            def _():
                wait_all(table.at[0, 0], NZ // 2, z_rs)

            for c in range(NX - 1):
                x_copy(xs[c]).start()

    def vectors_core():
        with jax.named_scope("vectors_wait_x"):
            wait_all(table.at[0], NX - 1, x_rs)
            m_copy().start()

    def vectors_done():
        with jax.named_scope("vectors_wait"):
            wait_all(table, 1, m_rs)
            wait_all(parts, NPB - 1, p_rs)

            def far_of(q):
                label = jnp.max(parts[q])
                plane = label // NX
                found = table[lax.rem(plane, 2), lax.rem(label, NX), plane // 2]
                far[q] = jnp.concatenate([found, found], axis=0)

            for q in range(NPB):
                far_of(q)

    def squares(q, line):
        field = jnp.concatenate([tmat[t, pl.ds(line, 32, stride=8), :] for t in (0, 2, 1, 3)], axis=0)
        got = lax.dot_general(
            field.astype(BF16).T, far[q], (((1,), (1,)), ((), ())), preferred_element_type=F32
        )
        got = got * got
        both = got[0:64] + got[64:128]
        return jnp.where(low, both[0:32], both[32:64]).astype(BF16)

    def rotate(n):
        v, h = n // 2, lax.rem(n, 2)
        with jax.named_scope("bloch_wait"):
            @pl.when(n == 0)
            def _():
                for i2 in range(2):
                    wait_pieces(brecv, 0, i2, b_rs)

            @pl.when(n == 2)
            def _():
                wait_all(brecv.at[1], NKA - 1, b_rs.at[1, 0])

            @pl.when(n > 3)
            def _():
                wait_pieces(brecv, 2, h, b_rs)

        def near(t, pieces, weights):
            field = jnp.concatenate([piece.reshape(128, 128) for piece in pieces], axis=1).astype(BF16)
            got = jnp.dot(field, weights[...], preferred_element_type=F32)
            for t4 in range(4):
                tmat[t4, pl.ds(t * 128, 128), :] = got[:, t4 * 128 : (t4 + 1) * 128]

        def near_folded(t):
            fields = [brecv[0, pl.ds(t * 16, 16), i2].astype(F32) for i2 in range(2)]
            near(t, [jnp.where(h == 0, field[:, 0:8], field[:, 8:16]) for field in fields], wfold)

        def near_other(t):
            field = brecv[v, pl.ds(t * 16, 16), h].astype(F32)
            near(t, [field[:, 0:8], field[:, 8:16]], wmat)

        with jax.named_scope("near_rotation"):
            @pl.when(n < 2)
            def _():
                loop(0, 2, near_folded)

            @pl.when(n > 1)
            def _():
                loop(0, 2, near_other)

        def four(m):
            others = []
            for s in range(4):
                line = 4 * m + s
                q = 2 * lax.rem(yi + ring_offset(4 * h + 2 * m + s // 2, 8), 8) + s % 2
                others.append(q)
                qsend[v, q] = squares(q, line)

            for s in range(4):
                @pl.when(others[s] != pb)
                def _():
                    q_copy(v, others[s]).start()

        with jax.named_scope("far_rotation"):
            loop(0, 2, four)

    bloch_folded(0)

    @pl.when(zi >= 3)
    def _():
        vectors_x()

    bloch_folded(1)

    @pl.when(zi < 3)
    def _():
        vectors_x()

    bloch_of(1, True)
    vectors_core()

    bloch_of(2, False)
    vectors_done()
    loop(0, 2 * VS, rotate)

    def keep(v):
        qrecv[v, pb] = qsend[v, pb]

    loop(0, VS, keep)

    def place(v):
        with jax.named_scope("squares_wait"):
            wait_all(qrecv.at[v], NPB - 1, q_rs.at[v])

        def one(s):
            spread[pl.ds(3 * s + v, 32, stride=48), :] = qrecv[v, s].astype(F32)

        loop(0, NPB, one)

    loop(0, VS, place)

    with jax.named_scope("output"):
        for n in range(12):
            block = spread[n * 128 : (n + 1) * 128, :].T.astype(BF16)
            out_ref[:, n * 128 : (n + 1) * 128] = block[0:64]
            out_ref[:, 1536 + n * 128 : 1536 + (n + 1) * 128] = block[64:128]

    with jax.named_scope("drain"):
        @pl.when(lax.rem(zi, 2) == core)
        def _():
            gone = cols.at[pl.ds(0, 64 * (NZ - 1))]
            pltpu.make_async_copy(gone, gone, z_ss).wait()

        wait_all(table.at[0], NX - 1, x_ss)
        wait_all(table, 1, m_ss)
        wait_all(parts, NPB - 1, p_ss)

        def drain(v):
            wait_all(qsend.at[v], NPB - 1, q_ss.at[v])

        loop(0, VS, drain)
        for n in range(2):
            wait_all(asend.at[n], NPB - 1, a_ss.at[n])
            wait_all(csend.at[n], NPB - 1, c_ss.at[n])
            wait_pieces(bsend, 0, n, b_ss)
            wait_pieces(bsend, 2, n, b_ss)
        wait_all(bsend.at[1], NKA - 1, b_ss.at[1, 0])


def couple(coupling, vectors, part, kp, qp, lat):
    vmem = pl.BlockSpec(memory_space=pltpu.VMEM)
    dma = pltpu.SemaphoreType.DMA
    return pl.pallas_call(
        kernel,
        out_shape=jax.ShapeDtypeStruct((64, 3072), BF16),
        in_specs=[pl.BlockSpec(memory_space=pltpu.HBM)] * 6,
        out_specs=vmem,
        scratch_shapes=[
            pltpu.VMEM((32, 2, 6144), BF16),
            pltpu.VMEM((1, 8192), BF16),
            pltpu.VMEM((1, 1), jnp.int32),
            pltpu.VMEM((3, NKA), F32),
            pltpu.VMEM((3, NPB), F32),
            pltpu.VMEM((6, 400), jnp.int32),
            pltpu.VMEM((3072, 128), F32),
            pltpu.VMEM((2, NPB, 13, 2, 128), BF16),
            pltpu.VMEM((2, NPB, 13, 2, 128), BF16),
            pltpu.VMEM((VS - 1, NPB, 25, 2, 128), BF16),
            pltpu.VMEM((VS - 1, NPB, 25, 2, 128), BF16),
            pltpu.VMEM((1024, 128), BF16),
            pltpu.VMEM((512, 128), BF16),
            pltpu.VMEM((8, 128), F32),
            pltpu.VMEM((NPB, 128), F32),
            pltpu.VMEM((8, 512), F32),
            pltpu.VMEM((64, 128), F32),
            pltpu.VMEM((64, 128), F32),
            pltpu.VMEM((64, 128), BF16),
            pltpu.VMEM((8, 128), jnp.int32),
            pltpu.VMEM((NKA, 1536), F32),
            pltpu.VMEM((NKA, 1536), F32),
            pltpu.VMEM((NPB, 1536), F32),
            pltpu.VMEM((NPB, 1536), F32),
            pltpu.VMEM((2, NKA, 16, 2048), BF16),
            pltpu.VMEM((256, 512), BF16),
            pltpu.VMEM((256, 512), BF16),
            pltpu.VMEM((VS, NKA, 2, 16, 128), BF16),
            pltpu.VMEM((VS, NKA, 2, 16, 128), BF16),
            pltpu.VMEM((2, NX, NZ // 2, 64, 128), BF16),
            pltpu.VMEM((NPB, 8, 128), jnp.int32),
            pltpu.VMEM((NPB, 128, 128), BF16),
            pltpu.VMEM((4, 256, 128), F32),
            pltpu.VMEM((VS, NPB, 32, 128), BF16),
            pltpu.VMEM((VS, NPB, 32, 128), BF16),
            pltpu.VMEM((1536, 128), F32),
            dma((2,)), dma((2,)),
            dma((VS - 1,)), dma((VS - 1,)),
            dma((VS, 2)), dma((VS, 2)),
            dma((VS,)), dma((VS,)),
            dma(()), dma(()),
            dma(()), dma(()),
            dma(()), dma(()),
            dma(()), dma(()),
            dma((5,)),
            dma((6,)),
            pltpu.SemaphoreType.REGULAR((NZ,)),
        ],
        compiler_params=pltpu.CompilerParams(
            collective_id=0, has_side_effects=True, vmem_limit_bytes=60 << 20
        ),
        name="couple",
    )(coupling, vectors, part, kp, qp, lat)


def body(coupling, eigvecs, partner, kpoints, qpoints, lattice):
    out = couple(coupling, eigvecs, partner, kpoints, qpoints, lattice)
    return out.reshape(1, 1, 196608)


def solution(mesh):
    in_specs = (P("pb", None, "ka"), P("ka", None), P("pb", "ka"), P(), P(), P())
    out_specs = P("pb", "ka", None)
    return jax.shard_map(body, mesh=mesh, in_specs=in_specs, out_specs=out_specs, check_vma=False)
```

```python
import math

import jax
import jax.numpy as jnp
from jax import lax
from jax.experimental import pallas as pl
from jax.experimental.pallas import tpu as pltpu
from jax.sharding import PartitionSpec as P

MESH = pl.DeviceIdType.MESH
NPB = 16
NKA = 32
NZ = 8
NX = 4
VS = 3
F32 = jnp.float32
BF16 = jnp.bfloat16


def kernel(
    c_hbm, vec_hbm, part_hbm, place_hbm, out_ref,
    c_ref, vec_ref, part_ref, place_ref, turned, asend, arecv, csend, crecv, cols, acols, points, grid, lat, vecs, lines, eig, part,
    ck, sk, cq, sq, phase, wmat, wfold, bsend, brecv, table, parts, far, tmat, qsend, qrecv, spread,
    a_ss, a_rs, c_ss, c_rs, b_ss, b_rs, q_ss, q_rs, z_ss, z_rs, x_ss, x_rs, m_ss, m_rs, p_ss, p_rs, in_sem, c_sem, inside,
):
    pb = lax.axis_index("pb")
    ka = lax.axis_index("ka")
    zi = ka // NX
    xi = lax.rem(ka, NX)

    def ring_offset(step, size):
        side = 1 - 2 * lax.rem(step, 2)
        return lax.rem(size // 2 + side * ((step + 1) // 2) + size, size)

    core = lax.rem(pb, 2)
    yi = pb // 2
    cores = [1 - core, core]
    xs = [lax.rem(xi + offset, NX) for offset in (2, 1, 3, 0)]

    def pb_each(do):
        def some(step, carry):
            y = lax.rem(yi + ring_offset(step, 8), 8)
            for c in range(2):
                do(2 * step + c, 2 * y + cores[c])
            return carry

        lax.fori_loop(0, 7, some, 0)
        do(14, 2 * yi + cores[0])

    def planes_each(do, first=0, last=NZ):
        def some(plane, carry):
            for c in range(NX):
                do(NX * plane + c, plane * NX + xs[c], True if c < NX - 1 else plane != zi)
            return carry

        lax.fori_loop(first, last, some, 0)

    def c_piece(n):
        lanes = pl.ds(n * 1024, 1024)
        return pltpu.make_async_copy(c_hbm.at[:, :, lanes], c_ref.at[pl.ds(0, 25), :, lanes], c_sem.at[n])

    for n in (0, 3, 1, 4, 2, 5):
        c_piece(n).start()
    inputs = [
        pltpu.make_async_copy(vec_hbm, vec_ref, in_sem.at[0]),
        pltpu.make_async_copy(part_hbm, part_ref, in_sem.at[1]),
        pltpu.make_async_copy(place_hbm, place_ref, in_sem.at[2]),
    ]
    for copy in inputs:
        copy.start()

    barrier = pltpu.get_barrier_semaphore()

    def greet(to):
        pl.semaphore_signal(barrier, inc=1, device_id=to, device_id_type=MESH)

    pb_each(lambda step, other: greet((other, ka)))
    for c in range(NX - 1):
        greet((pb, zi * NX + xs[c]))

    def greet_above(plane, carry):
        for c in range(NX):
            greet((pb, plane * NX + xs[c]))
        return carry

    lax.fori_loop(zi + 1, NZ, greet_above, 0)

    def a_copy(i2, to):
        return pltpu.make_async_remote_copy(
            src_ref=asend.at[i2, to], dst_ref=arecv.at[i2, pb],
            send_sem=a_ss.at[i2], recv_sem=a_rs.at[i2],
            device_id=(to, ka), device_id_type=MESH,
        )

    def c_copy(v, to):
        return pltpu.make_async_remote_copy(
            src_ref=csend.at[v - 1, to], dst_ref=crecv.at[v - 1, pb],
            send_sem=c_ss.at[v - 1], recv_sem=c_rs.at[v - 1],
            device_id=(to, ka), device_id_type=MESH,
        )

    def z_copy(plane):
        return pltpu.make_async_remote_copy(
            src_ref=eig, dst_ref=table.at[core, xi, zi // 2],
            send_sem=z_ss, recv_sem=z_rs,
            device_id=(pb, plane * NX + xi), device_id_type=MESH,
        )

    def x_copy(other):
        return pltpu.make_async_remote_copy(
            src_ref=table.at[core, xi], dst_ref=table.at[core, xi],
            send_sem=x_ss, recv_sem=x_rs,
            device_id=(pb, zi * NX + other), device_id_type=MESH,
        )

    def m_copy():
        return pltpu.make_async_remote_copy(
            src_ref=table.at[core], dst_ref=table.at[core],
            send_sem=m_ss, recv_sem=m_rs,
            device_id=(2 * yi + cores[0], ka), device_id_type=MESH,
        )

    def b_send(v, h, step, other, remote):
        if remote is True:
            b_copy(v, h, step, other).start()
        else:
            @pl.when(remote)
            def _():
                b_copy(v, h, step, other).start()

    def p_copy(other):
        return pltpu.make_async_remote_copy(
            src_ref=part, dst_ref=parts.at[pb],
            send_sem=p_ss, recv_sem=p_rs,
            device_id=(other, ka), device_id_type=MESH,
        )

    def b_copy(v, h, step, other):
        def piece(ref, row):
            return ref.at[v, row] if h is None else ref.at[v, row, h]

        sem = 0 if h is None else h
        return pltpu.make_async_remote_copy(
            src_ref=piece(bsend, step), dst_ref=piece(brecv, ka),
            send_sem=b_ss.at[v, sem], recv_sem=b_rs.at[v, sem],
            device_id=(pb, other), device_id_type=MESH,
        )

    def q_copy(v, other):
        return pltpu.make_async_remote_copy(
            src_ref=qsend.at[v, other], dst_ref=qrecv.at[v, pb],
            send_sem=q_ss.at[v], recv_sem=q_rs.at[v],
            device_id=(other, ka), device_id_type=MESH,
        )

    def wait_all(ref, count, sem):
        part = ref.at[pl.ds(0, count)]
        pltpu.make_async_copy(part, part, sem).wait()

    def wait_pieces(ref, v, h, sems):
        part = ref.at[v, pl.ds(0, NKA - 1), h]
        pltpu.make_async_copy(part, part, sems.at[v, h]).wait()

    def loop(first, last, do):
        def step_of(step, carry):
            do(step)
            return carry

        lax.fori_loop(first, last, step_of, 0)

    low = lax.broadcasted_iota(jnp.int32, (32, 128), 1) < 64
    low64 = lax.broadcasted_iota(jnp.int32, (64, 128), 1) < 64
    line = lax.broadcasted_iota(jnp.int32, (128, 128), 0)
    unit = (line == lax.broadcasted_iota(jnp.int32, (128, 128), 1)).astype(BF16)

    inner = lax.bitwise_and(line, 63)
    moved = (line - inner) + 2 * lax.bitwise_and(inner, 31) + lax.shift_right_logical(inner, 5)
    by_part = (moved == lax.broadcasted_iota(jnp.int32, (128, 128), 1)).astype(BF16)

    def flip(block, order=unit):
        return lax.dot_general(order, block, (((1,), (1,)), ((), ())), preferred_element_type=F32)

    def turn_some(n):
        c_piece(n).wait()
        c_piece(n + 3).wait()
        for t in range(8):
            first = pl.multiple_of((8 * n + t) * 128, 128)
            second = pl.multiple_of(3072 + (8 * n + t) * 128, 128)
            both = jnp.concatenate(
                [c_ref[:, :, pl.ds(first, 128)].reshape(64, 128), c_ref[:, :, pl.ds(second, 128)].reshape(64, 128)],
                axis=0,
            )
            turned[pl.ds(first, 128), :] = flip(both) if t % 3 else both.T.astype(F32)

    def mode_of(to, v):
        field = turned[pl.ds(3 * to + v, 64, stride=48), :].astype(BF16)
        return jnp.concatenate([field, field], axis=0)

    def pick_folded(n):
        for t in range(8):
            to = 8 * n + t
            got = flip(mode_of(to, 0), by_part)
            for i2 in range(2):
                block = jnp.where(low, got[64 * i2 : 64 * i2 + 32], got[64 * i2 + 32 : 64 * i2 + 64])
                asend[i2, to] = block[0:26].astype(BF16).reshape(13, 2, 128)

    def pick(v):
        def some(n):
            for t in range(8):
                to = 8 * n + t
                got = flip(mode_of(to, v))
                got = jnp.where(low64, got[0:64], got[64:128])
                csend[v - 1, to] = got[0:50].astype(BF16).reshape(25, 2, 128)

        loop(0, 2, some)
        crecv[v - 1, pb] = csend[v - 1, pb]

    c_ref[25:32] = jnp.zeros((7, 2, 6144), BF16)
    with jax.named_scope("transpose"):
        loop(0, 3, turn_some)
    with jax.named_scope("pick"):
        loop(0, 2, pick_folded)
        arecv[:, pb] = asend[:, pb]

    with jax.named_scope("entry"):
        pl.semaphore_wait(barrier, NPB - 1 + NX - 1 + NX * zi)

    pb_each(lambda step, other: a_copy(0, other).start())
    pb_each(lambda step, other: a_copy(1, other).start())

    def tell_below(plane, carry):
        for c in range(NX):
            pl.semaphore_signal(
                inside.at[zi], inc=1, device_id=(pb, plane * NX + xs[c]), device_id_type=MESH
            )
        return carry

    lax.fori_loop(0, zi, tell_below, 0)

    with jax.named_scope("pick"):
        pick(1)
        pick(2)
    pb_each(lambda step, other: c_copy(1, other).start())
    pb_each(lambda step, other: c_copy(2, other).start())

    with jax.named_scope("vectors"):
        for copy in inputs:
            copy.wait()
        for t in range(64):
            vecs[t : t + 1, :] = vec_ref[:, t * 128 : (t + 1) * 128].astype(F32)
        across = jnp.concatenate([vecs[...], vecs[...]], axis=0).T
        eig[...] = jnp.where(low64, across[0:64], across[64:128]).astype(BF16)

        @pl.when(lax.rem(zi, 2) == core)
        def _():
            table[core, xi, zi // 2] = eig[...]
            loop(0, zi, lambda plane: z_copy(plane).start())

        part[...] = jnp.broadcast_to(part_ref[...], (8, 128))
        parts[pb] = part[...]
        pb_each(lambda step, other: p_copy(other).start())

    def turn(where, first, order):
        points[...] = jnp.zeros_like(points)
        points[0:3, 0 : where.shape[1]] = where
        across = points[...].T
        if order is None:
            across = across[0:NKA]
        else:
            grid[...] = jnp.concatenate([across[0:NPB], jnp.zeros((NPB, 120), F32)], axis=1)
            across = jnp.concatenate([grid[pl.ds(q, 2), :] for q in order], axis=0)
        t = jnp.zeros((across.shape[0], 1536), F32)
        for axis in range(3):
            t = t + across[:, axis : axis + 1] * spots[first + axis : first + axis + 1, :]
        return t

    with jax.named_scope("tables"):
        lane = lax.broadcasted_iota(jnp.int32, (1, 1536), 1)
        inner = lane - 1024
        folded = inner - lax.shift_right_logical(inner * 2521, 16)
        pair = jnp.where(lane < 1024, lax.shift_right_logical(lane, 1), folded)
        second = jnp.where(lane < 1024, lax.bitwise_and(lane, 1), 0)
        quarter = jnp.where(second == 1, 0.25, 0.0)
        lat[...] = jnp.zeros_like(lat)
        lat[0:6, 0:400] = place_ref[:, 0:400]
        chosen = (lax.broadcasted_iota(jnp.int32, (512, 1536), 0) == pair).astype(BF16)
        spots = jnp.dot(lat[...].astype(BF16), chosen, preferred_element_type=F32)
        ang = turn(place_ref[0:3, 400:432], 0, None)
        ang = (2.0 * math.pi) * (ang - jnp.round(ang))
        ck[...] = jnp.cos(ang)
        sk[...] = jnp.sin(ang)
        ang = turn(place_ref[0:3, 432:448], 3, [2 * lax.rem(yi + ring_offset(t, 8), 8) for t in range(8)]) + quarter
        ang = (2.0 * math.pi) * (ang - jnp.round(ang))
        cq[...] = jnp.cos(ang)
        sq[...] = jnp.sin(ang)

    low32 = low64[0:32]
    real, imag = vecs[0:32], vecs[32:64]
    lines[pl.ds(0, 32, stride=2), :] = jnp.where(low32, real, pltpu.roll(imag, 64, 1))
    lines[pl.ds(1, 32, stride=2), :] = jnp.where(low32, pltpu.roll(real, 64, 1), imag)
    both = lines[...]
    near0 = both.astype(BF16)
    near1 = jnp.where(low64, -pltpu.roll(both, 64, 1), pltpu.roll(both, 64, 1)).astype(BF16)
    wmat[...] = jnp.zeros_like(wmat)
    wfold[...] = jnp.zeros_like(wfold)
    for i2 in range(2):
        rows0 = pl.ds(i2 * 64, 64)
        rows1 = pl.ds(128 + i2 * 64, 64)
        lanes0 = pl.ds(i2 * 128, 128)
        lanes1 = pl.ds(256 + i2 * 128, 128)
        wmat[rows0, lanes0] = near0
        wmat[rows1, lanes0] = near1
        wmat[rows0, lanes1] = -near1
        wmat[rows1, lanes1] = near0
        rows0 = pl.ds(i2 * 128, 64)
        rows1 = pl.ds(i2 * 128 + 64, 64)
        wfold[rows0, lanes0] = near0
        wfold[rows1, lanes0] = near1
        wfold[rows0, lanes1] = -near1
        wfold[rows1, lanes1] = near0

    def make_phase(step, k, other):
        c = ck[pl.ds(k, 1), :]
        s = sk[pl.ds(k, 1), :]
        for h in range(2):
            cos_q, sin_q = cq[8 * h : 8 * h + 8, :], sq[8 * h : 8 * h + 8, :]
            cosine, sine = c * cos_q - s * sin_q, s * cos_q + c * sin_q
            phase[h, step, :, 0:1536] = jnp.concatenate([cosine, sine], axis=0).astype(BF16)
            cosine, sine = -sine[:, 1024:1536], cosine[:, 1024:1536]
            phase[h, step, :, 1536:2048] = jnp.concatenate([cosine, sine], axis=0).astype(BF16)

    with jax.named_scope("phases"):
        planes_each(make_phase)

    with jax.named_scope("inside"):
        def enter_above(plane):
            pl.semaphore_wait(inside.at[plane], NX)

            @pl.when(lax.rem(zi, 2) == core)
            def _():
                z_copy(plane).start()

        loop(zi + 1, NZ, enter_above)

    cols[800:1024] = jnp.zeros((224, 128), BF16)
    acols[416:512] = jnp.zeros((96, 128), BF16)

    def bloch_folded(i2):
        with jax.named_scope("couplings_wait"):
            wait_all(arecv.at[i2], NPB - 1, a_rs.at[i2])
            acols[0:416] = arecv[i2].reshape(416, 128)

        def part(n):
            rows = pl.ds(8 * n, 8)
            with jax.named_scope("bloch"):
                first = jnp.dot(
                    phase[:, rows, :, 1024:1536].reshape(256, 512), acols[...], preferred_element_type=F32
                ).reshape(2, 8, 2, 8, 128)
                second = jnp.dot(
                    phase[:, rows, :, 1536:2048].reshape(256, 512), acols[...], preferred_element_type=F32
                ).reshape(2, 8, 2, 8, 128)

                def across(block):
                    return pltpu.roll(block.reshape(128, 128), 64, 1).reshape(2, 8, 8, 128)

                real = first[:, :, 0] + across(second[:, :, 0])
                imag = across(first[:, :, 1]) + second[:, :, 1]
                both = jnp.where(low_lane, real, imag)
                both = jnp.concatenate([both[0], both[1]], axis=1)
                bsend[0, rows, i2] = both.astype(BF16)
            with jax.named_scope("bloch_send"):
                planes_each(lambda *peer: b_send(0, i2, *peer), 2 * n, 2 * n + 2)

        loop(0, 4, part)
        brecv[0, ka, i2] = bsend[0, NX * zi + NX - 1, i2]

    low_lane = lax.broadcasted_iota(jnp.int32, (2, 8, 8, 128), 3) < 64

    def bloch_of(v, whole):
        with jax.named_scope("couplings_wait"):
            wait_all(crecv.at[v - 1], NPB - 1, c_rs.at[v - 1])
            cols[0:800] = crecv[v - 1].reshape(800, 128)

        def half(h, first):
            rows = pl.ds(first, 16)
            with jax.named_scope("bloch"):
                got = jnp.dot(
                    phase[h, rows, :, 0:1024].reshape(256, 1024), cols[...],
                    preferred_element_type=F32,
                )
                bsend[v, rows, h] = got.astype(BF16).reshape(16, 16, 128)

        def send(h, first):
            with jax.named_scope("bloch_send"):
                planes_each(lambda *peer: b_send(v, h, *peer), first // NX, first // NX + 4)

        if whole:
            for first in (0, 16):
                half(0, first)
                half(1, first)
                send(None, first)
        else:
            for h in range(2):
                for first in (0, 16):
                    half(h, first)
                    send(h, first)
        brecv[v, ka] = bsend[v, NX * zi + NX - 1]

    def vectors_x():
        with jax.named_scope("vectors_wait_z"):
            @pl.when(lax.rem(zi, 2) == core)
            def _():
                wait_all(table.at[0, 0], NZ // 2 - 1, z_rs)

            @pl.when(lax.rem(zi, 2) != core)
            def _():
                wait_all(table.at[0, 0], NZ // 2, z_rs)

            for c in range(NX - 1):
                x_copy(xs[c]).start()

    def vectors_core():
        with jax.named_scope("vectors_wait_x"):
            wait_all(table.at[0], NX - 1, x_rs)
            m_copy().start()

    def vectors_done():
        with jax.named_scope("vectors_wait"):
            wait_all(table, 1, m_rs)
            wait_all(parts, NPB - 1, p_rs)

            def far_of(q):
                label = jnp.max(parts[q])
                plane = label // NX
                found = table[lax.rem(plane, 2), lax.rem(label, NX), plane // 2]
                far[q] = jnp.concatenate([found, found], axis=0)

            for q in range(NPB):
                far_of(q)

    def squares(q, line):
        field = jnp.concatenate([tmat[t, pl.ds(line, 32, stride=8), :] for t in (0, 2, 1, 3)], axis=0)
        got = lax.dot_general(
            field.astype(BF16).T, far[q], (((1,), (1,)), ((), ())), preferred_element_type=F32
        )
        got = got * got
        both = got[0:64] + got[64:128]
        return jnp.where(low, both[0:32], both[32:64]).astype(BF16)

    def rotate(n):
        v, h = n // 2, lax.rem(n, 2)
        with jax.named_scope("bloch_wait"):
            @pl.when(n == 0)
            def _():
                for i2 in range(2):
                    wait_pieces(brecv, 0, i2, b_rs)

            @pl.when(n == 2)
            def _():
                wait_all(brecv.at[1], NKA - 1, b_rs.at[1, 0])

            @pl.when(n > 3)
            def _():
                wait_pieces(brecv, 2, h, b_rs)

        def near(t, pieces, weights):
            field = jnp.concatenate([piece.reshape(128, 128) for piece in pieces], axis=1).astype(BF16)
            got = jnp.dot(field, weights[...], preferred_element_type=F32)
            for t4 in range(4):
                tmat[t4, pl.ds(t * 128, 128), :] = got[:, t4 * 128 : (t4 + 1) * 128]

        def near_folded(t):
            fields = [brecv[0, pl.ds(t * 16, 16), i2].astype(F32) for i2 in range(2)]
            near(t, [jnp.where(h == 0, field[:, 0:8], field[:, 8:16]) for field in fields], wfold)

        def near_other(t):
            field = brecv[v, pl.ds(t * 16, 16), h].astype(F32)
            near(t, [field[:, 0:8], field[:, 8:16]], wmat)

        with jax.named_scope("near_rotation"):
            @pl.when(n < 2)
            def _():
                loop(0, 2, near_folded)

            @pl.when(n > 1)
            def _():
                loop(0, 2, near_other)

        def four(m):
            others = []
            for s in range(4):
                line = 4 * m + s
                q = 2 * lax.rem(yi + ring_offset(4 * h + 2 * m + s // 2, 8), 8) + s % 2
                others.append(q)
                qsend[v, q] = squares(q, line)

            for s in range(4):
                @pl.when(others[s] != pb)
                def _():
                    q_copy(v, others[s]).start()

        with jax.named_scope("far_rotation"):
            loop(0, 2, four)

    bloch_folded(0)

    @pl.when(zi >= 3)
    def _():
        vectors_x()

    bloch_folded(1)

    @pl.when(zi < 3)
    def _():
        vectors_x()

    bloch_of(1, True)
    vectors_core()

    bloch_of(2, False)
    vectors_done()
    loop(0, 2 * VS, rotate)

    def keep(v):
        qrecv[v, pb] = qsend[v, pb]

    loop(0, VS, keep)

    def place(v):
        with jax.named_scope("squares_wait"):
            wait_all(qrecv.at[v], NPB - 1, q_rs.at[v])

        def one(s):
            spread[pl.ds(3 * s + v, 32, stride=48), :] = qrecv[v, s].astype(F32)

        loop(0, NPB, one)

    loop(0, VS, place)

    with jax.named_scope("output"):
        for n in range(12):
            block = spread[n * 128 : (n + 1) * 128, :].T.astype(BF16)
            out_ref[:, n * 128 : (n + 1) * 128] = block[0:64]
            out_ref[:, 1536 + n * 128 : 1536 + (n + 1) * 128] = block[64:128]

    with jax.named_scope("drain"):
        @pl.when(lax.rem(zi, 2) == core)
        def _():
            gone = cols.at[pl.ds(0, 64 * (NZ - 1))]
            pltpu.make_async_copy(gone, gone, z_ss).wait()

        wait_all(table.at[0], NX - 1, x_ss)
        wait_all(table, 1, m_ss)
        wait_all(parts, NPB - 1, p_ss)

        def drain(v):
            wait_all(qsend.at[v], NPB - 1, q_ss.at[v])

        loop(0, VS, drain)
        for n in range(2):
            wait_all(asend.at[n], NPB - 1, a_ss.at[n])
            wait_all(csend.at[n], NPB - 1, c_ss.at[n])
            wait_pieces(bsend, 0, n, b_ss)
            wait_pieces(bsend, 2, n, b_ss)
        wait_all(bsend.at[1], NKA - 1, b_ss.at[1, 0])


def couple(coupling, vectors, part, places):
    vmem = pl.BlockSpec(memory_space=pltpu.VMEM)
    dma = pltpu.SemaphoreType.DMA
    return pl.pallas_call(
        kernel,
        out_shape=jax.ShapeDtypeStruct((64, 3072), BF16),
        in_specs=[pl.BlockSpec(memory_space=pltpu.HBM)] * 4,
        out_specs=vmem,
        scratch_shapes=[
            pltpu.VMEM((32, 2, 6144), BF16),
            pltpu.VMEM((1, 8192), BF16),
            pltpu.VMEM((1, 1), jnp.int32),
            pltpu.VMEM((6, 448), F32),
            pltpu.VMEM((3072, 128), F32),
            pltpu.VMEM((2, NPB, 13, 2, 128), BF16),
            pltpu.VMEM((2, NPB, 13, 2, 128), BF16),
            pltpu.VMEM((VS - 1, NPB, 25, 2, 128), BF16),
            pltpu.VMEM((VS - 1, NPB, 25, 2, 128), BF16),
            pltpu.VMEM((1024, 128), BF16),
            pltpu.VMEM((512, 128), BF16),
            pltpu.VMEM((8, 128), F32),
            pltpu.VMEM((NPB, 128), F32),
            pltpu.VMEM((8, 512), F32),
            pltpu.VMEM((64, 128), F32),
            pltpu.VMEM((64, 128), F32),
            pltpu.VMEM((64, 128), BF16),
            pltpu.VMEM((8, 128), jnp.int32),
            pltpu.VMEM((NKA, 1536), F32),
            pltpu.VMEM((NKA, 1536), F32),
            pltpu.VMEM((NPB, 1536), F32),
            pltpu.VMEM((NPB, 1536), F32),
            pltpu.VMEM((2, NKA, 16, 2048), BF16),
            pltpu.VMEM((256, 512), BF16),
            pltpu.VMEM((256, 512), BF16),
            pltpu.VMEM((VS, NKA, 2, 16, 128), BF16),
            pltpu.VMEM((VS, NKA, 2, 16, 128), BF16),
            pltpu.VMEM((2, NX, NZ // 2, 64, 128), BF16),
            pltpu.VMEM((NPB, 8, 128), jnp.int32),
            pltpu.VMEM((NPB, 128, 128), BF16),
            pltpu.VMEM((4, 256, 128), F32),
            pltpu.VMEM((VS, NPB, 32, 128), BF16),
            pltpu.VMEM((VS, NPB, 32, 128), BF16),
            pltpu.VMEM((1536, 128), F32),
            dma((2,)), dma((2,)),
            dma((VS - 1,)), dma((VS - 1,)),
            dma((VS, 2)), dma((VS, 2)),
            dma((VS,)), dma((VS,)),
            dma(()), dma(()),
            dma(()), dma(()),
            dma(()), dma(()),
            dma(()), dma(()),
            dma((3,)),
            dma((6,)),
            pltpu.SemaphoreType.REGULAR((NZ,)),
        ],
        compiler_params=pltpu.CompilerParams(
            collective_id=0, has_side_effects=True, vmem_limit_bytes=55900000
        ),
        name="couple",
    )(coupling, vectors, part, places)


def body(coupling, eigvecs, partner, kpoints, qpoints, lattice):
    places = (
        jnp.pad(lattice, ((0, 0), (0, 48))).astype(F32)
        + jnp.pad(kpoints, ((0, 3), (400, 16)))
        + jnp.pad(qpoints, ((0, 3), (432, 0)))
    )
    out = couple(coupling, eigvecs, partner, places)
    return out.reshape(1, 1, 196608)


def solution(mesh):
    in_specs = (P("pb", None, "ka"), P("ka", None), P("pb", "ka"), P(), P(), P())
    out_specs = P("pb", "ka", None)
    return jax.shard_map(body, mesh=mesh, in_specs=in_specs, out_specs=out_specs, check_vma=False)
```
